32 devices in a mesh: blk: 8 (over y, x, core), sub: 4 (over z).
Axes of the slice: x: 2, y: 2, z: 4, core: 2. Of those that a mesh axis runs over, the one named last changes fastest.
Arguments:
- fluid_temp: float32 [256, 128, 512], P('blk', 'sub'), may hold values from -6 to 6
- velocity: float32 [3, 256, 128, 512], P(None, 'blk', 'sub'), may hold values from -6 to 6
- eddy_diff: float32 [256, 128, 512], P('blk', 'sub'), may hold values from 0.05 to 0.5
- wall_prev: float32 [32768], P(('blk', 'sub')), may hold values from -6 to 6
- row_count: int32 [32], P(('blk', 'sub')), may hold values from 256 to 1024, as said below
- owner_table: int32 [32, 128], P(('blk', 'sub')), may hold values from 0 to 4, as said below
- landing_cell: int32 [32, 1536], P(('blk', 'sub')), may hold values from 0 to 1023
- solid_temp: float32 [256, 128, 256], P('blk', 'sub'), may hold values from -6 to 6
- conductivity: float32 [256, 128, 256], P('blk', 'sub'), may hold values from 0.2 to 5
- sink: float32 [256, 128, 256], P('blk', 'sub'), may hold values from 0.2 to 2
- heat_source: float32 [256, 128, 256], P('blk', 'sub'), may hold values from -6 to 6
Outputs:
- fluid_new: float32 [256, 128, 512], P('blk', 'sub')
- solid_new: float32 [256, 128, 256], P('blk', 'sub')
- wall_new: float32 [32768], P(('blk', 'sub'))
The draws below stay inside these ranges and needn't reach their ends.
Inputs may be any that keep to these rules, and one draw needn't show every extreme that they name: `row_count`: live rows of a fluid block; some block has all 1024 live in every draw. `owner_table`: no group points outside the grid of blocks; at least half of a block's groups are 0; at most 16 groups of a block have any one direction from 1 to 4, and some solid block receives exactly that many from every neighbour it has.
All inputs are finite; a program needn't handle non-finite values.
Results may differ from the reference program's by a relative error of at most 0.0003.
Values sent between devices are 32-bit elements; how exact they have to be, the bound alone decides.
No kernel may reach another device: no remote copies, remote signals or barrier semaphores. Data moves between devices by JAX's collectives and lax.ppermute only.
A program may use at most 128 MiB of HBM per device.

```python
import math
import jax
import jax.numpy as jnp
from jax import lax

FX = 32
FY = 32
FZ = 512
SX = 32
SY = 32
SZ = 256
CAP = 8
FLUID_SWEEPS = 2
SWEEPS = 8
OWNERS = 32
ROWS = 1024
GROUPS = 128
NEAR_GROUPS = 16
NEAR_ROWS = 128
INCOMING = 1536
TOTAL_ROWS = 32768
SURF = 1024
NX = 256
NY = 128
NSX = 256
NSY = 128
N_BLK = 8
N_SUB = 4


def draw_row_count(key, part):
    first_key = jax.random.fold_in(key, 11)
    second_key = jax.random.fold_in(key, 23)
    counts = jax.random.randint(first_key, (OWNERS,), ROWS // 4, ROWS + 1)
    fullest = jax.random.randint(second_key, (), 0, OWNERS)
    return jnp.where(jnp.arange(OWNERS) == fullest, ROWS, counts).astype(jnp.int32)


def draw_owner_table(key, part):
    count_key = jax.random.fold_in(key, 31)
    pick_key = jax.random.fold_in(key, 37)
    shuffle_key = jax.random.fold_in(key, 41)
    owner_ids = jnp.arange(OWNERS, dtype=jnp.int32)
    blk_of = owner_ids // N_SUB
    sub_of = owner_ids % N_SUB
    blk_total = OWNERS // N_SUB
    valid_dir = jnp.stack([blk_of + 1 < blk_total, blk_of > 0, sub_of + 1 < N_SUB, sub_of > 0], axis=1)
    offsets = jnp.array([N_SUB, -N_SUB, 1, -1], dtype=jnp.int32)
    target = owner_ids[:, None] + offsets[None, :]
    chosen = jax.random.randint(pick_key, (), 0, OWNERS)
    counts = jax.random.randint(count_key, (OWNERS, 4), 0, NEAR_GROUPS + 1)
    counts = jnp.where(target == chosen, NEAR_GROUPS, counts) * valid_dir.astype(jnp.int32)
    upper_end = jnp.cumsum(counts, axis=1)
    lower_end = upper_end - counts
    positions = jnp.arange(GROUPS, dtype=jnp.int32)
    inside = (positions[None, None, :] >= lower_end[:, :, None]) & (positions[None, None, :] < upper_end[:, :, None])
    dir_codes = jnp.sum(inside.astype(jnp.int32) * jnp.arange(1, 5, dtype=jnp.int32)[None, :, None], axis=1)
    owner_keys = jax.random.split(shuffle_key, OWNERS)
    orders = jax.vmap(lambda sub_key: jax.random.permutation(sub_key, GROUPS))(owner_keys)
    return jnp.take_along_axis(dir_codes, orders, axis=1).astype(jnp.int32)


def draw_landing_cell(key, part):
    row_index = jnp.arange(ROWS, dtype=jnp.int32)
    base_x = row_index // FY * SX // FX
    base_y = row_index % FY * SY // FY
    jitter_x = jax.random.randint(jax.random.fold_in(key, 51), (OWNERS, ROWS), -1, 2)
    jitter_y = jax.random.randint(jax.random.fold_in(key, 53), (OWNERS, ROWS), -1, 2)
    self_x = jnp.clip(base_x[None, :] + jitter_x, 0, SX - 1)
    self_y = jnp.clip(base_y[None, :] + jitter_y, 0, SY - 1)
    pieces = [self_x * SY + self_y]
    for band_no in range(4):
        depth = jax.random.randint(jax.random.fold_in(key, 61 + band_no), (OWNERS, NEAR_ROWS), 0, 2)
        along_x = jax.random.randint(jax.random.fold_in(key, 71 + band_no), (OWNERS, NEAR_ROWS), 0, SX)
        along_y = jax.random.randint(jax.random.fold_in(key, 81 + band_no), (OWNERS, NEAR_ROWS), 0, SY)
        if band_no == 0:
            pieces.append(depth * SY + along_y)
        elif band_no == 1:
            pieces.append((SX - 1 - depth) * SY + along_y)
        elif band_no == 2:
            pieces.append(along_x * SY + depth)
        else:
            pieces.append(along_x * SY + SY - 1 - depth)
    cells = jnp.concatenate(pieces, axis=1)
    cells = cells.at[0, ROWS].set(0).at[0, INCOMING - 1].set(SURF - 1)
    return cells.astype(jnp.int32)


def block_levels(key, dims, cuts, least, top_value):
    loudness = 1.0
    for position, blocks in cuts:
        steps = jax.random.uniform(jax.random.fold_in(jax.random.fold_in(key, 6), position), (blocks,), jnp.float32, least / len(cuts), top_value / len(cuts))
        loudness = loudness * jnp.repeat(jnp.exp(steps), dims[position] // blocks).reshape((-1,) + (1,) * (len(dims) - 1 - position))
    return loudness


def normal_values(stream_key, dims, width, limit, cuts=(), kind=jnp.bfloat16):
    values = width * jax.random.normal(stream_key, dims, jnp.float32)
    if cuts:
        values = values * block_levels(stream_key, dims, cuts, -0.22, 0.18)
    return jnp.clip(values, -limit, limit).astype(kind)


def setup_inputs(seed: int = 0) -> dict:
    keys = jax.random.split(jax.random.key(seed), 12)
    fluid_temp = normal_values(keys[0], (NX, NY, FZ), 1.0, 6.0, ((0, 8), (1, 4)), jnp.float32)
    velocity = normal_values(keys[1], (3, NX, NY, FZ), 1.0, 6.0, ((1, 8), (2, 4)), jnp.float32)
    eddy_diff = jnp.clip(jnp.exp(math.log(0.5) - 2.3025851 * jax.random.uniform(keys[2], (NX, NY, FZ), jnp.float32) ** block_levels(keys[2], (NX, NY, FZ), ((0, 8), (1, 4)), -0.2, 0.2)), 0.05, 0.5)
    wall_prev = normal_values(keys[3], (TOTAL_ROWS,), 1.0, 6.0, ((0, 32),), jnp.float32)
    row_count = draw_row_count(jax.random.fold_in(keys[11], 71), 0)
    owner_table = draw_owner_table(jax.random.fold_in(keys[11], 71), 0)
    landing_cell = draw_landing_cell(jax.random.fold_in(keys[11], 71), 0)
    solid_temp = normal_values(keys[7], (NSX, NSY, SZ), 1.0, 6.0, ((0, 8), (1, 4)), jnp.float32)
    conductivity = jnp.clip(jnp.exp(math.log(5.0) - 3.218876 * jax.random.uniform(keys[8], (NSX, NSY, SZ), jnp.float32) ** block_levels(keys[8], (NSX, NSY, SZ), ((0, 8), (1, 4)), -0.2, 0.2)), 0.2, 5.0)
    sink = jnp.clip(jnp.exp(math.log(2.0) - 2.3025851 * jax.random.uniform(keys[9], (NSX, NSY, SZ), jnp.float32) ** block_levels(keys[9], (NSX, NSY, SZ), ((0, 8), (1, 4)), -0.2, 0.2)), 0.2, 2.0)
    heat_source = normal_values(keys[10], (NSX, NSY, SZ), 1.0, 6.0, ((0, 8), (1, 4)), jnp.float32)
    return dict(fluid_temp=fluid_temp, velocity=velocity, eddy_diff=eddy_diff, wall_prev=wall_prev, row_count=row_count, owner_table=owner_table, landing_cell=landing_cell, solid_temp=solid_temp, conductivity=conductivity, sink=sink, heat_source=heat_source)


RELAX_FACTOR = 0.8
EIG_LOW = 0.02
EIG_HIGH = 2.0


def face_slice(values_in, axis_no, start):
    slicer = [slice(1, -1)] * 3
    slicer[axis_no] = slice(start, values_in.shape[axis_no] - 1 + start)
    return values_in[tuple(slicer)]


def fluid_update(temp_pad, velo_pad, alpha_pad):
    center_val = temp_pad[1:-1, 1:-1, 1:-1]
    residue = jnp.zeros_like(center_val)
    weight = jnp.zeros_like(center_val)
    for axis_no in range(3):
        lower_val = face_slice(temp_pad, axis_no, 0)
        upper_val = face_slice(temp_pad, axis_no, 1)
        face_speed = 0.5 * (face_slice(velo_pad[axis_no], axis_no, 0) + face_slice(velo_pad[axis_no], axis_no, 1))
        face_diff = 0.5 * (face_slice(alpha_pad, axis_no, 0) + face_slice(alpha_pad, axis_no, 1))
        face_flux = jnp.maximum(face_speed, 0.0) * lower_val + jnp.minimum(face_speed, 0.0) * upper_val - face_diff * (upper_val - lower_val)
        count_faces = face_flux.shape[axis_no]
        residue = residue - (lax.slice_in_dim(face_flux, 1, count_faces, axis=axis_no) - lax.slice_in_dim(face_flux, 0, count_faces - 1, axis=axis_no))
        face_weight = face_diff + 0.5 * jnp.abs(face_speed)
        weight = weight + lax.slice_in_dim(face_weight, 1, count_faces, axis=axis_no) + lax.slice_in_dim(face_weight, 0, count_faces - 1, axis=axis_no)
    return center_val + RELAX_FACTOR * residue / weight


def wall_pad(temp_rim, wall_temp, live_plane):
    wall_cell = temp_rim[1:-1, 1:-1, 0]
    ghost_val = jnp.pad(wall_cell + live_plane * 2.0 * (wall_temp - wall_cell), 1)
    return jnp.concatenate([ghost_val[:, :, None], temp_rim, jnp.zeros_like(ghost_val)[:, :, None]], axis=2)


def edge_pad(values_in):
    return jnp.pad(values_in, ((0, 0), (0, 0), (1, 1)), mode="edge")


def flow_pad(flow_rim):
    normal_speed = flow_rim[2]
    normal_pad = jnp.concatenate([-normal_speed[:, :, :1], normal_speed, normal_speed[:, :, -1:]], axis=2)
    velo_pad = jnp.stack([edge_pad(flow_rim[0]), edge_pad(flow_rim[1]), normal_pad])
    return velo_pad, edge_pad(flow_rim[3])


def conduct(state_pad, cond_pad, diag_extra, rhs_field):
    center_val = state_pad[1:-1, 1:-1]
    center_cond = cond_pad[1:-1, 1:-1]
    state_z = jnp.pad(center_val, ((0, 0), (0, 0), (1, 1)))
    cond_z = jnp.pad(center_cond, ((0, 0), (0, 0), (1, 1)))
    neighbours = [(state_pad[2:, 1:-1], cond_pad[2:, 1:-1]), (state_pad[:-2, 1:-1], cond_pad[:-2, 1:-1]),
                  (state_pad[1:-1, 2:], cond_pad[1:-1, 2:]), (state_pad[1:-1, :-2], cond_pad[1:-1, :-2]),
                  (state_z[:, :, 2:], cond_z[:, :, 2:]), (state_z[:, :, :-2], cond_z[:, :, :-2])]
    applied = diag_extra * center_val
    diag_sum = diag_extra
    for near_val, near_cond in neighbours:
        summed = center_cond + near_cond
        conduct_face = 2.0 * center_cond * near_cond / jnp.where(summed > 0.0, summed, 1.0)
        applied = applied + conduct_face * (center_val - near_val)
        diag_sum = diag_sum + conduct_face
    return (rhs_field - applied) / jnp.where(diag_sum > 0.0, diag_sum, 1.0)


def cheby_coefficients(count_sweeps):
    center_eig = 0.5 * (EIG_HIGH + EIG_LOW)
    half_width = 0.5 * (EIG_HIGH - EIG_LOW)
    ratio_eig = center_eig / half_width
    damping = 1.0 / ratio_eig
    coefficients = [(0.0, 1.0 / center_eig)]
    for sweep_no in range(1, count_sweeps):
        damping_new = 1.0 / (2.0 * ratio_eig - damping)
        coefficients.append((damping_new * damping, 2.0 * damping_new / half_width))
        damping = damping_new
    return coefficients


def pick_groups_all(group_dirs, dir_code):
    matched = group_dirs == dir_code
    group_rank = jnp.cumsum(matched.astype(jnp.int32), axis=1) - 1
    slot_ids = jnp.arange(NEAR_GROUPS, dtype=jnp.int32)
    return (matched[:, :, None] & (group_rank[:, :, None] == slot_ids[None, None, :])).astype(jnp.float32)


def reference(fluid_temp, velocity, eddy_diff, wall_prev, row_count, owner_table, landing_cell, solid_temp, conductivity, sink, heat_source):
    owner_total = N_BLK * N_SUB
    row_total = FX * FY
    live_rows = (jnp.arange(row_total, dtype=jnp.int32)[None, :] < row_count[:, None]).astype(jnp.float32)

    def to_plane(values_in):
        return values_in.reshape(N_BLK, N_SUB, FX, FY).transpose(0, 2, 1, 3).reshape(N_BLK * FX, N_SUB * FY)

    def from_plane(field):
        return field.reshape(N_BLK, FX, N_SUB, FY).transpose(0, 2, 1, 3).reshape(owner_total, row_total)

    wall_temp = to_plane(wall_prev.reshape(owner_total, row_total))
    live_plane = to_plane(live_rows)
    flow_stack = jnp.concatenate([velocity, eddy_diff[None]], axis=0)
    velo_pad, alpha_pad = flow_pad(jnp.pad(flow_stack, ((0, 0), (1, 1), (1, 1), (0, 0))))
    fluid_now = fluid_temp
    for sweep_no in range(FLUID_SWEEPS):
        fluid_now = fluid_update(wall_pad(jnp.pad(fluid_now, ((1, 1), (1, 1), (0, 0))), wall_temp, live_plane), velo_pad, alpha_pad)
    gas_temp = from_plane(fluid_now[:, :, 0])
    film_coeff = 2.0 * from_plane(eddy_diff[:, :, 0]) * live_rows
    dir_rows = jnp.repeat(owner_table, CAP, axis=1)
    self_mask = (dir_rows == 0).astype(jnp.float32)
    row_pair = jnp.stack([film_coeff, gas_temp], axis=1).reshape(owner_total, 2, GROUPS, CAP)
    owner_ids = jnp.arange(owner_total, dtype=jnp.int32)
    blk_of = owner_ids // N_SUB
    sub_of = owner_ids % N_SUB
    offsets = (N_SUB, -N_SUB, 1, -1)
    target_ok = (blk_of + 1 < N_BLK, blk_of > 0, sub_of + 1 < N_SUB, sub_of > 0)
    source_ok = (blk_of > 0, blk_of + 1 < N_BLK, sub_of > 0, sub_of + 1 < N_SUB)
    selections = []
    arrived = []
    for dir_index in range(4):
        selection = pick_groups_all(owner_table, dir_index + 1)
        selections.append(selection)
        outbound = jnp.einsum("ocgk,ogs->ocsk", row_pair, selection, precision=lax.Precision.HIGHEST).reshape(owner_total, 2, NEAR_ROWS)
        source = jnp.clip(owner_ids - offsets[dir_index], 0, owner_total - 1).astype(jnp.int32)
        arrived.append(jnp.where(source_ok[dir_index][:, None, None], outbound[source], 0.0))
    film_in = jnp.concatenate([film_coeff * self_mask] + [piece[:, 0] for piece in arrived], axis=1)
    gas_in = jnp.concatenate([gas_temp] + [piece[:, 1] for piece in arrived], axis=1)
    segment = (owner_ids[:, None] * SURF + landing_cell).reshape(-1).astype(jnp.int32)
    film_sum = jax.ops.segment_sum(film_in.reshape(-1), segment, num_segments=owner_total * SURF)
    film_gas = jax.ops.segment_sum((film_in * gas_in).reshape(-1), segment, num_segments=owner_total * SURF)

    def to_solid(values_in):
        return values_in.reshape(N_BLK, N_SUB, SX, SY).transpose(0, 2, 1, 3).reshape(N_BLK * SX, N_SUB * SY)

    surface_mask = (jnp.arange(SZ, dtype=jnp.int32) == 0).astype(jnp.float32)
    diag_extra = sink + to_solid(film_sum)[:, :, None] * surface_mask
    rhs_field = heat_source + to_solid(film_gas)[:, :, None] * surface_mask
    cond_pad = jnp.pad(conductivity, ((1, 1), (1, 1), (0, 0)))
    solid_now = solid_temp
    update = jnp.zeros_like(solid_temp)
    for decay, gain_term in cheby_coefficients(SWEEPS):
        scaled_res = conduct(jnp.pad(solid_now, ((1, 1), (1, 1), (0, 0))), cond_pad, diag_extra, rhs_field)
        update = decay * update + gain_term * scaled_res
        solid_now = solid_now + update
    surface = solid_now[:, :, 0].reshape(N_BLK, SX, N_SUB, SY).transpose(0, 2, 1, 3).reshape(owner_total, SURF)
    slot_values = surface[owner_ids[:, None], landing_cell]
    wall_sum = self_mask * slot_values[:, :row_total]
    for dir_index in range(4):
        band_start = row_total + dir_index * NEAR_ROWS
        band = slot_values[:, band_start:band_start + NEAR_ROWS]
        target = jnp.clip(owner_ids + offsets[dir_index], 0, owner_total - 1).astype(jnp.int32)
        returned = jnp.where(target_ok[dir_index][:, None], band[target], 0.0)
        spread = jnp.einsum("osk,ogs->ogk", returned.reshape(owner_total, NEAR_GROUPS, CAP), selections[dir_index], precision=lax.Precision.HIGHEST)
        wall_sum = wall_sum + spread.reshape(owner_total, row_total)
    wall_new = (wall_sum * live_rows).reshape(-1)
    return fluid_now, solid_now, wall_new
```

```python
import functools

import jax
import jax.numpy as jnp
from jax import lax
from jax.experimental import pallas as pl
from jax.experimental.pallas import tpu as pltpu
from jax.sharding import PartitionSpec as P

FLUID_SWEEPS = 2
SWEEPS = 8
RELAX_FACTOR = 0.8
EIG_LOW = 0.02
EIG_HIGH = 2.0
TILE = 8
LANES = 128
HIGHEST = lax.Precision.HIGHEST
VMEM = pl.BlockSpec(memory_space=pltpu.VMEM)
SMEM = pl.BlockSpec(memory_space=pltpu.SMEM)
ANY = pl.BlockSpec(memory_space=pl.ANY)


def cheby_coefficients(count_sweeps):
    center_eig = 0.5 * (EIG_HIGH + EIG_LOW)
    half_width = 0.5 * (EIG_HIGH - EIG_LOW)
    ratio_eig = center_eig / half_width
    damping = 1.0 / ratio_eig
    coefficients = [(0.0, 1.0 / center_eig)]
    for sweep_no in range(1, count_sweeps):
        damping_new = 1.0 / (2.0 * ratio_eig - damping)
        coefficients.append((damping_new * damping, 2.0 * damping_new / half_width))
        damping = damping_new
    return coefficients


def ring(value, axis, step):
    count = lax.axis_size(axis)
    return lax.ppermute(value, axis, [(i, (i + step) % count) for i in range(count)])


def chain(value, axis, step):
    count = lax.axis_size(axis)
    pairs = [(i, i + step) for i in range(count) if 0 <= i + step < count]
    return lax.ppermute(value, axis, pairs)


def sides(axis):
    place = lax.axis_index(axis)
    return place > 0, place < lax.axis_size(axis) - 1


def lasts(micros):
    return pl.CostEstimate(flops=0, bytes_accessed=int(micros * 3.69e6), transcendentals=0)


def quick_reciprocal(value):
    guess = pl.reciprocal(value, approx=True)
    return guess * (2.0 - value * guess)


def lane_index(shape):
    return lax.broadcasted_iota(jnp.int32, shape, 1)


def row_index(shape):
    return lax.broadcasted_iota(jnp.int32, shape, 0)


def first_lane(value, at_first):
    head = value[:, :LANES]
    head = jnp.where(lane_index(head.shape) == 0, at_first, head)
    if value.shape[1] == LANES:
        return head
    return jnp.concatenate([head, value[:, LANES:]], axis=1)


def last_lane(value, at_last):
    tail = value[:, -LANES:]
    tail = jnp.where(lane_index(tail.shape) == LANES - 1, at_last, tail)
    if value.shape[1] == LANES:
        return tail
    return jnp.concatenate([value[:, :-LANES], tail], axis=1)


def from_above(value, row):
    return jnp.where(row_index(value.shape) == 0, row, pltpu.roll(value, 1, 0))


def from_below(value, row):
    count = value.shape[0]
    return jnp.where(row_index(value.shape) == count - 1, row, pltpu.roll(value, count - 1, 0))


def part_depths(depth):
    return [(0, LANES), (LANES, depth - LANES)] if depth > LANES else [(0, depth)]


class Copies:
    def __init__(self, sems):
        self.sems, self.count, self.waits = sems, 0, {}

    def start(self, key, src, dst):
        made = pltpu.make_async_copy(src, dst, self.sems.at[self.count])
        self.count += 1
        made.start()
        self.waits.setdefault(key, []).append(made)

    def wait(self, key):
        for made in self.waits.pop(key, []):
            made.wait()

    def wait_all(self):
        for key in list(self.waits):
            self.wait(key)


def x_fields(temp, velo, diff, side, cells_x, zs):
    two, one = (pl.ds(0, 2), pl.ds(0, 1)) if side == 0 else (pl.ds(cells_x - 2, 2), pl.ds(cells_x - 1, 1))
    return (
        (temp.at[two, :, zs], 0, 2),
        (diff.at[two, :, zs], 2, 2),
        (velo.at[0, two, :, zs], 4, 2),
        (velo.at[1, one, :, zs], 6, 1),
        (velo.at[2, one, :, zs], 7, 1),
    )


def x_pack_kernel(cells_x, start, depth, noted, *refs):
    temp, velo, diff = refs[:3]
    notes = refs[3] if noted else None
    outs, sems = refs[-3:-1], refs[-1]
    copies = Copies(sems)
    zs = pl.ds(start, depth)
    for side in range(2):
        for src, at, count in x_fields(temp, velo, diff, side, cells_x, zs):
            copies.start(0, src, outs[side].at[pl.ds(at, count)])
        if noted:
            copies.start(0, notes.at[side], outs[side].at[8])
    copies.wait_all()


def x_pack(temp, velo, diff, notes, start, depth):
    cells_x, cells_y, _ = temp.shape
    noted = notes is not None
    shape = jax.ShapeDtypeStruct((9 if noted else 8, cells_y, depth), temp.dtype)
    return pl.pallas_call(
        functools.partial(x_pack_kernel, cells_x, start, depth, noted),
        out_shape=(shape, shape),
        in_specs=[ANY] * (4 if noted else 3),
        out_specs=(VMEM, VMEM),
        scratch_shapes=[pltpu.SemaphoreType.DMA((12,))],
        compiler_params=pltpu.CompilerParams(vmem_limit_bytes=32 * 1024 * 1024),
        cost_estimate=lasts(2),
    )(*((temp, velo, diff, notes) if noted else (temp, velo, diff)))


def y_pack_kernel(cells_x, cells_y, start, depth, noted, *refs):
    temp, velo, diff, xlo, xhi = refs[:5]
    notes = refs[5] if noted else None
    outs, (tiles, sems) = refs[-4:-2], refs[-2:]
    copies = Copies(sems)
    zs = pl.ds(start, depth)
    sources = (temp.at[:], diff.at[:], velo.at[1], velo.at[0], velo.at[2])
    for side in range(2):
        rows = pl.ds(0 if side == 0 else cells_y - TILE, TILE)
        for number, src in enumerate(sources):
            copies.start((side, number), src.at[:, rows, zs], tiles.at[side, number])
    base = 9 * cells_x if noted else 8 * cells_x
    for side in range(2):
        out = outs[side]
        first, near = (0, 0) if side == 0 else (TILE - 2, TILE - 1)
        edge = 0 if side == 0 else cells_y - 1
        for at, halo, inner in ((base, xlo, 1), (base + 4, xhi, 0)):
            for j, plane in enumerate((inner, 2 + inner, 4 + inner, 6)):
                out[pl.ds(at + j, 1), :] = halo[plane, pl.ds(edge, 1), :]
        if noted:
            out[pl.ds(8 * cells_x, cells_x), :] = notes[2 + side]
        for number in range(5):
            copies.wait((side, number))
            if number < 3:
                picks = [(2 * number, first), (2 * number + 1, first + 1)]
            else:
                picks = [(3 + number, near)]
            for plane, row in picks:
                for x in range(cells_x):
                    out[pl.ds(plane * cells_x + x, 1), :] = tiles[side, number, x, pl.ds(row, 1), :]


def y_pack(temp, velo, diff, xlo, xhi, notes, start, depth):
    cells_x, cells_y, _ = temp.shape
    noted = notes is not None
    shape = jax.ShapeDtypeStruct(((9 if noted else 8) * cells_x + TILE, depth), temp.dtype)
    return pl.pallas_call(
        functools.partial(y_pack_kernel, cells_x, cells_y, start, depth, noted),
        out_shape=(shape, shape),
        in_specs=[ANY] * 3 + [VMEM] * (3 if noted else 2),
        out_specs=(VMEM, VMEM),
        scratch_shapes=[
            pltpu.VMEM((2, 5, cells_x, TILE, depth), jnp.float32),
            pltpu.SemaphoreType.DMA((10,)),
        ],
        compiler_params=pltpu.CompilerParams(vmem_limit_bytes=32 * 1024 * 1024),
        cost_estimate=lasts(2),
    )(temp, velo, diff, xlo, xhi, *((notes,) if noted else ()))


def face(a_low, a_high, u_low, u_high):
    a_two = a_low + a_high
    u_two = u_low + u_high
    plus = a_two + jnp.maximum(u_two, 0.0)
    return plus, plus - u_two


def relaxation(a, ut, uz, low, high, above, below, live_two, wall):
    depth = a.shape[1]
    p_above, q_above = face(from_above(a, above[0]), a, from_above(ut, above[1]), ut)
    p_below, q_below = face(a, from_below(a, below[0]), ut, from_below(ut, below[1]))
    p_down, q_down = face(pltpu.roll(a, 1, 1), a, pltpu.roll(uz, 1, 1), uz)
    p_up, q_up = pltpu.roll(p_down, depth - 1, 1), pltpu.roll(q_down, depth - 1, 1)
    a_first = 2.0 * a[:, :LANES]
    u_last = 2.0 * uz[:, -LANES:]
    plus_last = 2.0 * a[:, -LANES:] + jnp.maximum(u_last, 0.0)
    weight = (low[0] + low[1]) + (high[0] + high[1]) + (p_above + q_above) + (p_below + q_below)
    weight = weight + first_lane(p_down + q_down, 2.0 * a_first) + last_lane(p_up + q_up, 2.0 * plus_last - u_last)
    factor = (2.0 * RELAX_FACTOR) * quick_reciprocal(weight)
    gain = a_first * live_two
    p_down, q_down = first_lane(p_down, 0.0), first_lane(q_down, gain)
    p_up, q_up = last_lane(p_up, plus_last), last_lane(q_up, 0.0)
    leaving = (low[1] + high[0]) + (q_above + p_below) + (q_down + p_up)
    ghost = jnp.where(lane_index(gain.shape) == 0, gain * wall * factor[:, :LANES], 0.0)
    return (low[0] * factor, high[1] * factor, p_above * factor, q_below * factor, p_down * factor, q_up * factor,
            1.0 - leaving * factor, ghost)


def apply(factors, t, t_low, t_high, t_above, t_below):
    depth = t.shape[1]
    new = factors[6] * t + (factors[0] * t_low + factors[1] * t_high)
    new = new + (factors[2] * from_above(t, t_above) + factors[3] * from_below(t, t_below))
    new = new + (factors[4] * pltpu.roll(t, 1, 1) + factors[5] * pltpu.roll(t, depth - 1, 1))
    head = new[:, :LANES] + factors[7]
    return head if depth == LANES else jnp.concatenate([head, new[:, LANES:]], axis=1)


def fluid_kernel(cells_x, cells_y, depth, parts, at_wall, flags, temp, velo, diff, wall_t, *refs):
    halos, refs = refs[:4 * len(parts)], refs[4 * len(parts):]
    out, (ts, us, as_, vs, ws, t1, yl, yc, xn, yn, cs, ks, sems) = refs[:-13], refs[-13:]
    rows_total = flags[4]
    xlo, xhi, ylo, yhi = (halos[i::4] for i in range(4))
    mid = pl.ds(TILE, cells_y)
    copies = Copies(sems)
    for (start, size), *strips in zip(parts, xlo, xhi, ylo, yhi):
        zs = pl.ds(start, size)
        for side in range(2):
            halo, key = strips[2 + side], "y"
            noted = start == 0
            for plane in range(8):
                copies.start(key, halo.at[pl.ds(plane * cells_x, cells_x)],
                             yl.at[side, plane, pl.ds(TILE, cells_x), zs])
            copies.start(key, halo.at[pl.ds((9 if noted else 8) * cells_x, TILE)], yc.at[side, :, zs])
            if noted:
                copies.start(key, halo.at[pl.ds(8 * cells_x, cells_x), pl.ds(0, LANES)], yn.at[side])
        for side in range(2):
            halo, at = strips[side], 0 if side == 0 else cells_x + 2
            near = 0 if side == 0 else cells_x + 1
            key = "x"
            copies.start(key, halo.at[pl.ds(0, 2)], ts.at[pl.ds(at, 2), mid, zs])
            copies.start(key, halo.at[pl.ds(2, 2)], as_.at[pl.ds(at, 2), mid, zs])
            copies.start(key, halo.at[pl.ds(4, 2)], us.at[pl.ds(at, 2), :, zs])
            copies.start(key, halo.at[pl.ds(6, 1)], vs.at[pl.ds(near, 1), mid, zs])
            copies.start(key, halo.at[pl.ds(7, 1)], ws.at[pl.ds(near, 1), :, zs])
            if start == 0:
                copies.start(key, halo.at[8, :, pl.ds(0, LANES)], xn.at[side])
    zs = pl.ds(0, depth)
    step = TILE
    starts = list(range(0, cells_x, step))
    for start in starts:
        here = pl.ds(start, step)
        copies.start(start, temp.at[here, :, zs], ts.at[pl.ds(start + 2, step), mid])
        copies.start(start, diff.at[here, :, zs], as_.at[pl.ds(start + 2, step), mid])
        copies.start(start, velo.at[0, here, :, zs], us.at[pl.ds(start + 2, step)])
        copies.start(start, velo.at[1, here, :, zs], vs.at[pl.ds(start + 1, step), mid])
        copies.start(start, velo.at[2, here, :, zs], ws.at[pl.ds(start + 1, step)])

    copies.wait("y")
    copies.wait("x")
    for side, row in ((0, TILE - 1), (1, TILE + cells_y)):
        inner = 1 - side
        for corner, at in ((0, TILE - 1), (4, TILE + cells_x)):
            for j, plane in enumerate((inner, 2 + inner, 6, 4 + inner)):
                yl[side, plane, pl.ds(at, 1), :] = yc[side, pl.ds(corner + j, 1), :]
        for j in range(cells_x + 2):
            at = pl.ds(TILE - 1 + j, 1)
            ts[j + 1, pl.ds(row, 1), :] = yl[side, inner, at, :]
            as_[j + 1, pl.ds(row, 1), :] = yl[side, 2 + inner, at, :]
            vs[j, pl.ds(row, 1), :] = yl[side, 4 + inner, at, :]

    def plane_factors(i, live_two, wall):
        a, un = as_[i + 1, mid, :], us[i + 1]
        low = face(as_[i, mid, :], a, us[i], un)
        high = face(a, as_[i + 2, mid, :], un, us[i + 2])
        up, down = pl.ds(TILE - 1, 1), pl.ds(TILE + cells_y, 1)
        return relaxation(a, vs[i, mid, :], ws[i], low, high, (as_[i + 1, up, :], vs[i, up, :]),
                          (as_[i + 1, down, :], vs[i, down, :]), live_two, wall)

    def plane_apply(factors, ref, i):
        up, down = pl.ds(TILE - 1, 1), pl.ds(TILE + cells_y, 1)
        return apply(factors, ref[i, mid, :], ref[i - 1, mid, :], ref[i + 1, mid, :], ref[i, up, :], ref[i, down, :])

    def note_of(note):
        return note, pltpu.roll(note, LANES - 1, 1)

    def first_sweep(i, carry):
        place = (i - 1) * cells_y + row_index((cells_y, LANES))
        live_two = jnp.where(place < rows_total, 2.0, 0.0)
        factors = plane_factors(i, live_two, pltpu.roll(wall_t[...], LANES + 1 - i, 1))
        for j in range(7):
            cs[j, i - 1] = factors[j]
        ks[i - 1] = factors[7]
        t1[i, mid, :] = plane_apply(factors, ts, i + 1)
        return carry

    def halo_plane(i, side):
        factors = plane_factors(i, *note_of(xn[side]))
        t1[i, mid, :] = jnp.where(flags[side] > 0, plane_apply(factors, ts, i + 1), 0.0)

    for start in starts:
        copies.wait(start)
        if start == 0:
            halo_plane(0, 0)
        last = cells_x + 1 if start == starts[-1] else start + step
        lax.fori_loop(max(start, 1), last, first_sweep, 0, unroll=4 if at_wall else 1)
    halo_plane(cells_x + 1, 1)

    for side, row in ((0, TILE - 1), (1, TILE + cells_y)):
        inner = 1 - side
        own = TILE if side == 0 else TILE + cells_y - 1
        rows, up, down = pl.ds(TILE, cells_x), pl.ds(TILE - 1, 1), pl.ds(TILE + cells_x, 1)

        def own_rows(ref, off):
            return jnp.concatenate([ref[off + x, pl.ds(own, 1), :] for x in range(cells_x)], axis=0)

        t, a, un = yl[side, inner, rows, :], yl[side, 2 + inner, rows, :], yl[side, 4 + inner, rows, :]
        t_far, a_far, un_far = (yl[side, 1 - inner, rows, :], yl[side, 3 - inner, rows, :],
                                yl[side, 5 - inner, rows, :])
        t_own, a_own, un_own = own_rows(ts, 2), own_rows(as_, 2), own_rows(vs, 1)
        if side == 0:
            low, high = face(a_far, a, un_far, un), face(a, a_own, un, un_own)
            t_low, t_high = t_far, t_own
        else:
            low, high = face(a_own, a, un_own, un), face(a, a_far, un, un_far)
            t_low, t_high = t_own, t_far
        factors = relaxation(
            a, yl[side, 6, rows, :], yl[side, 7, rows, :], low, high,
            (yl[side, 2 + inner, up, :], yl[side, 6, up, :]), (yl[side, 2 + inner, down, :], yl[side, 6, down, :]),
            *note_of(yn[side]))
        new = apply(factors, t, t_low, t_high, yl[side, inner, up, :], yl[side, inner, down, :])
        new = jnp.where(flags[2 + side] > 0, new, 0.0)
        for x in range(cells_x):
            t1[1 + x, pl.ds(row, 1), :] = new[x:x + 1, :]

    if at_wall:
        gas, film = out
        gas[...] = jnp.zeros_like(gas)
        film[...] = jnp.zeros_like(film)

        def second_wall(i, carry):
            factors = [cs[j, i - 1] for j in range(7)] + [ks[i - 1]]
            lane = lane_index((cells_y, LANES))
            shift = i - 1
            new = pltpu.roll(plane_apply(factors, t1, i)[:, :LANES], shift, 1)
            wall_diff = pltpu.roll(as_[i + 1, mid, pl.ds(0, LANES)], shift, 1)
            place = shift * cells_y + row_index((cells_y, LANES))
            wall_film = jnp.where(place < rows_total, 2.0 * wall_diff, 0.0)
            gas[...] = jnp.where(lane == shift, new, gas[...])
            film[...] = jnp.where(lane == shift, wall_film, film[...])
            return carry

        lax.fori_loop(1, cells_x + 1, second_wall, 0, unroll=4)
    else:
        def second_sweep(i, carry):
            factors = [cs[j, i - 1] for j in range(7)] + [ks[i - 1]]
            ts[i - 1, mid, :] = plane_apply(factors, t1, i)
            return carry

        for start in starts:
            lax.fori_loop(start + 1, start + step + 1, second_sweep, 0)
            copies.start("out", ts.at[pl.ds(start, step), mid], out[0].at[pl.ds(start, step)])
        copies.wait("out")


def fluid_call(temp, velo, diff, wall_t, flags, halos, depth, parts, at_wall):
    cells_x, cells_y, _ = temp.shape
    wide = cells_y + 2 * TILE
    chunks = cells_x // TILE
    plane = jax.ShapeDtypeStruct((cells_y, LANES), temp.dtype)
    copy_count = len(parts) * 28 + 4 + 6 * chunks
    return pl.pallas_call(
        functools.partial(fluid_kernel, cells_x, cells_y, depth, parts, at_wall),
        out_shape=(plane, plane) if at_wall else jax.ShapeDtypeStruct(temp.shape, temp.dtype),
        in_specs=[SMEM, ANY, ANY, ANY, VMEM] + [ANY] * len(halos),
        out_specs=(VMEM, VMEM) if at_wall else ANY,
        scratch_shapes=[
            pltpu.VMEM((cells_x + 4, wide, depth), jnp.float32),
            pltpu.VMEM((cells_x + 4, cells_y, depth), jnp.float32),
            pltpu.VMEM((cells_x + 4, wide, depth), jnp.float32),
            pltpu.VMEM((cells_x + 2, wide, depth), jnp.float32),
            pltpu.VMEM((cells_x + 2, cells_y, depth), jnp.float32),
            pltpu.VMEM((cells_x + 2, wide, depth), jnp.float32),
            pltpu.VMEM((2, 8, cells_x + 2 * TILE, depth), jnp.float32),
            pltpu.VMEM((2, TILE, depth), jnp.float32),
            pltpu.VMEM((2, cells_y, LANES), jnp.float32),
            pltpu.VMEM((2, cells_x, LANES), jnp.float32),
            pltpu.VMEM((7, cells_x, cells_y, depth), jnp.float32),
            pltpu.VMEM((cells_x, cells_y, LANES), jnp.float32),
            pltpu.SemaphoreType.DMA((copy_count,)),
        ],
        compiler_params=pltpu.CompilerParams(vmem_limit_bytes=52 * 1024 * 1024),
        cost_estimate=lasts(6 if at_wall else 18),
    )(flags, temp, velo, diff, wall_t, *halos)


def solid_kernel(
    cells_x, cells_y, depth, pad, coefficients,
    flags, cond, sink, heat, temp, xlo, xhi, ylo, yhi, film, film_lo, film_hi,
    out, surface, ks, es, bs, us, vs, gx, gy, gz, ss, ps, fs, sems,
):
    wide_x, wide_y = cells_x + 2 * pad, cells_y + 2 * TILE
    copies = Copies(sems)
    own_x, own_y = pl.ds(pad, cells_x), pl.ds(TILE, cells_y)
    for field, (src, dst) in enumerate(((cond, ks), (sink, es), (heat, bs), (temp, us))):
        for s, d in (
            (src, dst.at[own_x, own_y]),
            (xlo.at[field], dst.at[pl.ds(0, pad), own_y]),
            (xhi.at[field], dst.at[pl.ds(pad + cells_x, pad), own_y]),
            (ylo.at[field], dst.at[:, pl.ds(0, TILE)]),
            (yhi.at[field], dst.at[:, pl.ds(TILE + cells_y, TILE)]),
        ):
            copies.start(field // 2, s, d)
    fs[:, pl.ds(0, TILE), :] = jnp.where(flags[2] > 0, film_lo[...], 0.0)
    fs[:, own_y, :] = film[...]
    fs[:, pl.ds(TILE + cells_y, TILE), :] = jnp.where(flags[3] > 0, film_hi[...], 0.0)

    def harmonic(k, near):
        total = jnp.maximum(k + near, 1e-30)
        return (2.0 * k * near) * quick_reciprocal(total)

    def film_of(kind, x):
        return pltpu.roll(fs[kind], 2 * LANES + pad - x, 1)

    def add_first(value, extra):
        head = value[:, :LANES]
        head = head + jnp.where(lane_index(head.shape) == 0, extra, 0.0)
        return jnp.concatenate([head, value[:, LANES:]], axis=1) if depth > LANES else head

    gx[0, :, :] = jnp.zeros((wide_y, depth), jnp.float32)
    edge = row_index((wide_y, depth)) == wide_y - 1
    top = lane_index((wide_y, depth)) == depth - 1

    def conductances(x, carry):
        keep = jnp.where(x < wide_x - 1, 1.0, 0.0)
        follow = jnp.minimum(x + 1, wide_x - 1)
        k = ks[x]
        face_x = harmonic(k, ks[follow]) * keep
        face_y = jnp.where(edge, 0.0, harmonic(k, pltpu.roll(k, wide_y - 1, 0)))
        face_z = jnp.where(top, 0.0, harmonic(k, pltpu.roll(k, depth - 1, 1)))
        diag = add_first(es[x], film_of(0, x))
        diag = diag + (gx[x] + face_x) + (face_y + pltpu.roll(face_y, 1, 0))
        diag = diag + (face_z + pltpu.roll(face_z, 1, 1))
        gx[x + 1] = face_x
        gy[x] = face_y
        gz[x] = face_z
        es[x] = diag
        ss[x] = lax.rsqrt(jnp.maximum(diag, 1e-30))
        return carry

    copies.wait(0)
    lax.fori_loop(0, wide_x, conductances, 0, unroll=2)

    def scale(x, carry):
        follow = jnp.minimum(x + 1, wide_x - 1)
        s = ss[x]
        gx[x + 1] = gx[x + 1] * s * ss[follow]
        gy[x] = gy[x] * s * pltpu.roll(s, wide_y - 1, 0)
        gz[x] = gz[x] * s * pltpu.roll(s, depth - 1, 1)
        bs[x] = add_first(bs[x], film_of(1, x)) * s
        us[x] = us[x] * es[x] * s
        return carry

    copies.wait(1)
    lax.fori_loop(0, wide_x, scale, 0, unroll=2)

    total = len(coefficients)
    src, dst = us, vs
    for number, (decay, gain) in enumerate(coefficients):
        last = number == total - 1
        margin = total - 1 - number

        def one(x, carry, src=src, dst=dst, decay=decay, gain=gain, number=number, last=last):
            here = src[x]
            g_y, g_z = gy[x], gz[x]
            total_in = gx[x] * src[x - 1] + gx[x + 1] * src[x + 1]
            total_in += g_y * pltpu.roll(here, wide_y - 1, 0) + pltpu.roll(g_y * here, 1, 0)
            total_in += g_z * pltpu.roll(here, depth - 1, 1) + pltpu.roll(g_z * here, 1, 1)
            step = gain * ((bs[x] - here) + total_in)
            if number > 0:
                step = step + decay * ps[x]
            fresh = here + step
            if last:
                final = (fresh * ss[x])[TILE:TILE + cells_y]
                out[x - pad] = final
                shift = x - pad
                lane = lane_index((cells_y, LANES))
                surface[...] = jnp.where(lane == shift, pltpu.roll(final[:, :LANES], shift, 1), surface[...])
            else:
                ps[x] = step
                dst[x] = fresh
            return carry

        if last:
            surface[...] = jnp.zeros_like(surface)
        lax.fori_loop(pad - margin, pad + cells_x + margin, one, 0, unroll=2)
        src, dst = dst, src


def solid_x_kernel(cells_x, pad, *refs):
    outs, sems = refs[4:6], refs[6]
    copies = Copies(sems)
    for field in range(4):
        copies.start(0, refs[field].at[pl.ds(0, pad)], outs[0].at[field])
        copies.start(0, refs[field].at[pl.ds(cells_x - pad, pad)], outs[1].at[field])
    copies.wait_all()


def solid_y_kernel(cells_x, cells_y, pad, *refs):
    xlo, xhi = refs[4:6]
    outs, sems = refs[6:8], refs[8]
    copies = Copies(sems)
    for field in range(4):
        for side in range(2):
            rows = pl.ds(0 if side == 0 else cells_y - TILE, TILE)
            out = outs[side]
            copies.start(0, refs[field].at[:, rows], out.at[field, pl.ds(pad, cells_x)])
            copies.start(0, xlo.at[field, :, rows], out.at[field, pl.ds(0, pad)])
            copies.start(0, xhi.at[field, :, rows], out.at[field, pl.ds(pad + cells_x, pad)])
    copies.wait_all()


def solid_halo(cond, sink, heat, temp, pad):
    cells_x, cells_y, depth = cond.shape
    fields = (cond, sink, heat, temp)
    x_shape = jax.ShapeDtypeStruct((4, pad, cells_y, depth), cond.dtype)
    low, high = pl.pallas_call(
        functools.partial(solid_x_kernel, cells_x, pad),
        out_shape=(x_shape, x_shape), in_specs=[ANY] * 4, out_specs=(VMEM, VMEM),
        scratch_shapes=[pltpu.SemaphoreType.DMA((8,))],
        compiler_params=pltpu.CompilerParams(vmem_limit_bytes=32 * 1024 * 1024),
        cost_estimate=lasts(2),
    )(*fields)
    xlo, xhi = chain(high, "blk", 1), chain(low, "blk", -1)
    y_shape = jax.ShapeDtypeStruct((4, cells_x + 2 * pad, TILE, depth), cond.dtype)
    low, high = pl.pallas_call(
        functools.partial(solid_y_kernel, cells_x, cells_y, pad),
        out_shape=(y_shape, y_shape), in_specs=[ANY] * 6, out_specs=(VMEM, VMEM),
        scratch_shapes=[pltpu.SemaphoreType.DMA((24,))],
        compiler_params=pltpu.CompilerParams(vmem_limit_bytes=32 * 1024 * 1024),
        cost_estimate=lasts(3),
    )(*fields, xlo, xhi)
    return xlo, xhi, chain(high, "sub", 1), chain(low, "sub", -1)


def solid_step(flags, cond, sink, heat, temp, halo, films, pad):
    cells_x, cells_y, depth = cond.shape
    wide_x, wide_y = cells_x + 2 * pad, cells_y + 2 * TILE
    area = pltpu.VMEM((wide_x, wide_y, depth), jnp.float32)
    return pl.pallas_call(
        functools.partial(solid_kernel, cells_x, cells_y, depth, pad, cheby_coefficients(SWEEPS)),
        out_shape=(jax.ShapeDtypeStruct((cells_x, cells_y, depth), cond.dtype),
                   jax.ShapeDtypeStruct((cells_y, LANES), cond.dtype)),
        in_specs=[SMEM] + [ANY] * 8 + [VMEM] * 3,
        out_specs=(VMEM, VMEM),
        scratch_shapes=[area] * 5
        + [pltpu.VMEM((wide_x + 1, wide_y, depth), jnp.float32)]
        + [area] * 4
        + [pltpu.VMEM((2, wide_y, LANES), jnp.float32), pltpu.SemaphoreType.DMA((20,))],
        compiler_params=pltpu.CompilerParams(vmem_limit_bytes=48 * 1024 * 1024),
        cost_estimate=lasts(30),
    )(flags, cond, sink, heat, temp, *halo, *films)


def ones_where(condition):
    return jnp.where(condition, 1.0, 0.0)


def route_kernel(group_total, slot_cap, owner, out):
    dirs = owner[...]
    row_total = group_total * slot_cap
    codes = row_index((TILE, group_total))
    matched = ones_where((codes >= 1) & (codes <= 4) & (dirs == codes))
    before = ones_where(row_index((group_total, group_total)) < lane_index((group_total, group_total)))
    rank = jnp.dot(matched, before, precision=HIGHEST)
    start = jnp.where(matched > 0.5, rank * slot_cap, -1.0 * row_total)
    start = jnp.where(codes == 0, ones_where(dirs == 0), start)
    spread = ones_where(row_index((group_total, row_total)) == lane_index((group_total, row_total)) // slot_cap)
    wide = jnp.dot(start, spread, precision=HIGHEST)
    within = (lane_index((TILE, row_total)) % slot_cap).astype(jnp.float32)
    out[...] = jnp.where(row_index((TILE, row_total)) == 0, wide, wide + within)


def cell_values(plane_t, cells_x, cells_y, cells):
    count = cells.shape[1]
    in_x = ones_where(row_index((cells_x, count)) == cells // cells_y)
    in_y = ones_where(row_index((cells_y, count)) == cells % cells_y)
    lines = jnp.dot(plane_t[:, :cells_x], in_x, precision=HIGHEST)
    return jnp.sum(lines * in_y, axis=0, keepdims=True)


def rows_kernel(cells_x, cells_y, near_rows, route, gas_t, film_t, pair, *outs):
    row_total = cells_x * cells_y
    cells = lane_index((1, row_total))
    film = cell_values(film_t[...], cells_x, cells_y, cells)
    gas = cell_values(gas_t[...], cells_x, cells_y, cells)
    values = jnp.concatenate([film, gas], axis=0)
    pair[...] = values
    for d in range(4):
        slots = route[d + 1:d + 2, :].astype(jnp.int32)
        pick = ones_where(row_index((near_rows, row_total)) == slots)
        outs[d][...] = lax.dot_general(values, pick, (((1,), (1,)), ((), ())), precision=HIGHEST)


def film_kernel(cells_x, cells_y, pad, flags, route, landing, pair, from_0, from_1, from_2, from_3, plane, low, high):
    cells = landing[...]
    slots = cells.shape[1]
    arrived = [jnp.where(flags[d] > 0, piece[...], 0.0) for d, piece in enumerate((from_0, from_1, from_2, from_3))]
    own = pair[...]
    film = jnp.concatenate([own[:1] * route[0:1, :]] + [piece[:1] for piece in arrived], axis=1)
    gas = jnp.concatenate([own[1:]] + [piece[1:] for piece in arrived], axis=1)
    in_x = ones_where(row_index((LANES, slots)) == cells // cells_y)
    in_y = ones_where(row_index((cells_y, slots)) == cells % cells_y)
    weighted = jnp.concatenate([in_y * film, in_y * (film * gas)], axis=0)
    total = lax.dot_general(weighted, in_x, (((1,), (1,)), ((), ())), precision=HIGHEST)
    lane = lane_index(total.shape)
    to_high = jnp.where(lane >= LANES - pad, pltpu.roll(total, LANES - cells_x, 1), 0.0)
    to_low = jnp.where((lane >= cells_x) & (lane < cells_x + pad), pltpu.roll(total, cells_x, 1), 0.0)
    for ref, value in ((plane, total), (low, to_low), (high, to_high)):
        ref[0] = value[:cells_y]
        ref[1] = value[cells_y:]


def widen_kernel(cells_y, flags, plane, low, high, out, first, last):
    total = plane[...] + jnp.where(flags[0] > 0, low[...], 0.0) + jnp.where(flags[1] > 0, high[...], 0.0)
    out[...] = total
    first[...] = total[:, :TILE]
    last[...] = total[:, cells_y - TILE:]


def gather_kernel(cells_x, cells_y, row_total, near_rows, landing, surface_t, own, *outs):
    values = cell_values(surface_t[...], cells_x, cells_y, landing[...])
    own[...] = values[:, :row_total]
    for d in range(4):
        outs[d][...] = values[:, row_total + d * near_rows:row_total + (d + 1) * near_rows]


def wall_kernel(near_rows, flags, route, own, from_0, from_1, from_2, from_3, out):
    row_total = own.shape[1]
    total = own[...] * route[0:1, :]
    for d, (piece, side) in enumerate(((from_0, 1), (from_1, 0), (from_2, 3), (from_3, 2))):
        slots = route[d + 1:d + 2, :].astype(jnp.int32)
        pick = ones_where(row_index((near_rows, row_total)) == slots)
        total = total + jnp.dot(jnp.where(flags[side] > 0, piece[...], 0.0), pick, precision=HIGHEST)
    out[...] = jnp.where(lane_index((1, row_total)) < flags[4], total, 0.0)


def small_call(kernel, shapes, flags, *args):
    lead = [] if flags is None else [flags]
    return pl.pallas_call(
        kernel,
        out_shape=tuple(jax.ShapeDtypeStruct(shape, jnp.float32) for shape in shapes),
        in_specs=[SMEM] * len(lead) + [VMEM] * len(args),
        out_specs=tuple(VMEM for _ in shapes),
        compiler_params=pltpu.CompilerParams(vmem_limit_bytes=32 * 1024 * 1024),
        cost_estimate=lasts(1),
    )(*lead, *args)


def on_device(
    fluid_temp, velocity, eddy_diff, wall_prev, row_count, owner_table, landing_cell,
    solid_temp, conductivity, sink, heat_source,
):
    cells_x, cells_y, cells_z = fluid_temp.shape
    solid_x, solid_y, solid_z = solid_temp.shape
    row_total = cells_x * cells_y
    group_total = owner_table.shape[1]
    slot_cap = row_total // group_total
    near_rows = group_total // 8 * slot_cap
    pad = SWEEPS
    wall_plane = wall_prev.reshape(cells_x, cells_y)
    live_two = jnp.where(jnp.arange(row_total, dtype=jnp.int32) < row_count[0], 2.0, 0.0).reshape(cells_x, cells_y)
    flags = jnp.concatenate([jnp.stack([*sides("blk"), *sides("sub")]).astype(jnp.int32), row_count])

    both = jnp.stack([live_two, wall_plane])
    edges = jnp.stack([both[:, 0], both[:, -1], both[:, :, 0], both[:, :, -1]])
    notes = jnp.pad(edges.transpose(0, 2, 1), ((0, 0), (0, 0), (0, LANES - 2)))
    wall_t = jnp.pad(wall_plane.T, ((0, 0), (0, LANES - cells_x)))

    parts = part_depths(cells_z)
    strips = []
    for start, size in parts:
        here = notes if start == 0 else None
        low, high = x_pack(fluid_temp, velocity, eddy_diff, here, start, size)
        xlo, xhi = chain(high, "blk", 1), chain(low, "blk", -1)
        low, high = y_pack(fluid_temp, velocity, eddy_diff, xlo, xhi, here, start, size)
        strips.append((xlo, xhi, chain(high, "sub", 1), chain(low, "sub", -1)))
    fluid = (fluid_temp, velocity, eddy_diff, wall_t, flags)
    gas_t, film_t = fluid_call(*fluid, strips[0], parts[0][1], parts[:1], True)
    halo = solid_halo(conductivity, sink, heat_source, solid_temp, pad)
    fluid_new = fluid_call(*fluid, sum(strips, ()), cells_z, parts, False)

    (route,) = small_call(
        functools.partial(route_kernel, group_total, slot_cap), [(TILE, row_total)], None, owner_table
    )
    pair, *bands = small_call(
        functools.partial(rows_kernel, cells_x, cells_y, near_rows),
        [(2, row_total)] + [(2, near_rows)] * 4, None, route, gas_t, film_t,
    )
    moves = (("blk", 1), ("blk", -1), ("sub", 1), ("sub", -1))
    arrived = [ring(band, axis, step) for band, (axis, step) in zip(bands, moves)]
    plane = (2, solid_y, LANES)
    film, low, high = small_call(
        functools.partial(film_kernel, solid_x, solid_y, pad), [plane] * 3, flags, route, landing_cell, pair, *arrived
    )
    film, first, last = small_call(
        functools.partial(widen_kernel, solid_y), [plane] + [(2, TILE, LANES)] * 2,
        flags, film, ring(high, "blk", 1), ring(low, "blk", -1),
    )
    films = (film, ring(last, "sub", 1), ring(first, "sub", -1))
    solid_new, surface_t = solid_step(flags, conductivity, sink, heat_source, solid_temp, halo, films, pad)

    own, *backs = small_call(
        functools.partial(gather_kernel, solid_x, solid_y, row_total, near_rows),
        [(1, row_total)] + [(1, near_rows)] * 4, None, landing_cell, surface_t,
    )
    returned = [ring(back, axis, -step) for back, (axis, step) in zip(backs, moves)]
    (wall_new,) = small_call(
        functools.partial(wall_kernel, near_rows), [(1, row_total)], flags, route, own, *returned
    )
    return fluid_new, solid_new, wall_new.reshape(row_total)


def solution(mesh):
    return jax.shard_map(
        on_device,
        mesh=mesh,
        in_specs=(
            P("blk", "sub", None),
            P(None, "blk", "sub", None),
            P("blk", "sub", None),
            P(("blk", "sub")),
            P(("blk", "sub")),
            P(("blk", "sub"), None),
            P(("blk", "sub"), None),
            P("blk", "sub", None),
            P("blk", "sub", None),
            P("blk", "sub", None),
            P("blk", "sub", None),
        ),
        out_specs=(P("blk", "sub", None), P("blk", "sub", None), P(("blk", "sub"))),
        check_vma=False,
    )
```

```python
import functools

import jax
import jax.numpy as jnp
from jax import lax
from jax.experimental import pallas as pl
from jax.experimental.pallas import tpu as pltpu
from jax.sharding import PartitionSpec as P

FLUID_SWEEPS = 2
SWEEPS = 8
RELAX_FACTOR = 0.8
EIG_LOW = 0.02
EIG_HIGH = 2.0
TILE = 8
LANES = 128
VMEM_ALL = 60 * 1024 * 1024
BATCH = 8
HIGHEST = lax.Precision.HIGHEST
VMEM = pl.BlockSpec(memory_space=pltpu.VMEM)
SMEM = pl.BlockSpec(memory_space=pltpu.SMEM)
HBM = pl.BlockSpec(memory_space=pltpu.HBM)


def cheby_coefficients(count_sweeps):
    center_eig = 0.5 * (EIG_HIGH + EIG_LOW)
    half_width = 0.5 * (EIG_HIGH - EIG_LOW)
    ratio_eig = center_eig / half_width
    damping = 1.0 / ratio_eig
    coefficients = [(0.0, 1.0 / center_eig)]
    for sweep_no in range(1, count_sweeps):
        damping_new = 1.0 / (2.0 * ratio_eig - damping)
        coefficients.append((damping_new * damping, 2.0 * damping_new / half_width))
        damping = damping_new
    return coefficients


def ring(value, axis, step):
    count = lax.axis_size(axis)
    return lax.ppermute(value, axis, [(i, (i + step) % count) for i in range(count)])


def chain(value, axis, step):
    count = lax.axis_size(axis)
    pairs = [(i, i + step) for i in range(count) if 0 <= i + step < count]
    return lax.ppermute(value, axis, pairs)


def sides(axis):
    place = lax.axis_index(axis)
    return place > 0, place < lax.axis_size(axis) - 1


def lasts(micros):
    return pl.CostEstimate(flops=0, bytes_accessed=int(micros * 3.69e6), transcendentals=0)


def quick_reciprocal(value):
    guess = pl.reciprocal(value, approx=True)
    return guess * (2.0 - value * guess)


def lane_index(shape):
    return lax.broadcasted_iota(jnp.int32, shape, 1)


def row_index(shape):
    return lax.broadcasted_iota(jnp.int32, shape, 0)


def first_lane(value, at_first):
    head = value[:, :LANES]
    head = jnp.where(lane_index(head.shape) == 0, at_first, head)
    if value.shape[1] == LANES:
        return head
    return jnp.concatenate([head, value[:, LANES:]], axis=1)


def last_lane(value, at_last):
    tail = value[:, -LANES:]
    tail = jnp.where(lane_index(tail.shape) == LANES - 1, at_last, tail)
    if value.shape[1] == LANES:
        return tail
    return jnp.concatenate([value[:, :-LANES], tail], axis=1)


def from_above(value, row):
    return jnp.where(row_index(value.shape) == 0, row, pltpu.roll(value, 1, 0))


def from_below(value, row):
    count = value.shape[0]
    return jnp.where(row_index(value.shape) == count - 1, row, pltpu.roll(value, count - 1, 0))


class Copies:
    def __init__(self, sems):
        self.sems, self.count, self.waits = sems, 0, {}

    def start(self, key, src, dst):
        made = pltpu.make_async_copy(src, dst, self.sems.at[self.count])
        self.count += 1
        made.start()
        self.waits.setdefault(key, []).append(made)

    def wait(self, key):
        for made in self.waits.pop(key, []):
            made.wait()

    def wait_all(self):
        for key in list(self.waits):
            self.wait(key)


def x_fields(temp, velo, diff, side, cells_x, zs):
    two, one = (pl.ds(0, 2), pl.ds(0, 1)) if side == 0 else (pl.ds(cells_x - 2, 2), pl.ds(cells_x - 1, 1))
    return (
        (temp.at[two, :, zs], 0, 2),
        (diff.at[two, :, zs], 2, 2),
        (velo.at[0, two, :, zs], 4, 2),
        (velo.at[1, one, :, zs], 6, 1),
        (velo.at[2, one, :, zs], 7, 1),
    )


def near_kernel(cells_x, cells_y, depth, flags, wall, temp, velo, diff, xlow, xhigh, ylow, yhigh, wall_t, tiles, sems):
    copies = Copies(sems)
    count = depth // LANES
    sources = (temp, diff, velo.at[1], velo.at[0], velo.at[2])
    for side in range(2):
        rows = pl.ds(0 if side == 0 else cells_y - TILE, TILE)
        for number, src in enumerate(sources):
            copies.start((side, number), src.at[:, rows, :], tiles.at[side, number])
    for side, out in ((0, xlow), (1, xhigh)):
        for tile in range(count):
            for src, at, planes in x_fields(temp, velo, diff, side, cells_x, pl.ds(tile * LANES, LANES)):
                copies.start("x", src, out.at[pl.ds(8 * tile + at, planes)])
    same = ones_where(row_index((cells_x, LANES)) == lane_index((cells_x, LANES)))
    turned = lax.dot_general(wall[...], same, (((0,), (0,)), ((), ())), precision=HIGHEST)
    same = ones_where(row_index((cells_y, LANES)) == lane_index((cells_y, LANES)))
    plain = jnp.dot(wall[...], same, precision=HIGHEST)
    wall_t[...] = turned

    def note(plane, place, at):
        lane = lane_index(plane.shape)
        live_two = jnp.where(place < flags[4], 2.0, 0.0)
        return jnp.where(lane == 0, live_two, jnp.where(lane == 1, pltpu.roll(plane, (LANES + 1 - at) % LANES, 1), 0.0))

    for side in range(2):
        x, y = side * (cells_x - 1), side * (cells_y - 1)
        (xlow, xhigh)[side][8 * count] = note(turned, x * cells_y + row_index(turned.shape), x)
        (ylow, yhigh)[side][8 * count] = note(plain, row_index(plain.shape) * cells_y + y, y)
    for side, out in ((0, ylow), (1, yhigh)):
        first, near = (0, 0) if side == 0 else (TILE - 2, TILE - 1)
        for number in range(5):
            copies.wait((side, number))
            picks = [(2 * number, first), (2 * number + 1, first + 1)] if number < 3 else [(3 + number, near)]
            for plane, row in picks:
                for x in range(cells_x):
                    line = tiles[side, number, x, pl.ds(row, 1), :]
                    for tile in range(count):
                        out[8 * tile + plane, pl.ds(x, 1), :] = line[:, tile * LANES:(tile + 1) * LANES]
    copies.wait_all()


def near_step(flags, wall, temp, velo, diff):
    cells_x, cells_y, depth = temp.shape
    planes = 8 * (depth // LANES) + 1
    x_strip = jax.ShapeDtypeStruct((planes, cells_y, LANES), temp.dtype)
    y_strip = jax.ShapeDtypeStruct((planes, cells_x, LANES), temp.dtype)
    return pl.pallas_call(
        functools.partial(near_kernel, cells_x, cells_y, depth),
        out_shape=(x_strip, x_strip, y_strip, y_strip, jax.ShapeDtypeStruct((cells_y, LANES), temp.dtype)),
        in_specs=[SMEM, VMEM, HBM, HBM, HBM],
        out_specs=(VMEM,) * 5,
        scratch_shapes=[
            pltpu.VMEM((2, 5, cells_x, TILE, depth), jnp.float32),
            pltpu.SemaphoreType.DMA((10 + 10 * (depth // LANES),)),
        ],
        compiler_params=pltpu.CompilerParams(vmem_limit_bytes=VMEM_ALL),
        cost_estimate=lasts(4),
    )(flags, wall, temp, velo, diff)


def corner_kernel(cells_x, count, ylo, yhi, low, high):
    for out, x in ((low, 0), (high, cells_x - 1)):
        for half, (strip, inner) in enumerate(((ylo, 1), (yhi, 0))):
            for j, plane in enumerate((inner, 2 + inner, 6, 4 + inner)):
                for tile in range(count):
                    out[pl.ds(4 * half + j, 1), pl.ds(tile * LANES, LANES)] = strip[8 * tile + plane, pl.ds(x, 1), :]


def solid_pack_kernel(cells_x, cells_y, pad, depth, *refs):
    xlow, xhigh, ylow, yhigh, sems = refs[4:]
    copies = Copies(sems)
    for field, src in enumerate(refs[:4]):
        for tile in range(depth // LANES):
            number, zs = field * (depth // LANES) + tile, pl.ds(tile * LANES, LANES)
            for side, out in ((0, xlow), (1, xhigh)):
                here = pl.ds(side * (cells_x - pad), pad)
                copies.start(0, src.at[here, :, zs], out.at[pl.ds(number * pad, pad)])
            for side, out in ((0, ylow), (1, yhigh)):
                here = pl.ds(side * (cells_y - TILE), TILE)
                copies.start(0, src.at[:, here, zs], out.at[pl.ds(number * cells_x, cells_x)])
    copies.wait_all()


def solid_corner_kernel(cells_x, pad, numbers, ylo, yhi, low, high, sems):
    copies = Copies(sems)
    for out, x in ((low, 0), (high, cells_x - pad)):
        for half, strip in enumerate((ylo, yhi)):
            for number in range(numbers):
                copies.start(0, strip.at[pl.ds(number * cells_x + x, pad)],
                             out.at[pl.ds((half * numbers + number) * pad, pad)])
    copies.wait_all()


def packing(kernel, shapes, copies, micros, *args):
    return pl.pallas_call(
        kernel,
        out_shape=tuple(jax.ShapeDtypeStruct(shape, jnp.float32) for shape in shapes),
        in_specs=[HBM if copies else VMEM] * len(args),
        out_specs=(VMEM,) * len(shapes),
        scratch_shapes=[pltpu.SemaphoreType.DMA((copies,))] if copies else [],
        compiler_params=pltpu.CompilerParams(vmem_limit_bytes=VMEM_ALL if copies else VMEM_ALL // 2),
        cost_estimate=lasts(micros),
    )(*args)


def exchange(low, high, axis, move):
    return move(high, axis, 1), move(low, axis, -1)


def solid_strips(solids, pad):
    cells_x, cells_y, depth = solids[0].shape
    numbers = 4 * (depth // LANES)
    x_shape, y_shape = (numbers * pad, cells_y, LANES), (numbers * cells_x, TILE, LANES)
    return packing(functools.partial(solid_pack_kernel, cells_x, cells_y, pad, depth),
                   (x_shape, x_shape, y_shape, y_shape), 4 * numbers, 3, *solids)


def solid_corners(ylo, yhi, cells_x, numbers, pad):
    shape = (2 * numbers * pad, TILE, LANES)
    return packing(functools.partial(solid_corner_kernel, cells_x, pad, numbers), (shape, shape), 4 * numbers, 1,
                   ylo, yhi)


def face(a_low, a_high, u_low, u_high):
    a_two = a_low + a_high
    u_two = u_low + u_high
    plus = a_two + jnp.maximum(u_two, 0.0)
    return plus, plus - u_two


def relaxation(a, ut, uz, low, high, above, below, live_two, wall):
    depth = a.shape[1]
    p_above, q_above = face(from_above(a, above[0]), a, from_above(ut, above[1]), ut)
    p_below, q_below = face(a, from_below(a, below[0]), ut, from_below(ut, below[1]))
    p_down, q_down = face(pltpu.roll(a, 1, 1), a, pltpu.roll(uz, 1, 1), uz)
    p_up, q_up = pltpu.roll(p_down, depth - 1, 1), pltpu.roll(q_down, depth - 1, 1)
    a_first = 2.0 * a[:, :LANES]
    u_last = 2.0 * uz[:, -LANES:]
    plus_last = 2.0 * a[:, -LANES:] + jnp.maximum(u_last, 0.0)
    weight = (low[0] + low[1]) + (high[0] + high[1]) + (p_above + q_above) + (p_below + q_below)
    weight = weight + first_lane(p_down + q_down, 2.0 * a_first) + last_lane(p_up + q_up, 2.0 * plus_last - u_last)
    factor = (2.0 * RELAX_FACTOR) * quick_reciprocal(weight)
    gain = a_first * live_two
    p_down, q_down = first_lane(p_down, 0.0), first_lane(q_down, gain)
    p_up, q_up = last_lane(p_up, plus_last), last_lane(q_up, 0.0)
    leaving = (low[1] + high[0]) + (q_above + p_below) + (q_down + p_up)
    ghost = jnp.where(lane_index(gain.shape) == 0, gain * wall * factor[:, :LANES], 0.0)
    return (low[0] * factor, high[1] * factor, p_above * factor, q_below * factor, p_down * factor, q_up * factor,
            1.0 - leaving * factor, ghost)


def apply(factors, t, t_low, t_high, t_above, t_below):
    depth = t.shape[1]
    new = factors[6] * t + (factors[0] * t_low + factors[1] * t_high)
    new = new + (factors[2] * from_above(t, t_above) + factors[3] * from_below(t, t_below))
    new = new + (factors[4] * pltpu.roll(t, 1, 1) + factors[5] * pltpu.roll(t, depth - 1, 1))
    head = new[:, :LANES] + factors[7]
    return head if depth == LANES else jnp.concatenate([head, new[:, LANES:]], axis=1)


def fluid_kernel(cells_x, cells_y, depth, flags, wall_t, xlo, xhi, ylo, yhi, clo, chi, temp, velo, diff,
                 out, gas, ts, us, as_, vs, ws, t1, yl, cs, ks, sems):
    rows_total = flags[4]
    mid = pl.ds(TILE, cells_y)
    tiles = [(tile, pl.ds(tile * LANES, LANES)) for tile in range(depth // LANES)]
    copies = Copies(sems)
    step = TILE
    starts = list(range(0, cells_x, step))

    def load(start):
        here = pl.ds(start, step)
        copies.start(start, temp.at[here], ts.at[pl.ds(start + 2, step), mid])
        copies.start(start, diff.at[here], as_.at[pl.ds(start + 2, step), mid])
        copies.start(start, velo.at[0, here], us.at[pl.ds(start + 2, step)])
        copies.start(start, velo.at[1, here], vs.at[pl.ds(start + 1, step), mid])
        copies.start(start, velo.at[2, here], ws.at[pl.ds(start + 1, step)])

    for start in starts[:2]:
        load(start)
    for side, halo in enumerate((xlo, xhi)):
        at, beside = (0, 0) if side == 0 else (cells_x + 2, cells_x + 1)
        for tile, zs in tiles:
            for j in range(2):
                ts[at + j, mid, zs] = halo[8 * tile + j]
                as_[at + j, mid, zs] = halo[8 * tile + 2 + j]
                us[at + j, :, zs] = halo[8 * tile + 4 + j]
            vs[beside, mid, zs] = halo[8 * tile + 6]
            ws[beside, :, zs] = halo[8 * tile + 7]

        @pl.when(flags[side] == 0)
        def _():
            for ref, first, count in ((ts, at, 2), (as_, at, 2), (us, at, 2), (vs, beside, 1), (ws, beside, 1)):
                for j in range(count):
                    ref[first + j] = jnp.zeros(ref.shape[1:], jnp.float32)

    for side, (halo, row) in enumerate(((ylo, TILE - 1), (yhi, TILE + cells_y))):
        inner = 1 - side
        for plane in range(8):
            for tile, zs in tiles:
                yl[side, plane, pl.ds(TILE, cells_x), zs] = halo[8 * tile + plane]
        for end, (corner, at) in enumerate(((clo, TILE - 1), (chi, TILE + cells_x))):
            for j, plane in enumerate((inner, 2 + inner, 6, 4 + inner)):
                yl[side, plane, pl.ds(at, 1), :] = jnp.where(flags[end] > 0, corner[pl.ds(4 * side + j, 1), :], 0.0)
        for j in range(cells_x + 2):
            at = pl.ds(TILE - 1 + j, 1)
            ts[j + 1, pl.ds(row, 1), :] = yl[side, inner, at, :]
            as_[j + 1, pl.ds(row, 1), :] = yl[side, 2 + inner, at, :]
            vs[j, pl.ds(row, 1), :] = yl[side, 4 + inner, at, :]

    def plane_factors(i, live_two, wall):
        a, un = as_[i + 1, mid, :], us[i + 1]
        low = face(as_[i, mid, :], a, us[i], un)
        high = face(a, as_[i + 2, mid, :], un, us[i + 2])
        up, down = pl.ds(TILE - 1, 1), pl.ds(TILE + cells_y, 1)
        return relaxation(a, vs[i, mid, :], ws[i], low, high, (as_[i + 1, up, :], vs[i, up, :]),
                          (as_[i + 1, down, :], vs[i, down, :]), live_two, wall)

    def plane_apply(factors, ref, i):
        up, down = pl.ds(TILE - 1, 1), pl.ds(TILE + cells_y, 1)
        return apply(factors, ref[i, mid, :], ref[i - 1, mid, :], ref[i + 1, mid, :], ref[i, up, :], ref[i, down, :])

    def note_of(note):
        return note, pltpu.roll(note, LANES - 1, 1)

    def first_sweep(i, carry):
        place = (i - 1) * cells_y + row_index((cells_y, LANES))
        live_two = jnp.where(place < rows_total, 2.0, 0.0)
        factors = plane_factors(i, live_two, pltpu.roll(wall_t[...], LANES + 1 - i, 1))
        for j in range(7):
            cs[j, i - 1] = factors[j]
        ks[i - 1] = factors[7]
        t1[i, mid, :] = plane_apply(factors, ts, i + 1)
        return carry

    def halo_plane(i, side):
        factors = plane_factors(i, *note_of((xlo, xhi)[side][8 * len(tiles)]))
        t1[i, mid, :] = jnp.where(flags[side] > 0, plane_apply(factors, ts, i + 1), 0.0)

    for number, start in enumerate(starts):
        copies.wait(start)
        if number + 2 < len(starts):
            load(starts[number + 2])
        if start == 0:
            halo_plane(0, 0)
        last = cells_x + 1 if start == starts[-1] else start + step
        lax.fori_loop(max(start, 1), last, first_sweep, 0, unroll=2)
    halo_plane(cells_x + 1, 1)

    for side, row in ((0, TILE - 1), (1, TILE + cells_y)):
        inner = 1 - side
        own = TILE if side == 0 else TILE + cells_y - 1
        rows, up, down = pl.ds(TILE, cells_x), pl.ds(TILE - 1, 1), pl.ds(TILE + cells_x, 1)

        def own_rows(ref, off):
            return jnp.concatenate([ref[off + x, pl.ds(own, 1), :] for x in range(cells_x)], axis=0)

        t, a, un = yl[side, inner, rows, :], yl[side, 2 + inner, rows, :], yl[side, 4 + inner, rows, :]
        t_far, a_far, un_far = (yl[side, 1 - inner, rows, :], yl[side, 3 - inner, rows, :],
                                yl[side, 5 - inner, rows, :])
        t_own, a_own, un_own = own_rows(ts, 2), own_rows(as_, 2), own_rows(vs, 1)
        if side == 0:
            low, high = face(a_far, a, un_far, un), face(a, a_own, un, un_own)
            t_low, t_high = t_far, t_own
        else:
            low, high = face(a_own, a, un_own, un), face(a, a_far, un, un_far)
            t_low, t_high = t_own, t_far
        factors = relaxation(
            a, yl[side, 6, rows, :], yl[side, 7, rows, :], low, high,
            (yl[side, 2 + inner, up, :], yl[side, 6, up, :]), (yl[side, 2 + inner, down, :], yl[side, 6, down, :]),
            *note_of((ylo, yhi)[side][8 * len(tiles)]))
        new = apply(factors, t, t_low, t_high, yl[side, inner, up, :], yl[side, inner, down, :])
        new = jnp.where(flags[2 + side] > 0, new, 0.0)
        for x in range(cells_x):
            t1[1 + x, pl.ds(row, 1), :] = new[x:x + 1, :]

    def second_sweep(i, carry):
        factors = [cs[j, i - 1] for j in range(7)] + [ks[i - 1]]
        new = plane_apply(factors, t1, i)
        ts[i - 1, mid, :] = new
        shift = i - 1
        return jnp.where(lane_index((cells_y, LANES)) == shift, pltpu.roll(new[:, :LANES], shift, 1), carry)

    plane = jnp.zeros((cells_y, LANES), jnp.float32)
    for start in starts:
        plane = lax.fori_loop(start + 1, start + step + 1, second_sweep, plane, unroll=4)
        copies.start("out", ts.at[pl.ds(start, step), mid], out.at[pl.ds(start, step)])
    gas[...] = plane
    copies.wait("out")


def film_coefficients_kernel(cells_x, cells_y, flags, diff, out, tile, sem):
    copy = pltpu.make_async_copy(diff.at[:, :, pl.ds(0, LANES)], tile, sem)
    copy.start()
    copy.wait()
    shape = (cells_y, LANES)
    total = jnp.zeros(shape, jnp.float32)
    for x in range(cells_x):
        total = jnp.where(lane_index(shape) == x, pltpu.roll(tile[x], x, 1), total)
    place = lane_index(shape) * cells_y + row_index(shape)
    out[...] = jnp.where(place < flags[4], 2.0 * total, 0.0)


def film_coefficients(flags, diff):
    cells_x, cells_y, _ = diff.shape
    return pl.pallas_call(
        functools.partial(film_coefficients_kernel, cells_x, cells_y),
        out_shape=(jax.ShapeDtypeStruct((cells_y, LANES), diff.dtype),),
        in_specs=[SMEM, HBM],
        out_specs=(VMEM,),
        scratch_shapes=[pltpu.VMEM((cells_x, cells_y, LANES), jnp.float32), pltpu.SemaphoreType.DMA],
        compiler_params=pltpu.CompilerParams(vmem_limit_bytes=VMEM_ALL),
        cost_estimate=lasts(1),
    )(flags, diff)


def fluid_call(flags, wall_t, strips, temp, velo, diff):
    cells_x, cells_y, depth = temp.shape
    wide = cells_y + 2 * TILE
    chunks = cells_x // TILE
    plane = jax.ShapeDtypeStruct((cells_y, LANES), temp.dtype)
    return pl.pallas_call(
        functools.partial(fluid_kernel, cells_x, cells_y, depth),
        out_shape=(jax.ShapeDtypeStruct(temp.shape, temp.dtype), plane),
        in_specs=[SMEM] + [VMEM] * 7 + [HBM] * 3,
        out_specs=(HBM, VMEM),
        scratch_shapes=[
            pltpu.VMEM((cells_x + 4, wide, depth), jnp.float32),
            pltpu.VMEM((cells_x + 4, cells_y, depth), jnp.float32),
            pltpu.VMEM((cells_x + 4, wide, depth), jnp.float32),
            pltpu.VMEM((cells_x + 2, wide, depth), jnp.float32),
            pltpu.VMEM((cells_x + 2, cells_y, depth), jnp.float32),
            pltpu.VMEM((cells_x + 2, wide, depth), jnp.float32),
            pltpu.VMEM((2, 8, cells_x + 2 * TILE, depth), jnp.float32),
            pltpu.VMEM((7, cells_x, cells_y, depth), jnp.float32),
            pltpu.VMEM((cells_x, cells_y, LANES), jnp.float32),
            pltpu.SemaphoreType.DMA((6 * chunks,)),
        ],
        compiler_params=pltpu.CompilerParams(vmem_limit_bytes=VMEM_ALL),
        cost_estimate=lasts(13),
    )(flags, wall_t, *strips, temp, velo, diff)


def solid_kernel(
    cells_x, cells_y, depth, pad, coefficients,
    flags, cond, sink, heat, temp, xlo, xhi, ylo, yhi, clo, chi, film, film_lo, film_hi,
    out, surface, ks, es, bs, us, vs, gx, gy, gz, ss, ps, fs, sems,
):
    wide_x, wide_y = cells_x + 2 * pad, cells_y + 2 * TILE
    copies = Copies(sems)
    own_x, own_y = pl.ds(pad, cells_x), pl.ds(TILE, cells_y)
    for field, (src, dst) in enumerate(((cond, ks), (sink, es), (heat, bs), (temp, us))):
        copies.start(field // 2, src, dst.at[own_x, own_y])
        for tile in range(depth // LANES):
            zs, number = pl.ds(tile * LANES, LANES), field * (depth // LANES) + tile
            key, numbers = field // 2, 4 * (depth // LANES)
            x_from, y_from = pl.ds(number * pad, pad), pl.ds(number * cells_x, cells_x)
            x_low, x_high = pl.ds(0, pad), pl.ds(pad + cells_x, pad)
            y_low, y_high = pl.ds(0, TILE), pl.ds(TILE + cells_y, TILE)
            copies.start(key, xlo.at[x_from], dst.at[x_low, own_y, zs])
            copies.start(key, xhi.at[x_from], dst.at[x_high, own_y, zs])
            copies.start(key, ylo.at[y_from], dst.at[own_x, y_low, zs])
            copies.start(key, yhi.at[y_from], dst.at[own_x, y_high, zs])
            for half, y_at in enumerate((y_low, y_high)):
                c_from = pl.ds((half * numbers + number) * pad, pad)
                copies.start(key, clo.at[c_from], dst.at[x_low, y_at, zs])
                copies.start(key, chi.at[c_from], dst.at[x_high, y_at, zs])
    fs[:, pl.ds(0, TILE), :] = jnp.where(flags[2] > 0, film_lo[...], 0.0)
    fs[:, own_y, :] = film[...]
    fs[:, pl.ds(TILE + cells_y, TILE), :] = jnp.where(flags[3] > 0, film_hi[...], 0.0)

    def harmonic(k, near):
        total = jnp.maximum(k + near, 1e-30)
        return (2.0 * k * near) * quick_reciprocal(total)

    def film_of(kind, x):
        return pltpu.roll(fs[kind], 2 * LANES + pad - x, 1)

    def add_first(value, extra):
        head = value[:, :LANES]
        head = head + jnp.where(lane_index(head.shape) == 0, extra, 0.0)
        return jnp.concatenate([head, value[:, LANES:]], axis=1) if depth > LANES else head

    gx[0, :, :] = jnp.zeros((wide_y, depth), jnp.float32)
    edge = row_index((wide_y, depth)) == wide_y - 1
    top = lane_index((wide_y, depth)) == depth - 1

    def conductances(x, carry):
        keep = jnp.where(x < wide_x - 1, 1.0, 0.0)
        follow = jnp.minimum(x + 1, wide_x - 1)
        k = ks[x]
        face_x = harmonic(k, ks[follow]) * keep
        face_y = jnp.where(edge, 0.0, harmonic(k, pltpu.roll(k, wide_y - 1, 0)))
        face_z = jnp.where(top, 0.0, harmonic(k, pltpu.roll(k, depth - 1, 1)))
        diag = add_first(es[x], film_of(0, x))
        diag = diag + (gx[x] + face_x) + (face_y + pltpu.roll(face_y, 1, 0))
        diag = diag + (face_z + pltpu.roll(face_z, 1, 1))
        gx[x + 1] = face_x
        gy[x] = face_y
        gz[x] = face_z
        es[x] = diag
        ss[x] = lax.rsqrt(jnp.maximum(diag, 1e-30))
        return carry

    copies.wait(0)
    for side in range(2):
        @pl.when(flags[side] == 0)
        def _():
            for j in range(pad):
                ks[side * (pad + cells_x) + j] = jnp.zeros((wide_y, depth), jnp.float32)

    lax.fori_loop(0, wide_x, conductances, 0, unroll=4)

    def scale(x, carry):
        follow = jnp.minimum(x + 1, wide_x - 1)
        s = ss[x]
        gx[x + 1] = gx[x + 1] * s * ss[follow]
        gy[x] = gy[x] * s * pltpu.roll(s, wide_y - 1, 0)
        gz[x] = gz[x] * s * pltpu.roll(s, depth - 1, 1)
        bs[x] = add_first(bs[x], film_of(1, x)) * s
        us[x] = us[x] * es[x] * s
        return carry

    copies.wait(1)
    lax.fori_loop(0, wide_x, scale, 0, unroll=4)

    total = len(coefficients)
    src, dst = us, vs
    for number, (decay, gain) in enumerate(coefficients):
        last = number == total - 1
        margin = total - 1 - number

        def some(block, carry, src=src, dst=dst, decay=decay, gain=gain, number=number, last=last, margin=margin):
            planes = [pad - margin + block * BATCH + j for j in range(BATCH)]
            here = [src[x] for x in planes]
            before = [src[planes[0] - 1]] + here[:-1]
            after = here[1:] + [src[planes[-1] + 1]]
            g_x = [gx[planes[0]]] + [gx[x + 1] for x in planes]
            results = []
            for j, x in enumerate(planes):
                g_y, g_z, value = gy[x], gz[x], here[j]
                total_in = g_x[j] * before[j] + g_x[j + 1] * after[j]
                total_in += g_y * pltpu.roll(value, wide_y - 1, 0) + pltpu.roll(g_y * value, 1, 0)
                total_in += g_z * pltpu.roll(value, depth - 1, 1) + pltpu.roll(g_z * value, 1, 1)
                step = gain * ((bs[x] - value) + total_in)
                if number > 0:
                    step = step + decay * ps[x]
                results.append((step, value + step))
            for j, x in enumerate(planes):
                step, fresh = results[j]
                if last:
                    final = (fresh * ss[x])[TILE:TILE + cells_y]
                    out[x - pad] = final
                    shift = x - pad
                    lane = lane_index((cells_y, LANES))
                    surface[...] = jnp.where(lane == shift, pltpu.roll(final[:, :LANES], shift, 1), surface[...])
                else:
                    ps[x] = step
                    dst[x] = fresh
            return carry

        if last:
            surface[...] = jnp.zeros_like(surface)
        lax.fori_loop(0, -(-(cells_x + 2 * margin) // BATCH), some, 0)
        src, dst = dst, src


def solid_step(flags, cond, sink, heat, temp, halo, films, pad):
    cells_x, cells_y, depth = cond.shape
    wide_x, wide_y = cells_x + 2 * pad, cells_y + 2 * TILE
    area = pltpu.VMEM((wide_x + BATCH, wide_y, depth), jnp.float32)
    return pl.pallas_call(
        functools.partial(solid_kernel, cells_x, cells_y, depth, pad, cheby_coefficients(SWEEPS)),
        out_shape=(jax.ShapeDtypeStruct((cells_x, cells_y, depth), cond.dtype),
                   jax.ShapeDtypeStruct((cells_y, LANES), cond.dtype)),
        in_specs=[SMEM] + [HBM] * 10 + [VMEM] * 3,
        out_specs=(VMEM, VMEM),
        scratch_shapes=[area] * 5
        + [area]
        + [area] * 4
        + [pltpu.VMEM((2, wide_y, LANES), jnp.float32), pltpu.SemaphoreType.DMA((4 + 32 * (depth // LANES),))],
        compiler_params=pltpu.CompilerParams(vmem_limit_bytes=VMEM_ALL),
        cost_estimate=lasts(30),
    )(flags, cond, sink, heat, temp, *halo, *films)


def ones_where(condition):
    return jnp.where(condition, 1.0, 0.0)


def route_kernel(group_total, slot_cap, owner, out):
    dirs = owner[...]
    row_total = group_total * slot_cap
    codes = row_index((TILE, group_total))
    matched = ones_where((codes >= 1) & (codes <= 4) & (dirs == codes))
    before = ones_where(row_index((group_total, group_total)) < lane_index((group_total, group_total)))
    rank = jnp.dot(matched, before, precision=HIGHEST)
    start = jnp.where(matched > 0.5, rank * slot_cap, -1.0 * row_total)
    start = jnp.where(codes == 0, ones_where(dirs == 0), start)
    spread = ones_where(row_index((group_total, row_total)) == lane_index((group_total, row_total)) // slot_cap)
    wide = jnp.dot(start, spread, precision=HIGHEST)
    within = (lane_index((TILE, row_total)) % slot_cap).astype(jnp.float32)
    out[...] = jnp.where(row_index((TILE, row_total)) == 0, wide, wide + within)


def cell_values(plane_t, cells_x, cells_y, cells):
    count = cells.shape[1]
    in_x = ones_where(row_index((cells_x, count)) == cells // cells_y)
    in_y = ones_where(row_index((cells_y, count)) == cells % cells_y)
    lines = jnp.dot(plane_t[:, :cells_x], in_x, precision=HIGHEST)
    return jnp.sum(lines * in_y, axis=0, keepdims=True)


def rows_kernel(cells_x, cells_y, near_rows, route, gas_t, film_t, pair, *outs):
    row_total = cells_x * cells_y
    cells = lane_index((1, row_total))
    film = cell_values(film_t[...], cells_x, cells_y, cells)
    gas = cell_values(gas_t[...], cells_x, cells_y, cells)
    values = jnp.concatenate([film, gas], axis=0)
    pair[...] = values
    for d in range(4):
        slots = route[d + 1:d + 2, :].astype(jnp.int32)
        pick = ones_where(row_index((near_rows, row_total)) == slots)
        outs[d][...] = lax.dot_general(values, pick, (((1,), (1,)), ((), ())), precision=HIGHEST)


def film_kernel(cells_x, cells_y, pad, flags, route, landing, pair, from_0, from_1, from_2, from_3, plane, low, high):
    cells = landing[...]
    slots = cells.shape[1]
    arrived = [jnp.where(flags[d] > 0, piece[...], 0.0) for d, piece in enumerate((from_0, from_1, from_2, from_3))]
    own = pair[...]
    film = jnp.concatenate([own[:1] * route[0:1, :]] + [piece[:1] for piece in arrived], axis=1)
    gas = jnp.concatenate([own[1:]] + [piece[1:] for piece in arrived], axis=1)
    in_x = ones_where(row_index((LANES, slots)) == cells // cells_y)
    in_y = ones_where(row_index((cells_y, slots)) == cells % cells_y)
    weighted = jnp.concatenate([in_y * film, in_y * (film * gas)], axis=0)
    total = lax.dot_general(weighted, in_x, (((1,), (1,)), ((), ())), precision=HIGHEST)
    lane = lane_index(total.shape)
    to_high = jnp.where(lane >= LANES - pad, pltpu.roll(total, LANES - cells_x, 1), 0.0)
    to_low = jnp.where((lane >= cells_x) & (lane < cells_x + pad), pltpu.roll(total, cells_x, 1), 0.0)
    for ref, value in ((plane, total), (low, to_low), (high, to_high)):
        ref[0] = value[:cells_y]
        ref[1] = value[cells_y:]


def widen_kernel(cells_y, flags, plane, low, high, out, first, last):
    total = plane[...] + jnp.where(flags[0] > 0, low[...], 0.0) + jnp.where(flags[1] > 0, high[...], 0.0)
    out[...] = total
    first[...] = total[:, :TILE]
    last[...] = total[:, cells_y - TILE:]


def gather_kernel(cells_x, cells_y, row_total, near_rows, landing, surface_t, own, *outs):
    values = cell_values(surface_t[...], cells_x, cells_y, landing[...])
    own[...] = values[:, :row_total]
    for d in range(4):
        outs[d][...] = values[:, row_total + d * near_rows:row_total + (d + 1) * near_rows]


def wall_kernel(near_rows, flags, route, own, from_0, from_1, from_2, from_3, out):
    row_total = own.shape[1]
    total = own[...] * route[0:1, :]
    for d, (piece, side) in enumerate(((from_0, 1), (from_1, 0), (from_2, 3), (from_3, 2))):
        slots = route[d + 1:d + 2, :].astype(jnp.int32)
        pick = ones_where(row_index((near_rows, row_total)) == slots)
        total = total + jnp.dot(jnp.where(flags[side] > 0, piece[...], 0.0), pick, precision=HIGHEST)
    out[...] = jnp.where(lane_index((1, row_total)) < flags[4], total, 0.0)


def small_call(kernel, shapes, flags, *args):
    lead = [] if flags is None else [flags]
    return pl.pallas_call(
        kernel,
        out_shape=tuple(jax.ShapeDtypeStruct(shape, jnp.float32) for shape in shapes),
        in_specs=[SMEM] * len(lead) + [VMEM] * len(args),
        out_specs=tuple(VMEM for _ in shapes),
        compiler_params=pltpu.CompilerParams(vmem_limit_bytes=32 * 1024 * 1024),
        cost_estimate=lasts(1),
    )(*lead, *args)


def on_device(
    fluid_temp, velocity, eddy_diff, wall_prev, row_count, owner_table, landing_cell,
    solid_temp, conductivity, sink, heat_source,
):
    cells_x, cells_y, cells_z = fluid_temp.shape
    solid_x, solid_y, solid_z = solid_temp.shape
    row_total = cells_x * cells_y
    group_total = owner_table.shape[1]
    slot_cap = row_total // group_total
    near_rows = group_total // 8 * slot_cap
    pad = SWEEPS
    wall_plane = wall_prev.reshape(cells_x, cells_y)
    flags = jnp.concatenate([jnp.stack([*sides("blk"), *sides("sub")]).astype(jnp.int32), row_count])
    fluid = (fluid_temp, velocity, eddy_diff)
    solids = (conductivity, sink, heat_source, solid_temp)

    xlow, xhigh, ylow, yhigh, wall_t = near_step(flags, wall_plane, *fluid)
    xlo, xhi = exchange(xlow, xhigh, "blk", ring)
    ylo, yhi = exchange(ylow, yhigh, "sub", chain)
    after_near = lax.optimization_barrier((xlow, *solids, eddy_diff, owner_table))[1:]
    strips = solid_strips(after_near[:4], pad)
    (film_t,) = film_coefficients(flags, after_near[4])
    (route,) = small_call(
        functools.partial(route_kernel, group_total, slot_cap), [(TILE, row_total)], None, after_near[5]
    )
    xlo, xhi, ylo, yhi, film_t, route, *strips = lax.optimization_barrier((xlo, xhi, ylo, yhi, film_t, route, *strips))
    corner = (TILE, cells_z)
    low, high = packing(functools.partial(corner_kernel, cells_x, cells_z // LANES), (corner, corner), 0, 1, ylo, yhi)
    clo, chi = exchange(low, high, "blk", ring)
    clo, chi, *strips = lax.optimization_barrier((clo, chi, *strips))
    xlow, xhigh, ylow, yhigh = strips
    halo = [*exchange(xlow, xhigh, "blk", ring), *exchange(ylow, yhigh, "sub", chain)]
    fluid_new, gas_t = fluid_call(flags, wall_t, (xlo, xhi, ylo, yhi, clo, chi), *fluid)
    gas_t, *halo = lax.optimization_barrier((gas_t, *halo))
    low, high = solid_corners(halo[2], halo[3], solid_x, 4 * (solid_z // LANES), pad)

    pair, *bands = small_call(
        functools.partial(rows_kernel, cells_x, cells_y, near_rows),
        [(2, row_total)] + [(2, near_rows)] * 4, None, route, gas_t, film_t,
    )
    moves = (("blk", 1), ("blk", -1), ("sub", 1), ("sub", -1))
    arrived = [ring(band, axis, step) for band, (axis, step) in zip(bands, moves)]
    *arrived, low, high = lax.optimization_barrier((*arrived, low, high))
    halo += exchange(low, high, "blk", ring)
    plane = (2, solid_y, LANES)
    film, low, high = small_call(
        functools.partial(film_kernel, solid_x, solid_y, pad), [plane] * 3, flags, route, landing_cell, pair, *arrived
    )
    film, first, last = small_call(
        functools.partial(widen_kernel, solid_y), [plane] + [(2, TILE, LANES)] * 2,
        flags, film, ring(high, "blk", 1), ring(low, "blk", -1),
    )
    films = (film, ring(last, "sub", 1), ring(first, "sub", -1))
    solid_new, surface_t = solid_step(flags, *solids, halo, films, pad)

    own, *backs = small_call(
        functools.partial(gather_kernel, solid_x, solid_y, row_total, near_rows),
        [(1, row_total)] + [(1, near_rows)] * 4, None, landing_cell, surface_t,
    )
    returned = [ring(back, axis, -step) for back, (axis, step) in zip(backs, moves)]
    (wall_new,) = small_call(
        functools.partial(wall_kernel, near_rows), [(1, row_total)], flags, route, own, *returned
    )
    return fluid_new, solid_new, wall_new.reshape(row_total)


def solution(mesh):
    return jax.shard_map(
        on_device,
        mesh=mesh,
        in_specs=(
            P("blk", "sub", None),
            P(None, "blk", "sub", None),
            P("blk", "sub", None),
            P(("blk", "sub")),
            P(("blk", "sub")),
            P(("blk", "sub"), None),
            P(("blk", "sub"), None),
            P("blk", "sub", None),
            P("blk", "sub", None),
            P("blk", "sub", None),
            P("blk", "sub", None),
        ),
        out_specs=(P("blk", "sub", None), P("blk", "sub", None), P(("blk", "sub"))),
        check_vma=False,
    )
```

```python
import functools

import jax
import jax.numpy as jnp
from jax import lax
from jax.experimental import pallas as pl
from jax.experimental.pallas import tpu as pltpu
from jax.sharding import PartitionSpec as P

FLUID_SWEEPS = 2
SWEEPS = 8
RELAX_FACTOR = 0.8
EIG_LOW = 0.02
EIG_HIGH = 2.0
TILE = 8
LANES = 128
VMEM_ALL = 60 * 1024 * 1024
BATCH = 8
HIGHEST = lax.Precision.HIGHEST
VMEM = pl.BlockSpec(memory_space=pltpu.VMEM)
SMEM = pl.BlockSpec(memory_space=pltpu.SMEM)
HBM = pl.BlockSpec(memory_space=pltpu.HBM)


def cheby_coefficients(count_sweeps):
    center_eig = 0.5 * (EIG_HIGH + EIG_LOW)
    half_width = 0.5 * (EIG_HIGH - EIG_LOW)
    ratio_eig = center_eig / half_width
    damping = 1.0 / ratio_eig
    coefficients = [(0.0, 1.0 / center_eig)]
    for sweep_no in range(1, count_sweeps):
        damping_new = 1.0 / (2.0 * ratio_eig - damping)
        coefficients.append((damping_new * damping, 2.0 * damping_new / half_width))
        damping = damping_new
    return coefficients


def ring(value, axis, step):
    count = lax.axis_size(axis)
    return lax.ppermute(value, axis, [(i, (i + step) % count) for i in range(count)])


def chain(value, axis, step):
    count = lax.axis_size(axis)
    pairs = [(i, i + step) for i in range(count) if 0 <= i + step < count]
    return lax.ppermute(value, axis, pairs)


def sides(axis):
    place = lax.axis_index(axis)
    return place > 0, place < lax.axis_size(axis) - 1


def lasts(micros):
    return pl.CostEstimate(flops=0, bytes_accessed=int(micros * 3.69e6), transcendentals=0)


def quick_reciprocal(value):
    guess = pl.reciprocal(value, approx=True)
    return guess * (2.0 - value * guess)


def lane_index(shape):
    return lax.broadcasted_iota(jnp.int32, shape, 1)


def row_index(shape):
    return lax.broadcasted_iota(jnp.int32, shape, 0)


def first_lane(value, at_first):
    head = value[:, :LANES]
    head = jnp.where(lane_index(head.shape) == 0, at_first, head)
    if value.shape[1] == LANES:
        return head
    return jnp.concatenate([head, value[:, LANES:]], axis=1)


def last_lane(value, at_last):
    tail = value[:, -LANES:]
    tail = jnp.where(lane_index(tail.shape) == LANES - 1, at_last, tail)
    if value.shape[1] == LANES:
        return tail
    return jnp.concatenate([value[:, :-LANES], tail], axis=1)


def from_above(value, row):
    moved = pltpu.roll(value, 1, 0)
    head = jnp.where(row_index((TILE, value.shape[1])) == 0, row, moved[:TILE])
    return jnp.concatenate([head, moved[TILE:]], axis=0)


def from_below(value, row):
    moved = pltpu.roll(value, value.shape[0] - 1, 0)
    tail = jnp.where(row_index((TILE, value.shape[1])) == TILE - 1, row, moved[-TILE:])
    return jnp.concatenate([moved[:-TILE], tail], axis=0)


class Copies:
    def __init__(self, sems):
        self.sems, self.count, self.waits = sems, 0, {}

    def start(self, key, src, dst):
        made = pltpu.make_async_copy(src, dst, self.sems.at[self.count])
        self.count += 1
        made.start()
        self.waits.setdefault(key, []).append(made)

    def wait(self, key):
        for made in self.waits.pop(key, []):
            made.wait()

    def wait_all(self):
        for key in list(self.waits):
            self.wait(key)


def x_fields(temp, velo, diff, side, cells_x, zs):
    two, one = (pl.ds(0, 2), pl.ds(0, 1)) if side == 0 else (pl.ds(cells_x - 2, 2), pl.ds(cells_x - 1, 1))
    return (
        (temp.at[two, :, zs], 0, 2),
        (diff.at[two, :, zs], 2, 2),
        (velo.at[0, two, :, zs], 4, 2),
        (velo.at[1, one, :, zs], 6, 1),
        (velo.at[2, one, :, zs], 7, 1),
    )


def near_kernel(cells_x, cells_y, depth, count_ref, wall, temp, velo, diff, xlow, xhigh, ylow, yhigh, wall_t, sems):
    copies = Copies(sems)
    count = depth // LANES
    for side, out in ((0, ylow), (1, yhigh)):
        first, near = (0, 0) if side == 0 else (cells_y - 2, cells_y - 1)
        picks = ((temp, first), (temp, first + 1), (diff, first), (diff, first + 1), (velo.at[1], first),
                 (velo.at[1], first + 1), (velo.at[0], near), (velo.at[2], near))
        for tile in range(count):
            for plane, (src, row) in enumerate(picks):
                copies.start("y", src.at[:, row, pl.ds(tile * LANES, LANES)], out.at[8 * tile + plane])
    for side, out in ((0, xlow), (1, xhigh)):
        for tile in range(count):
            for src, at, planes in x_fields(temp, velo, diff, side, cells_x, pl.ds(tile * LANES, LANES)):
                copies.start("x", src, out.at[pl.ds(8 * tile + at, planes)])
    lines = wall[...]
    group = LANES // cells_y
    shape = (cells_x, lines.shape[0])
    plain = jnp.zeros((cells_x, LANES), jnp.float32)
    for j in range(group):
        pick = ones_where(row_index(shape) == lane_index(shape) * group + j)
        spread = jnp.dot(pick, lines, precision=HIGHEST)
        plain = plain + (pltpu.roll(spread, LANES - j * cells_y, 1) if j else spread)
    plain = jnp.where(lane_index(plain.shape) < cells_y, plain, 0.0)
    same = ones_where(row_index((cells_x, LANES)) == lane_index((cells_x, LANES)))
    turned = lax.dot_general(plain, same, (((0,), (0,)), ((), ())), precision=HIGHEST)[:cells_y]
    wall_t[...] = turned

    def note(plane, place, at):
        lane = lane_index(plane.shape)
        live_two = jnp.where(place < count_ref[0], 2.0, 0.0)
        return jnp.where(lane == 0, live_two, jnp.where(lane == 1, pltpu.roll(plane, (LANES + 1 - at) % LANES, 1), 0.0))

    for side in range(2):
        x, y = side * (cells_x - 1), side * (cells_y - 1)
        (xlow, xhigh)[side][8 * count] = note(turned, x * cells_y + row_index(turned.shape), x)
        (ylow, yhigh)[side][8 * count] = note(plain, row_index(plain.shape) * cells_y + y, y)
    copies.wait_all()


def near_step(row_count, wall, temp, velo, diff):
    cells_x, cells_y, depth = temp.shape
    planes = 8 * (depth // LANES) + 1
    x_strip = jax.ShapeDtypeStruct((planes, cells_y, LANES), temp.dtype)
    y_strip = jax.ShapeDtypeStruct((planes, cells_x, LANES), temp.dtype)
    return pl.pallas_call(
        functools.partial(near_kernel, cells_x, cells_y, depth),
        out_shape=(x_strip, x_strip, y_strip, y_strip, jax.ShapeDtypeStruct((cells_y, LANES), temp.dtype)),
        in_specs=[SMEM, VMEM, HBM, HBM, HBM],
        out_specs=(VMEM,) * 5,
        scratch_shapes=[pltpu.SemaphoreType.DMA((26 * (depth // LANES),))],
        compiler_params=pltpu.CompilerParams(vmem_limit_bytes=VMEM_ALL),
        cost_estimate=lasts(4),
    )(row_count, wall, temp, velo, diff)


def corner_kernel(cells_y, count, xlo, xhi, low, high):
    for out, y in ((low, 0), (high, cells_y - 1)):
        for end, (strip, inner) in enumerate(((xlo, 1), (xhi, 0))):
            for j, plane in enumerate((inner, 2 + inner, 4 + inner, 6)):
                for tile in range(count):
                    out[pl.ds(4 * end + j, 1), pl.ds(tile * LANES, LANES)] = strip[8 * tile + plane, pl.ds(y, 1), :]


def solid_pack_kernel(cells_x, cells_y, pad, depth, *refs):
    xlow, xhigh, ylow, yhigh, sems = refs[4:]
    copies = Copies(sems)
    for field, src in enumerate(refs[:4]):
        for tile in range(depth // LANES):
            number, zs = field * (depth // LANES) + tile, pl.ds(tile * LANES, LANES)
            for side, out in ((0, xlow), (1, xhigh)):
                here = pl.ds(side * (cells_x - pad), pad)
                copies.start(0, src.at[here, :, zs], out.at[pl.ds(number * pad, pad)])
            for side, out in ((0, ylow), (1, yhigh)):
                here = pl.ds(side * (cells_y - TILE), TILE)
                copies.start(0, src.at[:, here, zs], out.at[pl.ds(number * cells_x, cells_x)])
    copies.wait_all()


def solid_corner_kernel(cells_y, numbers, xlo, xhi, low, high, tiles, sems):
    copies = Copies(sems)
    for side in range(2):
        rows = pl.ds(side * (cells_y - TILE), TILE)
        for end, strip in enumerate((xlo, xhi)):
            copies.start((side, end), strip.at[:, rows], tiles.at[side, end])
    for side, out in enumerate((low, high)):
        for end in range(2):
            copies.wait((side, end))
            for number in range(numbers):
                for i in range(1, TILE // 2 + 1):
                    near, far = (TILE - i, i) if end == 0 else (i - 1, TILE - 1 - i)
                    tile = tiles[side, end, number * TILE + near]
                    other = tiles[side, end, number * TILE + far]
                    row = row_index(tile.shape)
                    if side == 1:
                        tile = jnp.where(row >= i, tile, pltpu.roll(other, i, 0))
                    else:
                        tile = jnp.where(row < TILE - i, tile, pltpu.roll(other, TILE - i, 0))
                    out[(end * numbers + number) * (TILE // 2) + i - 1] = tile


def packing(kernel, shapes, copies, micros, *args):
    return pl.pallas_call(
        kernel,
        out_shape=tuple(jax.ShapeDtypeStruct(shape, jnp.float32) for shape in shapes),
        in_specs=[HBM if copies else VMEM] * len(args),
        out_specs=(VMEM,) * len(shapes),
        scratch_shapes=[pltpu.SemaphoreType.DMA((copies,))] if copies else [],
        compiler_params=pltpu.CompilerParams(vmem_limit_bytes=VMEM_ALL if copies else VMEM_ALL // 2),
        cost_estimate=lasts(micros),
    )(*args)


def exchange(low, high, axis, move):
    return move(high, axis, 1), move(low, axis, -1)


def solid_strips(solids, pad):
    cells_x, cells_y, depth = solids[0].shape
    numbers = 4 * (depth // LANES)
    x_shape, y_shape = (numbers * pad, cells_y, LANES), (numbers * cells_x, TILE, LANES)
    return packing(functools.partial(solid_pack_kernel, cells_x, cells_y, pad, depth),
                   (x_shape, x_shape, y_shape, y_shape), 4 * numbers, 3, *solids)


def solid_corners(xlo, xhi, numbers):
    cells_y = xlo.shape[1]
    shape = jax.ShapeDtypeStruct((numbers * TILE, TILE, LANES), jnp.float32)
    return pl.pallas_call(
        functools.partial(solid_corner_kernel, cells_y, numbers),
        out_shape=(shape, shape),
        in_specs=[HBM, HBM],
        out_specs=(VMEM, VMEM),
        scratch_shapes=[pltpu.VMEM((2, 2, numbers * TILE, TILE, LANES), jnp.float32), pltpu.SemaphoreType.DMA((4,))],
        compiler_params=pltpu.CompilerParams(vmem_limit_bytes=VMEM_ALL),
        cost_estimate=lasts(2),
    )(xlo, xhi)


def face(a_low, a_high, u_low, u_high):
    a_two = a_low + a_high
    u_two = u_low + u_high
    plus = a_two + jnp.maximum(u_two, 0.0)
    return plus, plus - u_two


def relaxation(a, ut, uz, low, high, above, below, live_two, wall):
    depth = a.shape[1]
    p_above, q_above = face(from_above(a, above[0]), a, from_above(ut, above[1]), ut)
    p_below, q_below = face(a, from_below(a, below[0]), ut, from_below(ut, below[1]))
    p_down, q_down = face(pltpu.roll(a, 1, 1), a, pltpu.roll(uz, 1, 1), uz)
    p_up, q_up = pltpu.roll(p_down, depth - 1, 1), pltpu.roll(q_down, depth - 1, 1)
    a_first = 2.0 * a[:, :LANES]
    u_last = 2.0 * uz[:, -LANES:]
    plus_last = 2.0 * a[:, -LANES:] + jnp.maximum(u_last, 0.0)
    gain = a_first * live_two
    p_down, q_down = first_lane(p_down, 0.0), first_lane(q_down, gain)
    p_up, q_up = last_lane(p_up, plus_last), last_lane(q_up, 0.0)
    leaving = (low[1] + high[0]) + (q_above + p_below) + (q_down + p_up)
    weight = leaving + ((low[0] + high[1]) + (p_above + q_below) + (p_down + q_up))
    head = weight[:, :LANES] + jnp.where(lane_index(gain.shape) == 0, 2.0 * a_first - gain, 0.0)
    weight = head if depth == LANES else jnp.concatenate([head, weight[:, LANES:]], axis=1)
    tail = weight[:, -LANES:] + jnp.where(lane_index(gain.shape) == LANES - 1, plus_last - u_last, 0.0)
    weight = tail if depth == LANES else jnp.concatenate([weight[:, :-LANES], tail], axis=1)
    factor = (2.0 * RELAX_FACTOR) * quick_reciprocal(weight)
    ghost = jnp.where(lane_index(gain.shape) == 0, gain * wall * factor[:, :LANES], 0.0)
    return (low[0] * factor, high[1] * factor, p_above * factor, q_below * factor, p_down * factor, q_up * factor,
            1.0 - leaving * factor, ghost)


def apply(factors, t, t_low, t_high, t_above, t_below):
    depth = t.shape[1]
    new = factors[6] * t + (factors[0] * t_low + factors[1] * t_high)
    new = new + (factors[2] * from_above(t, t_above) + factors[3] * from_below(t, t_below))
    new = new + (factors[4] * pltpu.roll(t, 1, 1) + factors[5] * pltpu.roll(t, depth - 1, 1))
    head = new[:, :LANES] + factors[7]
    return head if depth == LANES else jnp.concatenate([head, new[:, LANES:]], axis=1)


def fluid_kernel(cells_x, cells_y, depth, flags, wall_t, xlo, xhi, ylo, yhi, clo, chi, own_lo, own_hi,
                 temp, velo, diff, out, gas, ts, us, as_, vs, ws, t1, yl, yt, cs, ks, sems):
    rows_total = flags[4]
    tiles = [(tile, pl.ds(tile * LANES, LANES)) for tile in range(depth // LANES)]
    copies = Copies(sems)
    step = TILE
    starts = list(range(0, cells_x, step))

    def load(start):
        here = pl.ds(start, step)
        copies.start(start, temp.at[here], ts.at[pl.ds(start + 2, step)])
        copies.start(start, diff.at[here], as_.at[pl.ds(start + 2, step)])
        copies.start(start, velo.at[0, here], us.at[pl.ds(start + 2, step)])
        copies.start(start, velo.at[1, here], vs.at[pl.ds(start + 1, step)])
        copies.start(start, velo.at[2, here], ws.at[pl.ds(start + 1, step)])

    for start in starts[:2]:
        load(start)
    for side, halo in enumerate((xlo, xhi)):
        at, beside = (0, 0) if side == 0 else (cells_x + 2, cells_x + 1)
        for tile, zs in tiles:
            for j in range(2):
                ts[at + j, :, zs] = halo[8 * tile + j]
                as_[at + j, :, zs] = halo[8 * tile + 2 + j]
                us[at + j, :, zs] = halo[8 * tile + 4 + j]
            vs[beside, :, zs] = halo[8 * tile + 6]
            ws[beside, :, zs] = halo[8 * tile + 7]

        @pl.when(flags[side] == 0)
        def _():
            for ref, first, count in ((ts, at, 2), (as_, at, 2), (us, at, 2), (vs, beside, 1), (ws, beside, 1)):
                for j in range(count):
                    ref[first + j] = jnp.zeros(ref.shape[1:], jnp.float32)

    for side, halo in enumerate((ylo, yhi)):
        inner = 1 - side
        for plane in range(8):
            for tile, zs in tiles:
                yl[side, plane, pl.ds(TILE, cells_x), zs] = halo[8 * tile + plane]
        for end, at in enumerate((TILE - 1, TILE + cells_x)):
            good = flags[end] * flags[2 + side] > 0
            for j, plane in enumerate((inner, 2 + inner, 6, 4 + inner)):
                yl[side, plane, pl.ds(at, 1), :] = jnp.where(good, (clo, chi)[side][pl.ds(4 * end + j, 1), :], 0.0)

    def batch_factors(first, count, notes):
        a = [as_[first + j] for j in range(count + 2)]
        un = [us[first + j] for j in range(count + 2)]
        faces = [face(a[j], a[j + 1], un[j], un[j + 1]) for j in range(count + 1)]
        results = []
        for j in range(count):
            row = pl.ds(TILE - 1 + first + j, 1)
            results.append(relaxation(
                a[j + 1], vs[first + j], ws[first + j], faces[j], faces[j + 1], (yl[0, 3, row, :], yl[0, 5, row, :]),
                (yl[1, 2, row, :], yl[1, 4, row, :]), *notes[j]))
        return results

    def batch_apply(factors, ref, offset, first, rows_above, rows_below):
        t = [ref[first + offset - 1 + j] for j in range(len(factors) + 2)]
        results = []
        for j, plane in enumerate(factors):
            row = pl.ds(TILE - 1 + first + j, 1)
            results.append(apply(plane, t[j + 1], t[j], t[j + 2], rows_above[row, :], rows_below[row, :]))
        return results

    def note_of(note):
        return note, pltpu.roll(note, LANES - 1, 1)

    def own_note(i):
        place = (i - 1) * cells_y + row_index((cells_y, LANES))
        return jnp.where(place < rows_total, 2.0, 0.0), pltpu.roll(wall_t[...], LANES + 1 - i, 1)

    pair = 2

    def first_sweep(block, first):
        i = first + pair * block
        factors = batch_factors(i, pair, [own_note(i + j) for j in range(pair)])
        new = batch_apply(factors, ts, 1, i, yl.at[0, 1], yl.at[1, 0])
        for j in range(pair):
            for number in range(7):
                cs[number, i + j - 1] = factors[j][number]
            ks[i + j - 1] = factors[j][7]
            t1[i + j] = new[j]
        return first

    def halo_plane(i, side):
        factors = batch_factors(i, 1, [note_of((xlo, xhi)[side][8 * len(tiles)])])
        (new,) = batch_apply(factors, ts, 1, i, yl.at[0, 1], yl.at[1, 0])
        t1[i] = jnp.where(flags[side] > 0, new, 0.0)

    following = 1
    for number, start in enumerate(starts):
        copies.wait(start)
        if number + 2 < len(starts):
            load(starts[number + 2])
        if start == 0:
            halo_plane(0, 0)
        last = cells_x + 1 if start == starts[-1] else start + step - 1
        lax.fori_loop(0, (last - following) // pair, first_sweep, following)
        following = last
    halo_plane(cells_x + 1, 1)

    for side, own in enumerate((own_lo, own_hi)):
        inner = 1 - side
        rows, up, down = pl.ds(TILE, cells_x), pl.ds(TILE - 1, 1), pl.ds(TILE + cells_x, 1)

        def own_plane(plane):
            return jnp.concatenate([own[8 * tile + plane] for tile, _ in tiles], axis=1)

        t, a, un = yl[side, inner, rows, :], yl[side, 2 + inner, rows, :], yl[side, 4 + inner, rows, :]
        t_far, a_far, un_far = (yl[side, 1 - inner, rows, :], yl[side, 3 - inner, rows, :],
                                yl[side, 5 - inner, rows, :])
        t_own, a_own, un_own = own_plane(side), own_plane(2 + side), own_plane(4 + side)
        if side == 0:
            low, high = face(a_far, a, un_far, un), face(a, a_own, un, un_own)
            t_low, t_high = t_far, t_own
        else:
            low, high = face(a_own, a, un_own, un), face(a, a_far, un, un_far)
            t_low, t_high = t_own, t_far
        factors = relaxation(
            a, yl[side, 6, rows, :], yl[side, 7, rows, :], low, high,
            (yl[side, 2 + inner, up, :], yl[side, 6, up, :]), (yl[side, 2 + inner, down, :], yl[side, 6, down, :]),
            *note_of((ylo, yhi)[side][8 * len(tiles)]))
        new = apply(factors, t, t_low, t_high, yl[side, inner, up, :], yl[side, inner, down, :])
        yt[side, rows, :] = jnp.where(flags[2 + side] > 0, new, 0.0)

    group = 4

    def second_sweep(block, carry):
        first, plane = carry
        i = first + group * block
        factors = [[cs[number, i + j - 1] for number in range(7)] + [ks[i + j - 1]] for j in range(group)]
        new = batch_apply(factors, t1, 0, i, yt.at[0], yt.at[1])
        for j in range(group):
            ts[i + j - 1] = new[j]
            shift = i + j - 1
            plane = jnp.where(lane_index((cells_y, LANES)) == shift, pltpu.roll(new[j][:, :LANES], shift, 1), plane)
        return first, plane

    plane = jnp.zeros((cells_y, LANES), jnp.float32)
    for start in starts:
        _, plane = lax.fori_loop(0, step // group, second_sweep, (start + 1, plane))
        copies.start("out", ts.at[pl.ds(start, step)], out.at[pl.ds(start, step)])
    gas[...] = plane
    copies.wait("out")


def film_coefficients_kernel(cells_x, cells_y, flags, diff, out, tile, sem):
    copy = pltpu.make_async_copy(diff.at[:, :, pl.ds(0, LANES)], tile, sem)
    copy.start()
    copy.wait()
    shape = (cells_y, LANES)
    total = jnp.zeros(shape, jnp.float32)
    for x in range(cells_x):
        total = jnp.where(lane_index(shape) == x, pltpu.roll(tile[x], x, 1), total)
    place = lane_index(shape) * cells_y + row_index(shape)
    out[...] = jnp.where(place < flags[4], 2.0 * total, 0.0)


def film_coefficients(flags, diff):
    cells_x, cells_y, _ = diff.shape
    return pl.pallas_call(
        functools.partial(film_coefficients_kernel, cells_x, cells_y),
        out_shape=(jax.ShapeDtypeStruct((cells_y, LANES), diff.dtype),),
        in_specs=[SMEM, HBM],
        out_specs=(VMEM,),
        scratch_shapes=[pltpu.VMEM((cells_x, cells_y, LANES), jnp.float32), pltpu.SemaphoreType.DMA],
        compiler_params=pltpu.CompilerParams(vmem_limit_bytes=VMEM_ALL),
        cost_estimate=lasts(1),
    )(flags, diff)


def fluid_call(flags, wall_t, strips, temp, velo, diff):
    cells_x, cells_y, depth = temp.shape
    chunks = cells_x // TILE
    plane = jax.ShapeDtypeStruct((cells_y, LANES), temp.dtype)

    def planes(count):
        return pltpu.VMEM((count, cells_y, depth), jnp.float32)

    return pl.pallas_call(
        functools.partial(fluid_kernel, cells_x, cells_y, depth),
        out_shape=(jax.ShapeDtypeStruct(temp.shape, temp.dtype), plane),
        in_specs=[SMEM] + [VMEM] * 9 + [HBM] * 3,
        out_specs=(HBM, VMEM),
        scratch_shapes=[
            planes(cells_x + 4),
            planes(cells_x + 4),
            planes(cells_x + 4),
            planes(cells_x + 2),
            planes(cells_x + 2),
            planes(cells_x + 2),
            pltpu.VMEM((2, 8, cells_x + 2 * TILE, depth), jnp.float32),
            pltpu.VMEM((2, cells_x + 2 * TILE, depth), jnp.float32),
            pltpu.VMEM((7, cells_x, cells_y, depth), jnp.float32),
            pltpu.VMEM((cells_x, cells_y, LANES), jnp.float32),
            pltpu.SemaphoreType.DMA((6 * chunks,)),
        ],
        compiler_params=pltpu.CompilerParams(vmem_limit_bytes=VMEM_ALL),
        cost_estimate=lasts(13),
    )(flags, wall_t, *strips, temp, velo, diff)


def solid_kernel(
    cells_x, cells_y, depth, pad, coefficients,
    flags, cond, sink, heat, temp, xlo, xhi, ylo, yhi, clo, chi, film, film_lo, film_hi,
    out, surface, ks, es, bs, us, vs, gx, gy, gz, ss, fs, sems,
):
    wide_x, wide_y = cells_x + 2 * pad, cells_y + 2 * TILE
    copies = Copies(sems)
    own_x, own_y = pl.ds(pad, cells_x), pl.ds(TILE, cells_y)

    def load(field):
        src, dst = ((cond, ks), (sink, es), (heat, bs), (temp, us))[field]
        copies.start(field // 2, src, dst.at[own_x, own_y])
        for tile in range(depth // LANES):
            zs, number = pl.ds(tile * LANES, LANES), field * (depth // LANES) + tile
            key, numbers = field // 2, 4 * (depth // LANES)
            x_from, y_from = pl.ds(number * pad, pad), pl.ds(number * cells_x, cells_x)
            x_low, x_high = pl.ds(0, pad), pl.ds(pad + cells_x, pad)
            y_low, y_high = pl.ds(0, TILE), pl.ds(TILE + cells_y, TILE)
            copies.start(key, xlo.at[x_from], dst.at[x_low, own_y, zs])
            copies.start(key, xhi.at[x_from], dst.at[x_high, own_y, zs])
            copies.start(key, ylo.at[y_from], dst.at[own_x, y_low, zs])
            copies.start(key, yhi.at[y_from], dst.at[own_x, y_high, zs])
            for side, (strip, y_at) in enumerate(((clo, y_low), (chi, y_high))):
                for end in range(2):
                    for i in range(1, TILE + 1):
                        shared = min(i, TILE - i) or 1
                        tile = strip[(end * numbers + number) * (TILE // 2) + shared - 1]
                        if i > TILE // 2:
                            tile = pltpu.roll(tile, TILE - shared if side == 0 else shared, 0)
                        dst[pad - i if end == 0 else pad + cells_x + i - 1, y_at, zs] = tile
    load(0)
    load(1)
    fs[:, pl.ds(0, TILE), :] = jnp.where(flags[2] > 0, film_lo[...], 0.0)
    fs[:, own_y, :] = film[...]
    fs[:, pl.ds(TILE + cells_y, TILE), :] = jnp.where(flags[3] > 0, film_hi[...], 0.0)

    def harmonic(k, near):
        total = jnp.maximum(k + near, 1e-30)
        return (2.0 * k * near) * quick_reciprocal(total)

    def film_of(kind, x):
        return pltpu.roll(fs[kind], 2 * LANES + pad - x, 1)

    def add_first(value, extra):
        head = value[:, :LANES]
        head = head + jnp.where(lane_index(head.shape) == 0, extra, 0.0)
        return jnp.concatenate([head, value[:, LANES:]], axis=1) if depth > LANES else head

    gx[0, :, :] = jnp.zeros((wide_y, depth), jnp.float32)
    edge = row_index((wide_y, depth)) == wide_y - 1
    top = lane_index((wide_y, depth)) == depth - 1

    def conductances(x, carry):
        keep = jnp.where(x < wide_x - 1, 1.0, 0.0)
        follow = jnp.minimum(x + 1, wide_x - 1)
        k = ks[x]
        face_x = harmonic(k, ks[follow]) * keep
        face_y = jnp.where(edge, 0.0, harmonic(k, pltpu.roll(k, wide_y - 1, 0)))
        face_z = jnp.where(top, 0.0, harmonic(k, pltpu.roll(k, depth - 1, 1)))
        diag = add_first(es[x], film_of(0, x))
        diag = diag + (gx[x] + face_x) + (face_y + pltpu.roll(face_y, 1, 0))
        diag = diag + (face_z + pltpu.roll(face_z, 1, 1))
        gx[x + 1] = face_x
        gy[x] = face_y
        gz[x] = face_z
        es[x] = diag
        ss[x] = lax.rsqrt(jnp.maximum(diag, 1e-30))
        return carry

    copies.wait(0)
    load(2)
    load(3)
    for side in range(2):
        @pl.when(flags[side] == 0)
        def _():
            for j in range(pad):
                ks[side * (pad + cells_x) + j] = jnp.zeros((wide_y, depth), jnp.float32)

    lax.fori_loop(0, wide_x, conductances, 0, unroll=4)

    def scale(x, carry):
        follow = jnp.minimum(x + 1, wide_x - 1)
        s = ss[x]
        gx[x + 1] = gx[x + 1] * s * ss[follow]
        gy[x] = gy[x] * s * pltpu.roll(s, wide_y - 1, 0)
        gz[x] = gz[x] * s * pltpu.roll(s, depth - 1, 1)
        bs[x] = add_first(bs[x], film_of(1, x)) * s
        us[x] = us[x] * es[x] * s
        return carry

    copies.wait(1)
    lax.fori_loop(0, wide_x, scale, 0, unroll=4)

    total = len(coefficients)
    src, dst = us, vs
    for number, (decay, gain) in enumerate(coefficients):
        last = number == total - 1
        margin = total - 1 - number

        def some(block, carry, src=src, dst=dst, decay=decay, gain=gain, number=number, last=last, margin=margin):
            planes = [pad - margin + block * BATCH + j for j in range(BATCH)]
            here = [src[x] for x in planes]
            before = [src[planes[0] - 1]] + here[:-1]
            after = here[1:] + [src[planes[-1] + 1]]
            g_x = [gx[planes[0]]] + [gx[x + 1] for x in planes]
            results = []
            for j, x in enumerate(planes):
                g_y, g_z, value = gy[x], gz[x], here[j]
                total_in = g_x[j] * before[j] + g_x[j + 1] * after[j]
                total_in += g_y * pltpu.roll(value, wide_y - 1, 0) + pltpu.roll(g_y * value, 1, 0)
                total_in += g_z * pltpu.roll(value, depth - 1, 1) + pltpu.roll(g_z * value, 1, 1)
                fresh = value + gain * ((bs[x] - value) + total_in)
                if number > 0:
                    fresh = fresh + decay * (value - dst[x])
                results.append(fresh)
            for j, x in enumerate(planes):
                fresh = results[j]
                if last:
                    final = (fresh * ss[x])[TILE:TILE + cells_y]
                    out[x - pad] = final
                    shift = x - pad
                    lane = lane_index((cells_y, LANES))
                    surface[...] = jnp.where(lane == shift, pltpu.roll(final[:, :LANES], shift, 1), surface[...])
                else:
                    dst[x] = fresh
            return carry

        if last:
            surface[...] = jnp.zeros_like(surface)
        lax.fori_loop(0, -(-(cells_x + 2 * margin) // BATCH), some, 0)
        src, dst = dst, src


def solid_step(flags, cond, sink, heat, temp, halo, films, pad):
    cells_x, cells_y, depth = cond.shape
    wide_x, wide_y = cells_x + 2 * pad, cells_y + 2 * TILE
    area = pltpu.VMEM((wide_x + BATCH, wide_y, depth), jnp.float32)
    return pl.pallas_call(
        functools.partial(solid_kernel, cells_x, cells_y, depth, pad, cheby_coefficients(SWEEPS)),
        out_shape=(jax.ShapeDtypeStruct((cells_x, cells_y, depth), cond.dtype),
                   jax.ShapeDtypeStruct((cells_y, LANES), cond.dtype)),
        in_specs=[SMEM] + [HBM] * 8 + [VMEM] * 5,
        out_specs=(VMEM, VMEM),
        scratch_shapes=[area] * 5
        + [area] * 4
        + [pltpu.VMEM((2, wide_y, LANES), jnp.float32), pltpu.SemaphoreType.DMA((4 + 16 * (depth // LANES),))],
        compiler_params=pltpu.CompilerParams(vmem_limit_bytes=VMEM_ALL),
        cost_estimate=lasts(30),
    )(flags, cond, sink, heat, temp, *halo, *films)


def ones_where(condition):
    return jnp.where(condition, 1.0, 0.0)


def pick_dot(values, picks, dims):
    parts, rest = [], values
    for _ in range(2):
        scaled = rest * 65537.0
        parts.append(scaled - (scaled - rest))
        rest = rest - parts[-1]
    parts.append(rest)
    count = values.shape[0]
    if count % TILE:
        parts = [jnp.pad(part, ((0, TILE - count), (0, 0))) for part in parts]
    total = lax.dot_general(jnp.concatenate(parts, axis=0), picks, (dims, ((), ())),
                            precision=lax.Precision.DEFAULT, preferred_element_type=jnp.float32)
    size = parts[0].shape[0]
    total = total[:size] + (total[size:2 * size] + total[2 * size:])
    return total[:count]


def route_kernel(group_total, slot_cap, owner, out):
    dirs = owner[...]
    row_total = group_total * slot_cap
    codes = row_index((TILE, group_total))
    matched = ones_where((codes >= 1) & (codes <= 4) & (dirs == codes))
    before = ones_where(row_index((group_total, group_total)) < lane_index((group_total, group_total)))
    rank = jnp.dot(matched, before, precision=HIGHEST)
    start = jnp.where(matched > 0.5, rank * slot_cap, -1.0 * row_total)
    start = jnp.where(codes == 0, ones_where(dirs == 0), start)
    spread = ones_where(row_index((group_total, row_total)) == lane_index((group_total, row_total)) // slot_cap)
    wide = jnp.dot(start, spread, precision=HIGHEST)
    within = (lane_index((TILE, row_total)) % slot_cap).astype(jnp.float32)
    out[...] = jnp.where(row_index((TILE, row_total)) == 0, wide, wide + within)


def cell_values(plane_t, cells_x, cells_y, cells):
    count = cells.shape[1]
    in_x = ones_where(row_index((cells_x, count)) == cells // cells_y)
    in_y = ones_where(row_index((cells_y, count)) == cells % cells_y)
    lines = pick_dot(plane_t[:, :cells_x], in_x, ((1,), (0,)))
    return jnp.sum(lines * in_y, axis=0, keepdims=True)


def rows_kernel(cells_x, cells_y, near_rows, route, gas_t, film_t, pair, *outs):
    row_total = cells_x * cells_y
    cells = lane_index((1, row_total))
    film = cell_values(film_t[...], cells_x, cells_y, cells)
    gas = cell_values(gas_t[...], cells_x, cells_y, cells)
    values = jnp.concatenate([film, gas], axis=0)
    pair[...] = values
    for d in range(4):
        slots = route[d + 1:d + 2, :].astype(jnp.int32)
        pick = ones_where(row_index((near_rows, row_total)) == slots)
        outs[d][...] = pick_dot(values, pick, ((1,), (1,)))


def film_kernel(cells_x, cells_y, pad, flags, route, landing, pair, from_0, from_1, from_2, from_3, plane, low, high):
    cells = landing[...]
    slots = cells.shape[1]
    arrived = [jnp.where(flags[d] > 0, piece[...], 0.0) for d, piece in enumerate((from_0, from_1, from_2, from_3))]
    own = pair[...]
    film = jnp.concatenate([own[:1] * route[0:1, :]] + [piece[:1] for piece in arrived], axis=1)
    gas = jnp.concatenate([own[1:]] + [piece[1:] for piece in arrived], axis=1)
    in_x = ones_where(row_index((LANES, slots)) == cells // cells_y)
    in_y = ones_where(row_index((cells_y, slots)) == cells % cells_y)
    weighted = jnp.concatenate([in_y * film, in_y * (film * gas)], axis=0)
    total = pick_dot(weighted, in_x, ((1,), (1,)))
    lane = lane_index(total.shape)
    to_high = jnp.where(lane >= LANES - pad, pltpu.roll(total, LANES - cells_x, 1), 0.0)
    to_low = jnp.where((lane >= cells_x) & (lane < cells_x + pad), pltpu.roll(total, cells_x, 1), 0.0)
    for ref, value in ((plane, total), (low, to_low), (high, to_high)):
        ref[0] = value[:cells_y]
        ref[1] = value[cells_y:]


def widen_kernel(cells_y, flags, plane, low, high, out, first, last):
    total = plane[...] + jnp.where(flags[0] > 0, low[...], 0.0) + jnp.where(flags[1] > 0, high[...], 0.0)
    out[...] = total
    first[...] = total[:, :TILE]
    last[...] = total[:, cells_y - TILE:]


def gather_kernel(cells_x, cells_y, row_total, near_rows, landing, surface_t, own, *outs):
    values = cell_values(surface_t[...], cells_x, cells_y, landing[...])
    own[...] = values[:, :row_total]
    for d in range(4):
        outs[d][...] = values[:, row_total + d * near_rows:row_total + (d + 1) * near_rows]


def wall_kernel(near_rows, flags, route, own, from_0, from_1, from_2, from_3, out):
    row_total = own.shape[1]
    total = own[...] * route[0:1, :]
    for d, (piece, side) in enumerate(((from_0, 1), (from_1, 0), (from_2, 3), (from_3, 2))):
        slots = route[d + 1:d + 2, :].astype(jnp.int32)
        pick = ones_where(row_index((near_rows, row_total)) == slots)
        total = total + pick_dot(jnp.where(flags[side] > 0, piece[...], 0.0), pick, ((1,), (0,)))
    out[...] = jnp.where(lane_index((1, row_total)) < flags[4], total, 0.0)


def small_call(kernel, shapes, flags, *args):
    lead = [] if flags is None else [flags]
    return pl.pallas_call(
        kernel,
        out_shape=tuple(jax.ShapeDtypeStruct(shape, jnp.float32) for shape in shapes),
        in_specs=[SMEM] * len(lead) + [VMEM] * len(args),
        out_specs=tuple(VMEM for _ in shapes),
        compiler_params=pltpu.CompilerParams(vmem_limit_bytes=32 * 1024 * 1024),
        cost_estimate=lasts(1),
    )(*lead, *args)


def on_device(
    fluid_temp, velocity, eddy_diff, wall_prev, row_count, owner_table, landing_cell,
    solid_temp, conductivity, sink, heat_source,
):
    cells_x, cells_y, cells_z = fluid_temp.shape
    solid_x, solid_y, solid_z = solid_temp.shape
    row_total = cells_x * cells_y
    group_total = owner_table.shape[1]
    slot_cap = row_total // group_total
    near_rows = group_total // 8 * slot_cap
    pad = SWEEPS
    flags = jnp.concatenate([jnp.stack([*sides("blk"), *sides("sub")]).astype(jnp.int32), row_count])
    fluid = (fluid_temp, velocity, eddy_diff)
    solids = (conductivity, sink, heat_source, solid_temp)

    xlow, xhigh, ylow, yhigh, wall_t = near_step(row_count, wall_prev.reshape(row_total // LANES, LANES), *fluid)
    xlo, xhi = exchange(xlow, xhigh, "blk", ring)
    ylo, yhi = exchange(ylow, yhigh, "sub", chain)
    after_near = lax.optimization_barrier((xlow, *solids, eddy_diff, owner_table))[1:]
    strips = solid_strips(after_near[:4], pad)
    (film_t,) = film_coefficients(flags, after_near[4])
    (route,) = small_call(
        functools.partial(route_kernel, group_total, slot_cap), [(TILE, row_total)], None, after_near[5]
    )
    xlo, xhi, film_t, route, *strips = lax.optimization_barrier((xlo, xhi, film_t, route, *strips))
    blk_halo = exchange(*strips[:2], "blk", ring)
    corner = (TILE, cells_z)
    low, high = packing(functools.partial(corner_kernel, cells_y, cells_z // LANES), (corner, corner), 0, 1, xlo, xhi)
    clo, chi = exchange(low, high, "sub", ring)
    ylo, yhi, clo, chi, *sub_strips = lax.optimization_barrier((ylo, yhi, clo, chi, *strips[2:]))
    sub_halo = exchange(*sub_strips, "sub", chain)
    fluid_new, gas_t = fluid_call(flags, wall_t, (xlo, xhi, ylo, yhi, clo, chi, ylow, yhigh), *fluid)
    pair, *bands = small_call(
        functools.partial(rows_kernel, cells_x, cells_y, near_rows),
        [(2, row_total)] + [(2, near_rows)] * 4, None, route, gas_t, film_t,
    )
    moves = (("blk", 1), ("blk", -1), ("sub", 1), ("sub", -1))
    *bands, blk_low, blk_high, sub_low, sub_high = lax.optimization_barrier((*bands, *blk_halo, *sub_halo))
    arrived = [ring(band, axis, step) for band, (axis, step) in zip(bands, moves)]
    low, high = solid_corners(blk_low, blk_high, 4 * (solid_z // LANES))
    *arrived, low, high = lax.optimization_barrier((*arrived, low, high))
    halo = (blk_low, blk_high, sub_low, sub_high, *exchange(low, high, "sub", chain))
    plane = (2, solid_y, LANES)
    film, low, high = small_call(
        functools.partial(film_kernel, solid_x, solid_y, pad), [plane] * 3, flags, route, landing_cell, pair, *arrived
    )
    film, first, last = small_call(
        functools.partial(widen_kernel, solid_y), [plane] + [(2, TILE, LANES)] * 2,
        flags, film, ring(high, "blk", 1), ring(low, "blk", -1),
    )
    films = (film, ring(last, "sub", 1), ring(first, "sub", -1))
    solid_new, surface_t = solid_step(flags, *solids, halo, films, pad)

    own, *backs = small_call(
        functools.partial(gather_kernel, solid_x, solid_y, row_total, near_rows),
        [(1, row_total)] + [(1, near_rows)] * 4, None, landing_cell, surface_t,
    )
    returned = [ring(back, axis, -step) for back, (axis, step) in zip(backs, moves)]
    (wall_new,) = small_call(
        functools.partial(wall_kernel, near_rows), [(1, row_total)], flags, route, own, *returned
    )
    return fluid_new, solid_new, wall_new.reshape(row_total)


def solution(mesh):
    return jax.shard_map(
        on_device,
        mesh=mesh,
        in_specs=(
            P("blk", "sub", None),
            P(None, "blk", "sub", None),
            P("blk", "sub", None),
            P(("blk", "sub")),
            P(("blk", "sub")),
            P(("blk", "sub"), None),
            P(("blk", "sub"), None),
            P("blk", "sub", None),
            P("blk", "sub", None),
            P("blk", "sub", None),
            P("blk", "sub", None),
        ),
        out_specs=(P("blk", "sub", None), P("blk", "sub", None), P(("blk", "sub"))),
        check_vma=False,
    )
```

```python
import functools

import jax
import jax.numpy as jnp
from jax import lax
from jax.experimental import pallas as pl
from jax.experimental.pallas import tpu as pltpu
from jax.sharding import PartitionSpec as P

FLUID_SWEEPS = 2
SWEEPS = 8
RELAX_FACTOR = 0.8
EIG_LOW = 0.02
EIG_HIGH = 2.0
TILE = 8
LANES = 128
VMEM_ALL = 60 * 1024 * 1024
VMEM_FLUID = 53 * 1024 * 1024
VMEM_SOLID = 53 * 1024 * 1024
BATCH = 8
HIGHEST = lax.Precision.HIGHEST
VMEM = pl.BlockSpec(memory_space=pltpu.VMEM)
SMEM = pl.BlockSpec(memory_space=pltpu.SMEM)
HBM = pl.BlockSpec(memory_space=pltpu.HBM)


def cheby_coefficients(count_sweeps):
    center_eig = 0.5 * (EIG_HIGH + EIG_LOW)
    half_width = 0.5 * (EIG_HIGH - EIG_LOW)
    ratio_eig = center_eig / half_width
    damping = 1.0 / ratio_eig
    coefficients = [(0.0, 1.0 / center_eig)]
    for sweep_no in range(1, count_sweeps):
        damping_new = 1.0 / (2.0 * ratio_eig - damping)
        coefficients.append((damping_new * damping, 2.0 * damping_new / half_width))
        damping = damping_new
    return coefficients


def ring(value, axis, step):
    count = lax.axis_size(axis)
    return lax.ppermute(value, axis, [(i, (i + step) % count) for i in range(count)])


def chain(value, axis, step):
    count = lax.axis_size(axis)
    pairs = [(i, i + step) for i in range(count) if 0 <= i + step < count]
    return lax.ppermute(value, axis, pairs)


def sides(axis):
    place = lax.axis_index(axis)
    return place > 0, place < lax.axis_size(axis) - 1


def lasts(micros):
    return pl.CostEstimate(flops=0, bytes_accessed=int(micros * 3.69e6), transcendentals=0)


def quick_reciprocal(value):
    guess = pl.reciprocal(value, approx=True)
    return guess * (2.0 - value * guess)


def lane_index(shape):
    return lax.broadcasted_iota(jnp.int32, shape, 1)


def row_index(shape):
    return lax.broadcasted_iota(jnp.int32, shape, 0)


def first_lane(value, at_first):
    head = value[:, :LANES]
    head = jnp.where(lane_index(head.shape) == 0, at_first, head)
    if value.shape[1] == LANES:
        return head
    return jnp.concatenate([head, value[:, LANES:]], axis=1)


def last_lane(value, at_last):
    tail = value[:, -LANES:]
    tail = jnp.where(lane_index(tail.shape) == LANES - 1, at_last, tail)
    if value.shape[1] == LANES:
        return tail
    return jnp.concatenate([value[:, :-LANES], tail], axis=1)


def from_above(value, row):
    moved = pltpu.roll(value, 1, 0)
    head = jnp.where(row_index((TILE, value.shape[1])) == 0, row, moved[:TILE])
    return jnp.concatenate([head, moved[TILE:]], axis=0)


def from_below(value, row):
    moved = pltpu.roll(value, value.shape[0] - 1, 0)
    tail = jnp.where(row_index((TILE, value.shape[1])) == TILE - 1, row, moved[-TILE:])
    return jnp.concatenate([moved[:-TILE], tail], axis=0)


class Copies:
    def __init__(self, sems):
        self.sems, self.count, self.waits = sems, 0, {}

    def start(self, key, src, dst):
        made = pltpu.make_async_copy(src, dst, self.sems.at[self.count])
        self.count += 1
        made.start()
        self.waits.setdefault(key, []).append(made)

    def wait(self, key):
        for made in self.waits.pop(key, []):
            made.wait()

    def wait_all(self):
        for key in list(self.waits):
            self.wait(key)


def x_fields(temp, velo, diff, side, cells_x, zs):
    two, one = (pl.ds(0, 2), pl.ds(0, 1)) if side == 0 else (pl.ds(cells_x - 2, 2), pl.ds(cells_x - 1, 1))
    return (
        (temp.at[two, :, zs], 0, 2),
        (diff.at[two, :, zs], 2, 2),
        (velo.at[0, two, :, zs], 4, 2),
        (velo.at[1, one, :, zs], 6, 1),
        (velo.at[2, one, :, zs], 7, 1),
    )


def near_kernel(cells_x, cells_y, depth, count_ref, wall, temp, velo, diff, xlow, xhigh, ylow, yhigh, wall_t, sems):
    copies = Copies(sems)
    count = depth // LANES
    for side, out in ((0, ylow), (1, yhigh)):
        first, near = (0, 0) if side == 0 else (cells_y - 2, cells_y - 1)
        picks = ((temp, first), (temp, first + 1), (diff, first), (diff, first + 1), (velo.at[1], first),
                 (velo.at[1], first + 1), (velo.at[0], near), (velo.at[2], near))
        for tile in range(count):
            for plane, (src, row) in enumerate(picks):
                copies.start("y", src.at[:, row, pl.ds(tile * LANES, LANES)], out.at[8 * tile + plane])
    for side, out in ((0, xlow), (1, xhigh)):
        for tile in range(count):
            for src, at, planes in x_fields(temp, velo, diff, side, cells_x, pl.ds(tile * LANES, LANES)):
                copies.start("x", src, out.at[pl.ds(8 * tile + at, planes)])
    lines = wall[...]
    group = LANES // cells_y
    shape = (cells_x, lines.shape[0])
    plain = jnp.zeros((cells_x, LANES), jnp.float32)
    for j in range(group):
        pick = ones_where(row_index(shape) == lane_index(shape) * group + j)
        spread = jnp.dot(pick, lines, precision=HIGHEST)
        plain = plain + (pltpu.roll(spread, LANES - j * cells_y, 1) if j else spread)
    plain = jnp.where(lane_index(plain.shape) < cells_y, plain, 0.0)
    same = ones_where(row_index((cells_x, LANES)) == lane_index((cells_x, LANES)))
    turned = lax.dot_general(plain, same, (((0,), (0,)), ((), ())), precision=HIGHEST)[:cells_y]
    wall_t[...] = turned

    def note(plane, place, at):
        lane = lane_index(plane.shape)
        live_two = jnp.where(place < count_ref[0], 2.0, 0.0)
        return jnp.where(lane == 0, live_two, jnp.where(lane == 1, pltpu.roll(plane, (LANES + 1 - at) % LANES, 1), 0.0))

    for side in range(2):
        x, y = side * (cells_x - 1), side * (cells_y - 1)
        (xlow, xhigh)[side][8 * count] = note(turned, x * cells_y + row_index(turned.shape), x)
        (ylow, yhigh)[side][8 * count] = note(plain, row_index(plain.shape) * cells_y + y, y)
    copies.wait_all()


def near_step(row_count, wall, temp, velo, diff):
    cells_x, cells_y, depth = temp.shape
    planes = 8 * (depth // LANES) + 1
    x_strip = jax.ShapeDtypeStruct((planes, cells_y, LANES), temp.dtype)
    y_strip = jax.ShapeDtypeStruct((planes, cells_x, LANES), temp.dtype)
    return pl.pallas_call(
        functools.partial(near_kernel, cells_x, cells_y, depth),
        out_shape=(x_strip, x_strip, y_strip, y_strip, jax.ShapeDtypeStruct((cells_y, LANES), temp.dtype)),
        in_specs=[SMEM, VMEM, HBM, HBM, HBM],
        out_specs=(VMEM,) * 5,
        scratch_shapes=[pltpu.SemaphoreType.DMA((26 * (depth // LANES),))],
        compiler_params=pltpu.CompilerParams(vmem_limit_bytes=VMEM_ALL),
        cost_estimate=lasts(4),
    )(row_count, wall, temp, velo, diff)


def corner_kernel(cells_y, count, xlo, xhi, low, high):
    for out, y in ((low, 0), (high, cells_y - 1)):
        for end, (strip, inner) in enumerate(((xlo, 1), (xhi, 0))):
            for j, plane in enumerate((inner, 2 + inner, 4 + inner, 6)):
                for tile in range(count):
                    out[pl.ds(4 * end + j, 1), pl.ds(tile * LANES, LANES)] = strip[8 * tile + plane, pl.ds(y, 1), :]


def solid_pack_kernel(cells_x, cells_y, pad, depth, *refs):
    xlow, xhigh, ylow, yhigh, sems = refs[4:]
    copies = Copies(sems)
    for field, src in enumerate(refs[:4]):
        for tile in range(depth // LANES):
            number, zs = field * (depth // LANES) + tile, pl.ds(tile * LANES, LANES)
            for side, out in ((0, xlow), (1, xhigh)):
                here = pl.ds(side * (cells_x - pad), pad)
                copies.start(0, src.at[here, :, zs], out.at[pl.ds(number * pad, pad)])
            for side, out in ((0, ylow), (1, yhigh)):
                here = pl.ds(side * (cells_y - TILE), TILE)
                copies.start(0, src.at[:, here, zs], out.at[pl.ds(number * cells_x, cells_x)])
    copies.wait_all()


def solid_corner_kernel(cells_y, numbers, xlo, xhi, low, high):
    for side, out in enumerate((low, high)):
        rows = pl.ds(side * (cells_y - TILE), TILE)
        for end, strip in enumerate((xlo, xhi)):
            for number in range(numbers):
                for i in range(1, TILE // 2 + 1):
                    near, far = (TILE - i, i) if end == 0 else (i - 1, TILE - 1 - i)
                    tile = strip[number * TILE + near, rows, :]
                    other = strip[number * TILE + far, rows, :]
                    row = row_index(tile.shape)
                    if side == 1:
                        tile = jnp.where(row >= i, tile, pltpu.roll(other, i, 0))
                    else:
                        tile = jnp.where(row < TILE - i, tile, pltpu.roll(other, TILE - i, 0))
                    out[(end * numbers + number) * (TILE // 2) + i - 1] = tile


def packing(kernel, shapes, copies, micros, *args):
    return pl.pallas_call(
        kernel,
        out_shape=tuple(jax.ShapeDtypeStruct(shape, jnp.float32) for shape in shapes),
        in_specs=[HBM if copies else VMEM] * len(args),
        out_specs=(VMEM,) * len(shapes),
        scratch_shapes=[pltpu.SemaphoreType.DMA((copies,))] if copies else [],
        compiler_params=pltpu.CompilerParams(vmem_limit_bytes=VMEM_ALL if copies else VMEM_ALL // 2),
        cost_estimate=lasts(micros),
    )(*args)


def exchange(low, high, axis, move):
    return move(high, axis, 1), move(low, axis, -1)


def solid_strips(solids, pad):
    cells_x, cells_y, depth = solids[0].shape
    numbers = 4 * (depth // LANES)
    x_shape, y_shape = (numbers * pad, cells_y, LANES), (numbers * cells_x, TILE, LANES)
    return packing(functools.partial(solid_pack_kernel, cells_x, cells_y, pad, depth),
                   (x_shape, x_shape, y_shape, y_shape), 4 * numbers, 3, *solids)


def solid_corners(xlo, xhi, numbers):
    shape = (numbers * TILE, TILE, LANES)
    return packing(functools.partial(solid_corner_kernel, xlo.shape[1], numbers), (shape, shape), 0, 1, xlo, xhi)


def face(a_low, a_high, u_low, u_high):
    a_two = a_low + a_high
    u_two = u_low + u_high
    plus = a_two + jnp.maximum(u_two, 0.0)
    return plus, plus - u_two


def relaxation(a, ut, uz, low, high, above, below, live_two, wall):
    depth = a.shape[1]
    p_above, q_above = face(from_above(a, above[0]), a, from_above(ut, above[1]), ut)
    p_below, q_below = face(a, from_below(a, below[0]), ut, from_below(ut, below[1]))
    p_down, q_down = face(pltpu.roll(a, 1, 1), a, pltpu.roll(uz, 1, 1), uz)
    p_up, q_up = pltpu.roll(p_down, depth - 1, 1), pltpu.roll(q_down, depth - 1, 1)
    a_first = 2.0 * a[:, :LANES]
    u_last = 2.0 * uz[:, -LANES:]
    plus_last = 2.0 * a[:, -LANES:] + jnp.maximum(u_last, 0.0)
    gain = a_first * live_two
    p_down, q_down = first_lane(p_down, 0.0), first_lane(q_down, gain)
    p_up, q_up = last_lane(p_up, plus_last), last_lane(q_up, 0.0)
    leaving = (low[1] + high[0]) + (q_above + p_below) + (q_down + p_up)
    weight = leaving + ((low[0] + high[1]) + (p_above + q_below) + (p_down + q_up))
    head = weight[:, :LANES] + jnp.where(lane_index(gain.shape) == 0, 2.0 * a_first - gain, 0.0)
    weight = head if depth == LANES else jnp.concatenate([head, weight[:, LANES:]], axis=1)
    tail = weight[:, -LANES:] + jnp.where(lane_index(gain.shape) == LANES - 1, plus_last - u_last, 0.0)
    weight = tail if depth == LANES else jnp.concatenate([weight[:, :-LANES], tail], axis=1)
    factor = (2.0 * RELAX_FACTOR) * quick_reciprocal(weight)
    ghost = jnp.where(lane_index(gain.shape) == 0, gain * wall * factor[:, :LANES], 0.0)
    return (low[0] * factor, high[1] * factor, p_above * factor, q_below * factor, p_down * factor, q_up * factor,
            1.0 - leaving * factor, ghost)


def apply(factors, t, t_low, t_high, t_above, t_below):
    depth = t.shape[1]
    new = factors[6] * t + (factors[0] * t_low + factors[1] * t_high)
    new = new + (factors[2] * from_above(t, t_above) + factors[3] * from_below(t, t_below))
    new = new + (factors[4] * pltpu.roll(t, 1, 1) + factors[5] * pltpu.roll(t, depth - 1, 1))
    head = new[:, :LANES] + factors[7]
    return head if depth == LANES else jnp.concatenate([head, new[:, LANES:]], axis=1)


def fluid_kernel(cells_x, cells_y, depth, near_rows, flags, wall_t, xlo, xhi, ylo, yhi, clo, chi, own_lo, own_hi,
                 route, film_t, temp, velo, diff, out, pair_out, to_0, to_1, to_2, to_3, ts, us, as_, vs, ws, t1, yl, yt, cs, ks, sems):
    rows_total = flags[4]
    tiles = [(tile, pl.ds(tile * LANES, LANES)) for tile in range(depth // LANES)]
    copies = Copies(sems)
    step = TILE
    starts = list(range(0, cells_x, step))

    def load(start):
        here = pl.ds(start, step)
        copies.start(start, temp.at[here], ts.at[pl.ds(start + 2, step)])
        copies.start(start, diff.at[here], as_.at[pl.ds(start + 2, step)])
        copies.start(start, velo.at[0, here], us.at[pl.ds(start + 2, step)])
        copies.start(start, velo.at[1, here], vs.at[pl.ds(start + 1, step)])
        copies.start(start, velo.at[2, here], ws.at[pl.ds(start + 1, step)])

    for start in starts[:2]:
        load(start)
    for side, halo in enumerate((xlo, xhi)):
        at, beside = (0, 0) if side == 0 else (cells_x + 2, cells_x + 1)
        for tile, zs in tiles:
            for j in range(2):
                ts[at + j, :, zs] = halo[8 * tile + j]
                as_[at + j, :, zs] = halo[8 * tile + 2 + j]
                us[at + j, :, zs] = halo[8 * tile + 4 + j]
            vs[beside, :, zs] = halo[8 * tile + 6]
            ws[beside, :, zs] = halo[8 * tile + 7]

        @pl.when(flags[side] == 0)
        def _():
            for ref, first, count in ((ts, at, 2), (as_, at, 2), (us, at, 2), (vs, beside, 1), (ws, beside, 1)):
                for j in range(count):
                    ref[first + j] = jnp.zeros(ref.shape[1:], jnp.float32)

    for side, halo in enumerate((ylo, yhi)):
        inner = 1 - side
        for plane in range(8):
            for tile, zs in tiles:
                yl[side, plane, pl.ds(TILE, cells_x), zs] = halo[8 * tile + plane]
        for end, at in enumerate((TILE - 1, TILE + cells_x)):
            good = flags[end] * flags[2 + side] > 0
            for j, plane in enumerate((inner, 2 + inner, 6, 4 + inner)):
                yl[side, plane, pl.ds(at, 1), :] = jnp.where(good, (clo, chi)[side][pl.ds(4 * end + j, 1), :], 0.0)

    def batch_factors(first, count, notes):
        a = [as_[first + j] for j in range(count + 2)]
        un = [us[first + j] for j in range(count + 2)]
        faces = [face(a[j], a[j + 1], un[j], un[j + 1]) for j in range(count + 1)]
        results = []
        for j in range(count):
            row = pl.ds(TILE - 1 + first + j, 1)
            results.append(relaxation(
                a[j + 1], vs[first + j], ws[first + j], faces[j], faces[j + 1], (yl[0, 3, row, :], yl[0, 5, row, :]),
                (yl[1, 2, row, :], yl[1, 4, row, :]), *notes[j]))
        return results

    def batch_apply(factors, ref, offset, first, rows_above, rows_below):
        t = [ref[first + offset - 1 + j] for j in range(len(factors) + 2)]
        results = []
        for j, plane in enumerate(factors):
            row = pl.ds(TILE - 1 + first + j, 1)
            results.append(apply(plane, t[j + 1], t[j], t[j + 2], rows_above[row, :], rows_below[row, :]))
        return results

    def note_of(note):
        return note, pltpu.roll(note, LANES - 1, 1)

    def own_note(i):
        place = (i - 1) * cells_y + row_index((cells_y, LANES))
        return jnp.where(place < rows_total, 2.0, 0.0), pltpu.roll(wall_t[...], LANES + 1 - i, 1)

    pair = 2

    def first_sweep(block, first):
        i = first + pair * block
        factors = batch_factors(i, pair, [own_note(i + j) for j in range(pair)])
        new = batch_apply(factors, ts, 1, i, yl.at[0, 1], yl.at[1, 0])
        for j in range(pair):
            for number in range(7):
                cs[number, i + j - 1] = factors[j][number]
            ks[i + j - 1] = factors[j][7]
            t1[i + j] = new[j]
        return first

    def halo_plane(i, side):
        factors = batch_factors(i, 1, [note_of((xlo, xhi)[side][8 * len(tiles)])])
        (new,) = batch_apply(factors, ts, 1, i, yl.at[0, 1], yl.at[1, 0])
        t1[i] = jnp.where(flags[side] > 0, new, 0.0)

    following = 1
    for number, start in enumerate(starts):
        copies.wait(start)
        if number + 2 < len(starts):
            load(starts[number + 2])
        if start == 0:
            halo_plane(0, 0)
        last = cells_x + 1 if start == starts[-1] else start + step - 1
        lax.fori_loop(0, (last - following) // pair, first_sweep, following)
        following = last
    halo_plane(cells_x + 1, 1)

    for side, own in enumerate((own_lo, own_hi)):
        inner = 1 - side
        rows, up, down = pl.ds(TILE, cells_x), pl.ds(TILE - 1, 1), pl.ds(TILE + cells_x, 1)

        def own_plane(plane):
            return jnp.concatenate([own[8 * tile + plane] for tile, _ in tiles], axis=1)

        t, a, un = yl[side, inner, rows, :], yl[side, 2 + inner, rows, :], yl[side, 4 + inner, rows, :]
        t_far, a_far, un_far = (yl[side, 1 - inner, rows, :], yl[side, 3 - inner, rows, :],
                                yl[side, 5 - inner, rows, :])
        t_own, a_own, un_own = own_plane(side), own_plane(2 + side), own_plane(4 + side)
        if side == 0:
            low, high = face(a_far, a, un_far, un), face(a, a_own, un, un_own)
            t_low, t_high = t_far, t_own
        else:
            low, high = face(a_own, a, un_own, un), face(a, a_far, un, un_far)
            t_low, t_high = t_own, t_far
        factors = relaxation(
            a, yl[side, 6, rows, :], yl[side, 7, rows, :], low, high,
            (yl[side, 2 + inner, up, :], yl[side, 6, up, :]), (yl[side, 2 + inner, down, :], yl[side, 6, down, :]),
            *note_of((ylo, yhi)[side][8 * len(tiles)]))
        new = apply(factors, t, t_low, t_high, yl[side, inner, up, :], yl[side, inner, down, :])
        yt[side, rows, :] = jnp.where(flags[2 + side] > 0, new, 0.0)

    group = 4

    def second_sweep(block, carry):
        first, plane = carry
        i = first + group * block
        factors = [[cs[number, i + j - 1] for number in range(7)] + [ks[i + j - 1]] for j in range(group)]
        new = batch_apply(factors, t1, 0, i, yt.at[0], yt.at[1])
        for j in range(group):
            ts[i + j - 1] = new[j]
            shift = i + j - 1
            plane = jnp.where(lane_index((cells_y, LANES)) == shift, pltpu.roll(new[j][:, :LANES], shift, 1), plane)
        return first, plane

    plane = jnp.zeros((cells_y, LANES), jnp.float32)
    for start in starts:
        _, plane = lax.fori_loop(0, step // group, second_sweep, (start + 1, plane))
        copies.start("out", ts.at[pl.ds(start, step)], out.at[pl.ds(start, step)])
    rows_out(cells_x, cells_y, near_rows, route, plane, film_t, pair_out, to_0, to_1, to_2, to_3)
    copies.wait("out")


def film_coefficients_kernel(cells_x, cells_y, flags, diff, out, tile, sem):
    copy = pltpu.make_async_copy(diff.at[:, :, pl.ds(0, LANES)], tile, sem)
    copy.start()
    copy.wait()
    shape = (cells_y, LANES)
    total = jnp.zeros(shape, jnp.float32)
    for x in range(cells_x):
        total = jnp.where(lane_index(shape) == x, pltpu.roll(tile[x], x, 1), total)
    place = lane_index(shape) * cells_y + row_index(shape)
    out[...] = jnp.where(place < flags[4], 2.0 * total, 0.0)


def film_coefficients(flags, diff):
    cells_x, cells_y, _ = diff.shape
    return pl.pallas_call(
        functools.partial(film_coefficients_kernel, cells_x, cells_y),
        out_shape=(jax.ShapeDtypeStruct((cells_y, LANES), diff.dtype),),
        in_specs=[SMEM, HBM],
        out_specs=(VMEM,),
        scratch_shapes=[pltpu.VMEM((cells_x, cells_y, LANES), jnp.float32), pltpu.SemaphoreType.DMA],
        compiler_params=pltpu.CompilerParams(vmem_limit_bytes=VMEM_ALL),
        cost_estimate=lasts(1),
    )(flags, diff)


def fluid_call(flags, wall_t, strips, route, film_t, near_rows, temp, velo, diff):
    cells_x, cells_y, depth = temp.shape
    chunks = cells_x // TILE
    pair = jax.ShapeDtypeStruct((2, cells_x * cells_y), temp.dtype)
    band = jax.ShapeDtypeStruct((2, near_rows), temp.dtype)

    def planes(count):
        return pltpu.VMEM((count, cells_y, depth), jnp.float32)

    return pl.pallas_call(
        functools.partial(fluid_kernel, cells_x, cells_y, depth, near_rows),
        out_shape=(jax.ShapeDtypeStruct(temp.shape, temp.dtype), pair) + (band,) * 4,
        in_specs=[SMEM] + [VMEM] * 11 + [HBM] * 3,
        out_specs=(HBM,) + (VMEM,) * 5,
        scratch_shapes=[
            planes(cells_x + 4),
            planes(cells_x + 4),
            planes(cells_x + 4),
            planes(cells_x + 2),
            planes(cells_x + 2),
            planes(cells_x + 2),
            pltpu.VMEM((2, 8, cells_x + 2 * TILE, depth), jnp.float32),
            pltpu.VMEM((2, cells_x + 2 * TILE, depth), jnp.float32),
            pltpu.VMEM((7, cells_x, cells_y, depth), jnp.float32),
            pltpu.VMEM((cells_x, cells_y, LANES), jnp.float32),
            pltpu.SemaphoreType.DMA((6 * chunks,)),
        ],
        compiler_params=pltpu.CompilerParams(vmem_limit_bytes=VMEM_FLUID),
        cost_estimate=lasts(13),
    )(flags, wall_t, *strips, route, film_t, temp, velo, diff)


def solid_kernel(
    cells_x, cells_y, depth, pad, coefficients,
    near_rows, flags, cond, sink, heat, temp, xlo, xhi, ylo, yhi, clo, chi, film, film_lo, film_hi, landing,
    out, own_rows, to_0, to_1, to_2, to_3, ks, es, bs, us, vs, gx, gy, gz, ss, fs, sems,
):
    wide_x, wide_y = cells_x + 2 * pad, cells_y + 2 * TILE
    copies = Copies(sems)
    own_x, own_y = pl.ds(pad, cells_x), pl.ds(TILE, cells_y)

    def load(field):
        src, dst = ((cond, ks), (sink, es), (heat, bs), (temp, us))[field]
        copies.start(field // 2, src, dst.at[own_x, own_y])
        for tile in range(depth // LANES):
            zs, number = pl.ds(tile * LANES, LANES), field * (depth // LANES) + tile
            key, numbers = field // 2, 4 * (depth // LANES)
            x_from, y_from = pl.ds(number * pad, pad), pl.ds(number * cells_x, cells_x)
            x_low, x_high = pl.ds(0, pad), pl.ds(pad + cells_x, pad)
            y_low, y_high = pl.ds(0, TILE), pl.ds(TILE + cells_y, TILE)
            copies.start(key, xlo.at[x_from], dst.at[x_low, own_y, zs])
            copies.start(key, xhi.at[x_from], dst.at[x_high, own_y, zs])
            copies.start(key, ylo.at[y_from], dst.at[own_x, y_low, zs])
            copies.start(key, yhi.at[y_from], dst.at[own_x, y_high, zs])
            for side, (strip, y_at) in enumerate(((clo, y_low), (chi, y_high))):
                for end in range(2):
                    for i in range(1, TILE + 1):
                        shared = min(i, TILE - i) or 1
                        tile = strip[(end * numbers + number) * (TILE // 2) + shared - 1]
                        if i > TILE // 2:
                            tile = pltpu.roll(tile, TILE - shared if side == 0 else shared, 0)
                        dst[pad - i if end == 0 else pad + cells_x + i - 1, y_at, zs] = tile
    load(0)
    load(1)
    fs[:, pl.ds(0, TILE), :] = jnp.where(flags[2] > 0, film_lo[...], 0.0)
    fs[:, own_y, :] = film[...]
    fs[:, pl.ds(TILE + cells_y, TILE), :] = jnp.where(flags[3] > 0, film_hi[...], 0.0)

    def harmonic(k, near):
        total = jnp.maximum(k + near, 1e-30)
        return (2.0 * k * near) * quick_reciprocal(total)

    def film_of(kind, x):
        return pltpu.roll(fs[kind], 2 * LANES + pad - x, 1)

    def add_first(value, extra):
        head = value[:, :LANES]
        head = head + jnp.where(lane_index(head.shape) == 0, extra, 0.0)
        return jnp.concatenate([head, value[:, LANES:]], axis=1) if depth > LANES else head

    gx[0, :, :] = jnp.zeros((wide_y, depth), jnp.float32)
    edge = row_index((wide_y, depth)) == wide_y - 1
    top = lane_index((wide_y, depth)) == depth - 1

    def conductances(x, carry):
        keep = jnp.where(x < wide_x - 1, 1.0, 0.0)
        follow = jnp.minimum(x + 1, wide_x - 1)
        k = ks[x]
        face_x = harmonic(k, ks[follow]) * keep
        face_y = jnp.where(edge, 0.0, harmonic(k, pltpu.roll(k, wide_y - 1, 0)))
        face_z = jnp.where(top, 0.0, harmonic(k, pltpu.roll(k, depth - 1, 1)))
        diag = add_first(es[x], film_of(0, x))
        diag = diag + (gx[x] + face_x) + (face_y + pltpu.roll(face_y, 1, 0))
        diag = diag + (face_z + pltpu.roll(face_z, 1, 1))
        gx[x + 1] = face_x
        gy[x] = face_y
        gz[x] = face_z
        es[x] = diag
        ss[x] = lax.rsqrt(jnp.maximum(diag, 1e-30))
        return carry

    copies.wait(0)
    load(2)
    load(3)
    for side in range(2):
        @pl.when(flags[side] == 0)
        def _():
            for j in range(pad):
                ks[side * (pad + cells_x) + j] = jnp.zeros((wide_y, depth), jnp.float32)

    lax.fori_loop(0, wide_x, conductances, 0, unroll=4)

    def scale(x, carry):
        follow = jnp.minimum(x + 1, wide_x - 1)
        s = ss[x]
        gx[x + 1] = gx[x + 1] * s * ss[follow]
        gy[x] = gy[x] * s * pltpu.roll(s, wide_y - 1, 0)
        gz[x] = gz[x] * s * pltpu.roll(s, depth - 1, 1)
        bs[x] = add_first(bs[x], film_of(1, x)) * s
        us[x] = us[x] * es[x] * s
        return carry

    copies.wait(1)
    lax.fori_loop(0, wide_x, scale, 0, unroll=4)

    total = len(coefficients)
    src, dst = us, vs
    for number, (decay, gain) in enumerate(coefficients):
        last = number == total - 1
        margin = total - 1 - number

        def some(block, surface, src=src, dst=dst, decay=decay, gain=gain, number=number, last=last, margin=margin):
            planes = [pad - margin + block * BATCH + j for j in range(BATCH)]
            here = [src[x] for x in planes]
            before = [src[planes[0] - 1]] + here[:-1]
            after = here[1:] + [src[planes[-1] + 1]]
            g_x = [gx[planes[0]]] + [gx[x + 1] for x in planes]
            results = []
            for j, x in enumerate(planes):
                g_y, g_z, value = gy[x], gz[x], here[j]
                total_in = g_x[j] * before[j] + g_x[j + 1] * after[j]
                total_in += g_y * pltpu.roll(value, wide_y - 1, 0) + pltpu.roll(g_y * value, 1, 0)
                total_in += g_z * pltpu.roll(value, depth - 1, 1) + pltpu.roll(g_z * value, 1, 1)
                fresh = value + gain * ((bs[x] - value) + total_in)
                if number > 0:
                    fresh = fresh + decay * (value - dst[x])
                results.append(fresh)
            for j, x in enumerate(planes):
                fresh = results[j]
                if last:
                    final = (fresh * ss[x])[TILE:TILE + cells_y]
                    es[x, pl.ds(0, cells_y), :] = final
                    shift = x - pad
                    lane = lane_index((cells_y, LANES))
                    surface = jnp.where(lane == shift, pltpu.roll(final[:, :LANES], shift, 1), surface)
                else:
                    dst[x] = fresh
            return surface

        if last:
            surface = jnp.zeros((cells_y, LANES), jnp.float32)
            for block in range(cells_x // BATCH):
                surface = some(block, surface)
                here = pl.ds(block * BATCH, BATCH)
                copies.start("out", es.at[pl.ds(pad + block * BATCH, BATCH), pl.ds(0, cells_y)], out.at[here])
            gather_out(cells_x, cells_y, near_rows, landing, surface, own_rows, to_0, to_1, to_2, to_3)
            copies.wait("out")
            break
        lax.fori_loop(0, -(-(cells_x + 2 * margin) // BATCH), some, 0)
        src, dst = dst, src


def solid_step(flags, cond, sink, heat, temp, halo, films, landing, row_total, near_rows, pad):
    cells_x, cells_y, depth = cond.shape
    wide_x, wide_y = cells_x + 2 * pad, cells_y + 2 * TILE
    area = pltpu.VMEM((wide_x + BATCH, wide_y, depth), jnp.float32)
    return pl.pallas_call(
        functools.partial(solid_kernel, cells_x, cells_y, depth, pad, cheby_coefficients(SWEEPS), near_rows),
        out_shape=tuple(jax.ShapeDtypeStruct(shape, cond.dtype)
                        for shape in [(cells_x, cells_y, depth), (1, row_total)] + [(1, near_rows)] * 4),
        in_specs=[SMEM] + [HBM] * 8 + [VMEM] * 6,
        out_specs=(HBM,) + (VMEM,) * 5,
        scratch_shapes=[area] * 5
        + [area] * 4
        + [pltpu.VMEM((2, wide_y, LANES), jnp.float32), pltpu.SemaphoreType.DMA((4 + 16 * (depth // LANES) + cells_x // BATCH,))],
        compiler_params=pltpu.CompilerParams(vmem_limit_bytes=VMEM_SOLID),
        cost_estimate=lasts(30),
    )(flags, cond, sink, heat, temp, *halo, *films, landing)


def ones_where(condition):
    return jnp.where(condition, 1.0, 0.0)


def pick_dot(values, picks, dims):
    parts, rest = [], values
    for _ in range(2):
        scaled = rest * 65537.0
        parts.append(scaled - (scaled - rest))
        rest = rest - parts[-1]
    parts.append(rest)
    count = values.shape[0]
    if count % TILE:
        parts = [jnp.pad(part, ((0, TILE - count), (0, 0))) for part in parts]
    total = lax.dot_general(jnp.concatenate(parts, axis=0), picks, (dims, ((), ())),
                            precision=lax.Precision.DEFAULT, preferred_element_type=jnp.float32)
    size = parts[0].shape[0]
    total = total[:size] + (total[size:2 * size] + total[2 * size:])
    return total[:count]


def route_kernel(group_total, slot_cap, owner, out):
    dirs = owner[...]
    row_total = group_total * slot_cap
    codes = row_index((TILE, group_total))
    matched = ones_where((codes >= 1) & (codes <= 4) & (dirs == codes))
    before = ones_where(row_index((group_total, group_total)) < lane_index((group_total, group_total)))
    rank = jnp.dot(matched, before, precision=HIGHEST)
    start = jnp.where(matched > 0.5, rank * slot_cap, -1.0 * row_total)
    start = jnp.where(codes == 0, ones_where(dirs == 0), start)
    spread = ones_where(row_index((group_total, row_total)) == lane_index((group_total, row_total)) // slot_cap)
    wide = jnp.dot(start, spread, precision=HIGHEST)
    within = (lane_index((TILE, row_total)) % slot_cap).astype(jnp.float32)
    out[...] = jnp.where(row_index((TILE, row_total)) == 0, wide, wide + within)


def cell_values(plane_t, cells_x, cells_y, cells):
    count = cells.shape[1]
    in_x = ones_where(row_index((cells_x, count)) == cells // cells_y)
    in_y = ones_where(row_index((cells_y, count)) == cells % cells_y)
    lines = pick_dot(plane_t[:, :cells_x], in_x, ((1,), (0,)))
    return jnp.sum(lines * in_y, axis=0, keepdims=True)


def rows_out(cells_x, cells_y, near_rows, route, gas_t, film_t, pair, *outs):
    row_total = cells_x * cells_y
    cells = lane_index((1, row_total))
    film = cell_values(film_t[...], cells_x, cells_y, cells)
    gas = cell_values(gas_t, cells_x, cells_y, cells)
    values = jnp.concatenate([film, gas], axis=0)
    pair[...] = values
    for d in range(4):
        slots = route[d + 1:d + 2, :].astype(jnp.int32)
        pick = ones_where(row_index((near_rows, row_total)) == slots)
        outs[d][...] = pick_dot(values, pick, ((1,), (1,)))


def film_kernel(cells_x, cells_y, pad, flags, route, landing, pair, from_0, from_1, from_2, from_3, plane, low, high):
    cells = landing[...]
    slots = cells.shape[1]
    arrived = [jnp.where(flags[d] > 0, piece[...], 0.0) for d, piece in enumerate((from_0, from_1, from_2, from_3))]
    own = pair[...]
    film = jnp.concatenate([own[:1] * route[0:1, :]] + [piece[:1] for piece in arrived], axis=1)
    gas = jnp.concatenate([own[1:]] + [piece[1:] for piece in arrived], axis=1)
    in_x = ones_where(row_index((LANES, slots)) == cells // cells_y)
    in_y = ones_where(row_index((cells_y, slots)) == cells % cells_y)
    weighted = jnp.concatenate([in_y * film, in_y * (film * gas)], axis=0)
    total = pick_dot(weighted, in_x, ((1,), (1,)))
    lane = lane_index(total.shape)
    to_high = jnp.where(lane >= LANES - pad, pltpu.roll(total, LANES - cells_x, 1), 0.0)
    to_low = jnp.where((lane >= cells_x) & (lane < cells_x + pad), pltpu.roll(total, cells_x, 1), 0.0)
    for ref, value in ((plane, total), (low, to_low), (high, to_high)):
        ref[0] = value[:cells_y]
        ref[1] = value[cells_y:]


def widen_kernel(cells_y, flags, plane, low, high, out, first, last):
    total = plane[...] + jnp.where(flags[0] > 0, low[...], 0.0) + jnp.where(flags[1] > 0, high[...], 0.0)
    out[...] = total
    first[...] = total[:, :TILE]
    last[...] = total[:, cells_y - TILE:]


def gather_out(cells_x, cells_y, near_rows, landing, surface_t, own, *outs):
    values = cell_values(surface_t, cells_x, cells_y, landing[...])
    row_total = own.shape[1]
    own[...] = values[:, :row_total]
    for d in range(4):
        outs[d][...] = values[:, row_total + d * near_rows:row_total + (d + 1) * near_rows]


def wall_kernel(near_rows, flags, route, own, from_0, from_1, from_2, from_3, out):
    row_total = own.shape[1]
    total = own[...] * route[0:1, :]
    for d, (piece, side) in enumerate(((from_0, 1), (from_1, 0), (from_2, 3), (from_3, 2))):
        slots = route[d + 1:d + 2, :].astype(jnp.int32)
        pick = ones_where(row_index((near_rows, row_total)) == slots)
        total = total + pick_dot(jnp.where(flags[side] > 0, piece[...], 0.0), pick, ((1,), (0,)))
    out[...] = jnp.where(lane_index((1, row_total)) < flags[4], total, 0.0)


def small_call(kernel, shapes, flags, *args):
    lead = [] if flags is None else [flags]
    return pl.pallas_call(
        kernel,
        out_shape=tuple(jax.ShapeDtypeStruct(shape, jnp.float32) for shape in shapes),
        in_specs=[SMEM] * len(lead) + [VMEM] * len(args),
        out_specs=tuple(VMEM for _ in shapes),
        compiler_params=pltpu.CompilerParams(vmem_limit_bytes=32 * 1024 * 1024),
        cost_estimate=lasts(1),
    )(*lead, *args)


def on_device(
    fluid_temp, velocity, eddy_diff, wall_prev, row_count, owner_table, landing_cell,
    solid_temp, conductivity, sink, heat_source,
):
    cells_x, cells_y, cells_z = fluid_temp.shape
    solid_x, solid_y, solid_z = solid_temp.shape
    row_total = cells_x * cells_y
    group_total = owner_table.shape[1]
    slot_cap = row_total // group_total
    near_rows = group_total // 8 * slot_cap
    pad = SWEEPS
    flags = jnp.concatenate([jnp.stack([*sides("blk"), *sides("sub")]).astype(jnp.int32), row_count])
    fluid = (fluid_temp, velocity, eddy_diff)
    solids = (conductivity, sink, heat_source, solid_temp)

    xlow, xhigh, ylow, yhigh, wall_t = near_step(row_count, wall_prev.reshape(row_total // LANES, LANES), *fluid)
    xlo, xhi = exchange(xlow, xhigh, "blk", ring)
    ylo, yhi = exchange(ylow, yhigh, "sub", chain)
    after_near = lax.optimization_barrier((xlow, *solids, eddy_diff))[1:]
    strips = solid_strips(after_near[:4], pad)
    (film_t,) = film_coefficients(flags, after_near[4])
    xlo, xhi, owners, film_t, *strips = lax.optimization_barrier((xlo, xhi, owner_table, film_t, *strips))
    blk_halo = exchange(*strips[:2], "blk", ring)
    (route,) = small_call(
        functools.partial(route_kernel, group_total, slot_cap), [(TILE, row_total)], None, owners
    )
    xlo, xhi, route = lax.optimization_barrier((xlo, xhi, route))
    corner = (TILE, cells_z)
    low, high = packing(functools.partial(corner_kernel, cells_y, cells_z // LANES), (corner, corner), 0, 1, xlo, xhi)
    clo, chi = exchange(low, high, "sub", ring)
    ylo, yhi, clo, chi, *sub_strips = lax.optimization_barrier((ylo, yhi, clo, chi, *strips[2:]))
    sub_halo = exchange(*sub_strips, "sub", chain)
    fluid_new, pair, *bands = fluid_call(
        flags, wall_t, (xlo, xhi, ylo, yhi, clo, chi, ylow, yhigh), route, film_t, near_rows, *fluid
    )
    moves = (("blk", 1), ("blk", -1), ("sub", 1), ("sub", -1))
    *bands, blk_low, blk_high = lax.optimization_barrier((*bands, *blk_halo))
    bands[2], bands[3], sub_low, sub_high = lax.optimization_barrier((bands[2], bands[3], *sub_halo))
    arrived = [ring(band, axis, step) for band, (axis, step) in zip(bands, moves)]
    low, high = solid_corners(blk_low, blk_high, 4 * (solid_z // LANES))
    *arrived, low, high = lax.optimization_barrier((*arrived, low, high))
    halo = (blk_low, blk_high, sub_low, sub_high, *exchange(low, high, "sub", chain))
    plane = (2, solid_y, LANES)
    film, low, high = small_call(
        functools.partial(film_kernel, solid_x, solid_y, pad), [plane] * 3, flags, route, landing_cell, pair, *arrived
    )
    film, first, last = small_call(
        functools.partial(widen_kernel, solid_y), [plane] + [(2, TILE, LANES)] * 2,
        flags, film, ring(high, "blk", 1), ring(low, "blk", -1),
    )
    films = (film, ring(last, "sub", 1), ring(first, "sub", -1))
    solid_new, own, *backs = solid_step(flags, *solids, halo, films, landing_cell, row_total, near_rows, pad)
    returned = [ring(back, axis, -step) for back, (axis, step) in zip(backs, moves)]
    (wall_new,) = small_call(
        functools.partial(wall_kernel, near_rows), [(1, row_total)], flags, route, own, *returned
    )
    return fluid_new, solid_new, wall_new.reshape(row_total)


def solution(mesh):
    return jax.shard_map(
        on_device,
        mesh=mesh,
        in_specs=(
            P("blk", "sub", None),
            P(None, "blk", "sub", None),
            P("blk", "sub", None),
            P(("blk", "sub")),
            P(("blk", "sub")),
            P(("blk", "sub"), None),
            P(("blk", "sub"), None),
            P("blk", "sub", None),
            P("blk", "sub", None),
            P("blk", "sub", None),
            P("blk", "sub", None),
        ),
        out_specs=(P("blk", "sub", None), P("blk", "sub", None), P(("blk", "sub"))),
        check_vma=False,
    )
```

```python
import functools

import jax
import jax.numpy as jnp
from jax import lax
from jax.experimental import pallas as pl
from jax.experimental.pallas import tpu as pltpu
from jax.sharding import PartitionSpec as P

FLUID_SWEEPS = 2
SWEEPS = 8
RELAX_FACTOR = 0.8
EIG_LOW = 0.02
EIG_HIGH = 2.0
TILE = 8
LANES = 128
VMEM_ALL = 60 * 1024 * 1024
VMEM_FLUID = 53 * 1024 * 1024
VMEM_SOLID = 53 * 1024 * 1024
BATCH = 8
HIGHEST = lax.Precision.HIGHEST
VMEM = pl.BlockSpec(memory_space=pltpu.VMEM)
SMEM = pl.BlockSpec(memory_space=pltpu.SMEM)
HBM = pl.BlockSpec(memory_space=pltpu.HBM)


def cheby_coefficients(count_sweeps):
    center_eig = 0.5 * (EIG_HIGH + EIG_LOW)
    half_width = 0.5 * (EIG_HIGH - EIG_LOW)
    ratio_eig = center_eig / half_width
    damping = 1.0 / ratio_eig
    coefficients = [(0.0, 1.0 / center_eig)]
    for sweep_no in range(1, count_sweeps):
        damping_new = 1.0 / (2.0 * ratio_eig - damping)
        coefficients.append((damping_new * damping, 2.0 * damping_new / half_width))
        damping = damping_new
    return coefficients


def ring(value, axis, step):
    count = lax.axis_size(axis)
    return lax.ppermute(value, axis, [(i, (i + step) % count) for i in range(count)])


def chain(value, axis, step):
    count = lax.axis_size(axis)
    pairs = [(i, i + step) for i in range(count) if 0 <= i + step < count]
    return lax.ppermute(value, axis, pairs)


def sides(axis):
    place = lax.axis_index(axis)
    return place > 0, place < lax.axis_size(axis) - 1


def lasts(micros):
    return pl.CostEstimate(flops=0, bytes_accessed=int(micros * 3.69e6), transcendentals=0)


def quick_reciprocal(value):
    guess = pl.reciprocal(value, approx=True)
    return guess * (2.0 - value * guess)


def lane_index(shape):
    return lax.broadcasted_iota(jnp.int32, shape, 1)


def row_index(shape):
    return lax.broadcasted_iota(jnp.int32, shape, 0)


def first_lane(value, at_first):
    head = value[:, :LANES]
    head = jnp.where(lane_index(head.shape) == 0, at_first, head)
    if value.shape[1] == LANES:
        return head
    return jnp.concatenate([head, value[:, LANES:]], axis=1)


def last_lane(value, at_last):
    tail = value[:, -LANES:]
    tail = jnp.where(lane_index(tail.shape) == LANES - 1, at_last, tail)
    if value.shape[1] == LANES:
        return tail
    return jnp.concatenate([value[:, :-LANES], tail], axis=1)


def from_above(value, row):
    moved = pltpu.roll(value, 1, 0)
    head = jnp.where(row_index((TILE, value.shape[1])) == 0, row, moved[:TILE])
    return jnp.concatenate([head, moved[TILE:]], axis=0)


def from_below(value, row):
    moved = pltpu.roll(value, value.shape[0] - 1, 0)
    tail = jnp.where(row_index((TILE, value.shape[1])) == TILE - 1, row, moved[-TILE:])
    return jnp.concatenate([moved[:-TILE], tail], axis=0)


class Copies:
    def __init__(self, sems):
        self.sems, self.count, self.waits = sems, 0, {}

    def start(self, key, src, dst):
        made = pltpu.make_async_copy(src, dst, self.sems.at[self.count])
        self.count += 1
        made.start()
        self.waits.setdefault(key, []).append(made)

    def wait(self, key):
        for made in self.waits.pop(key, []):
            made.wait()

    def wait_all(self):
        for key in list(self.waits):
            self.wait(key)


PLANES = 6


def strip_sums(side, t, a, un, uz, t_far, a_far, un_far, live_two, wall):
    depth = t.shape[1]
    if side == 0:
        plus, minus = face(a, a_far, un, un_far)
        total = minus * t_far - plus * t
    else:
        plus, minus = face(a_far, a, un_far, un)
        total = plus * t_far - minus * t
    p_down, q_down = face(pltpu.roll(a, 1, 1), a, pltpu.roll(uz, 1, 1), uz)
    p_up, q_up = pltpu.roll(p_down, depth - 1, 1), pltpu.roll(q_down, depth - 1, 1)
    a_first, a_last, u_last = 2.0 * a[:, :LANES], 2.0 * a[:, -LANES:], 2.0 * uz[:, -LANES:]
    plus_last = a_last + jnp.maximum(u_last, 0.0)
    weight = (plus + minus) + first_lane(p_down + q_down, 2.0 * a_first)
    weight = weight + last_lane(p_up + q_up, 2.0 * plus_last - u_last)
    gain = a_first * live_two
    p_down, q_down = first_lane(p_down, 0.0), first_lane(q_down, gain)
    p_up, q_up = last_lane(p_up, plus_last), last_lane(q_up, 0.0)
    total = total + (p_down * pltpu.roll(t, 1, 1) + q_up * pltpu.roll(t, depth - 1, 1)) - (q_down + p_up) * t
    head = total[:, :LANES] + jnp.where(lane_index(gain.shape) == 0, gain * wall, 0.0)
    return (head if depth == LANES else jnp.concatenate([head, total[:, LANES:]], axis=1)), weight


def near_kernel(cells_x, cells_y, depth, count_ref, wall, temp, velo, diff, xlow, xhigh, ylow, yhigh, wall_t,
                sx, sy, sems):
    copies = Copies(sems)
    for side in range(2):
        edge, far = (0, 1) if side == 0 else (cells_y - 1, cells_y - 2)
        sources = ((temp, edge), (diff, edge), (velo.at[1], edge), (velo.at[0], edge), (velo.at[2], edge),
                   (temp, far), (diff, far), (velo.at[1], far))
        for plane, (src, y) in enumerate(sources):
            copies.start(("y", side), src.at[:, y, :], sy.at[side, plane])
    for side in range(2):
        edge, far = (0, 1) if side == 0 else (cells_x - 1, cells_x - 2)
        sources = ((temp, edge), (diff, edge), (velo.at[0], edge), (velo.at[1], edge), (velo.at[2], edge),
                   (temp, far), (diff, far), (velo.at[0], far))
        for plane, (src, x) in enumerate(sources):
            copies.start(("x", side), src.at[x], sx.at[side, plane])
    lines = wall[...]
    group = LANES // cells_y
    shape = (cells_x, lines.shape[0])
    plain = jnp.zeros((cells_x, LANES), jnp.float32)
    for j in range(group):
        pick = ones_where(row_index(shape) == lane_index(shape) * group + j)
        spread = jnp.dot(pick, lines, precision=HIGHEST)
        plain = plain + (pltpu.roll(spread, LANES - j * cells_y, 1) if j else spread)
    plain = jnp.where(lane_index(plain.shape) < cells_y, plain, 0.0)
    same = ones_where(row_index((cells_x, LANES)) == lane_index((cells_x, LANES)))
    turned = lax.dot_general(plain, same, (((0,), (0,)), ((), ())), precision=HIGHEST)[:cells_y]
    wall_t[...] = turned
    for side in range(2):
        x, y = side * (cells_x - 1), side * (cells_y - 1)
        for key, ref, out, plane, place, at in (
            ("x", sx, (xlow, xhigh)[side], turned, x * cells_y + row_index(turned.shape), x),
            ("y", sy, (ylow, yhigh)[side], plain, row_index(plain.shape) * cells_y + y, y),
        ):
            copies.wait((key, side))
            t, a, un, ut, uz, t_far, a_far, un_far = [ref[side, number] for number in range(8)]
            live_two = jnp.where(place < count_ref[0], 2.0, 0.0)
            sums = strip_sums(side, t, a, un, uz, t_far, a_far, un_far, live_two,
                              pltpu.roll(plane, LANES - at, 1) if at else plane)
            for number, value in enumerate((t, a, un, ut) + sums):
                for tile in range(depth // LANES):
                    out[PLANES * tile + number] = value[:, tile * LANES:(tile + 1) * LANES]


def near_step(row_count, wall, temp, velo, diff):
    cells_x, cells_y, depth = temp.shape
    planes = PLANES * (depth // LANES)
    x_strip = jax.ShapeDtypeStruct((planes, cells_y, LANES), temp.dtype)
    y_strip = jax.ShapeDtypeStruct((planes, cells_x, LANES), temp.dtype)
    return pl.pallas_call(
        functools.partial(near_kernel, cells_x, cells_y, depth),
        out_shape=(x_strip, x_strip, y_strip, y_strip, jax.ShapeDtypeStruct((cells_y, LANES), temp.dtype)),
        in_specs=[SMEM, VMEM, HBM, HBM, HBM],
        out_specs=(VMEM,) * 5,
        scratch_shapes=[
            pltpu.VMEM((2, 8, cells_y, depth), jnp.float32),
            pltpu.VMEM((2, 8, cells_x, depth), jnp.float32),
            pltpu.SemaphoreType.DMA((32,)),
        ],
        compiler_params=pltpu.CompilerParams(vmem_limit_bytes=VMEM_ALL),
        cost_estimate=lasts(4),
    )(row_count, wall, temp, velo, diff)


def corner_kernel(cells_y, count, xlo, xhi, low, high):
    for out, y in ((low, 0), (high, cells_y - 1)):
        for end, strip in enumerate((xlo, xhi)):
            for j in range(4):
                for tile in range(count):
                    out[pl.ds(4 * end + j, 1), pl.ds(tile * LANES, LANES)] = strip[PLANES * tile + j, pl.ds(y, 1), :]


def layers_of(field, pad):
    return pad


def layers_before(field, tile, tiles, pad):
    return sum(tiles * layers_of(other, pad) for other in range(field)) + tile * layers_of(field, pad)


def solid_pack_kernel(cells_x, cells_y, pad, depth, *refs):
    xlow, xhigh, ylow, yhigh, sems = refs[4:]
    copies = Copies(sems)
    for field, src in enumerate(refs[:4]):
        for tile in range(depth // LANES):
            number, zs = field * (depth // LANES) + tile, pl.ds(tile * LANES, LANES)
            layers, before = layers_of(field, pad), layers_before(field, tile, depth // LANES, pad)
            for side, out in ((0, xlow), (1, xhigh)):
                here = pl.ds(side * (cells_x - layers), layers)
                copies.start(0, src.at[here, :, zs], out.at[pl.ds(before, layers)])
            for side, out in ((0, ylow), (1, yhigh)):
                here = pl.ds(side * (cells_y - TILE), TILE)
                copies.start(0, src.at[:, here, zs], out.at[pl.ds(number * cells_x, cells_x)])
    copies.wait_all()


def solid_corner_kernel(cells_y, numbers, xlo, xhi, low, high):
    for side, out in enumerate((low, high)):
        rows = pl.ds(side * (cells_y - TILE), TILE)
        for end, strip in enumerate((xlo, xhi)):
            for number in range(numbers):
                field, part = divmod(number, numbers // 4)
                layers, before = layers_of(field, TILE), layers_before(field, part, numbers // 4, TILE)
                for i in range(1, TILE // 2 + 1):
                    near, far = (layers - i, layers - TILE + i) if end == 0 else (i - 1, TILE - 1 - i)
                    tile = strip[before + near, rows, :]
                    other = strip[before + far, rows, :]
                    row = row_index(tile.shape)
                    if side == 1:
                        tile = jnp.where(row >= i, tile, pltpu.roll(other, i, 0))
                    else:
                        tile = jnp.where(row < TILE - i, tile, pltpu.roll(other, TILE - i, 0))
                    out[(end * numbers + number) * (TILE // 2) + i - 1] = tile


def packing(kernel, shapes, copies, micros, *args):
    return pl.pallas_call(
        kernel,
        out_shape=tuple(jax.ShapeDtypeStruct(shape, jnp.float32) for shape in shapes),
        in_specs=[HBM if copies else VMEM] * len(args),
        out_specs=(VMEM,) * len(shapes),
        scratch_shapes=[pltpu.SemaphoreType.DMA((copies,))] if copies else [],
        compiler_params=pltpu.CompilerParams(vmem_limit_bytes=VMEM_ALL if copies else VMEM_ALL // 2),
        cost_estimate=lasts(micros),
    )(*args)


def exchange(low, high, axis, move):
    return move(high, axis, 1), move(low, axis, -1)


def solid_strips(solids, pad):
    cells_x, cells_y, depth = solids[0].shape
    numbers = 4 * (depth // LANES)
    planes = layers_before(4, 0, depth // LANES, pad)
    x_shape, y_shape = (planes, cells_y, LANES), (numbers * cells_x, TILE, LANES)
    return packing(functools.partial(solid_pack_kernel, cells_x, cells_y, pad, depth),
                   (x_shape, x_shape, y_shape, y_shape), 4 * numbers, 3, *solids)


def solid_corners(xlo, xhi, numbers):
    shape = (numbers * TILE, TILE, LANES)
    return packing(functools.partial(solid_corner_kernel, xlo.shape[1], numbers), (shape, shape), 0, 1, xlo, xhi)


def face(a_low, a_high, u_low, u_high):
    a_two = a_low + a_high
    u_two = u_low + u_high
    plus = a_two + jnp.maximum(u_two, 0.0)
    return plus, plus - u_two


def relaxation(a, ut, uz, low, high, above, below, live_two, wall):
    depth = a.shape[1]
    p_above, q_above = face(from_above(a, above[0]), a, from_above(ut, above[1]), ut)
    p_below, q_below = face(a, from_below(a, below[0]), ut, from_below(ut, below[1]))
    p_down, q_down = face(pltpu.roll(a, 1, 1), a, pltpu.roll(uz, 1, 1), uz)
    p_up, q_up = pltpu.roll(p_down, depth - 1, 1), pltpu.roll(q_down, depth - 1, 1)
    a_first = 2.0 * a[:, :LANES]
    u_last = 2.0 * uz[:, -LANES:]
    plus_last = 2.0 * a[:, -LANES:] + jnp.maximum(u_last, 0.0)
    gain = a_first * live_two
    p_down, q_down = first_lane(p_down, 0.0), first_lane(q_down, gain)
    p_up, q_up = last_lane(p_up, plus_last), last_lane(q_up, 0.0)
    leaving = (low[1] + high[0]) + (q_above + p_below) + (q_down + p_up)
    weight = leaving + ((low[0] + high[1]) + (p_above + q_below) + (p_down + q_up))
    head = weight[:, :LANES] + jnp.where(lane_index(gain.shape) == 0, 2.0 * a_first - gain, 0.0)
    weight = head if depth == LANES else jnp.concatenate([head, weight[:, LANES:]], axis=1)
    tail = weight[:, -LANES:] + jnp.where(lane_index(gain.shape) == LANES - 1, plus_last - u_last, 0.0)
    weight = tail if depth == LANES else jnp.concatenate([weight[:, :-LANES], tail], axis=1)
    factor = (2.0 * RELAX_FACTOR) * quick_reciprocal(weight)
    ghost = jnp.where(lane_index(gain.shape) == 0, gain * wall * factor[:, :LANES], 0.0)
    return (low[0] * factor, high[1] * factor, p_above * factor, q_below * factor, p_down * factor, q_up * factor,
            1.0 - leaving * factor, ghost)


def apply(factors, t, t_low, t_high, t_above, t_below):
    depth = t.shape[1]
    new = factors[6] * t + (factors[0] * t_low + factors[1] * t_high)
    new = new + (factors[2] * from_above(t, t_above) + factors[3] * from_below(t, t_below))
    new = new + (factors[4] * pltpu.roll(t, 1, 1) + factors[5] * pltpu.roll(t, depth - 1, 1))
    head = new[:, :LANES] + factors[7]
    return head if depth == LANES else jnp.concatenate([head, new[:, LANES:]], axis=1)


def fluid_kernel(cells_x, cells_y, depth, near_rows, flags, wall_t, xlo, xhi, ylo, yhi, clo, chi, own_lo, own_hi,
                 route, temp, velo, diff, out, pair_out, to_0, to_1, to_2, to_3, ts, us, as_, vs, ws, t1, yl, yt, cs, ks, sems):
    rows_total = flags[4]
    tiles = [(tile, pl.ds(tile * LANES, LANES)) for tile in range(depth // LANES)]
    copies = Copies(sems)
    step = TILE
    starts = list(range(0, cells_x, step))

    def load(start):
        here = pl.ds(start, step)
        copies.start(start, temp.at[here], ts.at[pl.ds(start + 2, step)])
        copies.start(start, diff.at[here], as_.at[pl.ds(start + 2, step)])
        copies.start(start, velo.at[0, here], us.at[pl.ds(start + 2, step)])
        copies.start(start, velo.at[1, here], vs.at[pl.ds(start + 1, step)])
        copies.start(start, velo.at[2, here], ws.at[pl.ds(start + 1, step)])

    for start in starts[:2]:
        load(start)
    for side, halo in enumerate((xlo, xhi)):
        at = 1 if side == 0 else cells_x + 2
        for tile, zs in tiles:
            for number, ref in enumerate((ts, as_, us)):
                ref[at, :, zs] = halo[PLANES * tile + number]

        @pl.when(flags[side] == 0)
        def _():
            for ref in (ts, as_, us):
                ref[at] = jnp.zeros(ref.shape[1:], jnp.float32)

    for side, halo in enumerate((ylo, yhi)):
        for number in range(PLANES):
            for tile, zs in tiles:
                yl[side, number, pl.ds(TILE, cells_x), zs] = halo[PLANES * tile + number]
        for end, at in enumerate((TILE - 1, TILE + cells_x)):
            good = flags[end] * flags[2 + side] > 0
            for j, number in enumerate((0, 1, 3, 2)):
                yl[side, number, pl.ds(at, 1), :] = jnp.where(good, (clo, chi)[side][pl.ds(4 * end + j, 1), :], 0.0)

    def strip_plane(strip, number):
        return jnp.concatenate([strip[PLANES * tile + number] for tile, _ in tiles], axis=1)

    def beside(side, t, a, un, ut, total, weight, own, above, below):
        low, high = (t, a, un), own
        if side == 1:
            low, high = high, low
        plus, minus = face(low[1], high[1], low[2], high[2])
        total = total + (minus * own[0] - plus * t if side == 0 else plus * own[0] - minus * t)
        weight = weight + (plus + minus)
        plus, minus = face(from_above(a, above[1]), a, from_above(ut, above[2]), ut)
        total = total + (plus * from_above(t, above[0]) - minus * t)
        weight = weight + (plus + minus)
        plus, minus = face(a, from_below(a, below[1]), ut, from_below(ut, below[2]))
        total = total + (minus * from_below(t, below[0]) - plus * t)
        weight = weight + (plus + minus)
        return t + (2.0 * RELAX_FACTOR) * total * quick_reciprocal(weight)

    def batch_factors(first, count, notes):
        a = [as_[first + j] for j in range(count + 2)]
        un = [us[first + j] for j in range(count + 2)]
        faces = [face(a[j], a[j + 1], un[j], un[j + 1]) for j in range(count + 1)]
        results = []
        for j in range(count):
            row = pl.ds(TILE - 1 + first + j, 1)
            results.append(relaxation(
                a[j + 1], vs[first + j], ws[first + j], faces[j], faces[j + 1], (yl[0, 1, row, :], yl[0, 2, row, :]),
                (yl[1, 1, row, :], yl[1, 2, row, :]), *notes[j]))
        return results

    def batch_apply(factors, ref, offset, first, rows_above, rows_below):
        t = [ref[first + offset - 1 + j] for j in range(len(factors) + 2)]
        results = []
        for j, plane in enumerate(factors):
            row = pl.ds(TILE - 1 + first + j, 1)
            results.append(apply(plane, t[j + 1], t[j], t[j + 2], rows_above[row, :], rows_below[row, :]))
        return results

    def own_note(i):
        place = (i - 1) * cells_y + row_index((cells_y, LANES))
        return jnp.where(place < rows_total, 2.0, 0.0), pltpu.roll(wall_t[...], LANES + 1 - i, 1)

    pair = 2

    def first_sweep(block, first):
        i = first + pair * block
        factors = batch_factors(i, pair, [own_note(i + j) for j in range(pair)])
        new = batch_apply(factors, ts, 1, i, yl.at[0, 0], yl.at[1, 0])
        for j in range(pair):
            for number in range(7):
                cs[number, i + j - 1] = factors[j][number]
            ks[i + j - 1] = factors[j][7]
            t1[i + j] = new[j]
        return first

    def halo_plane(side):
        at, inside, row = (1, 2, TILE - 1) if side == 0 else (cells_x + 2, cells_x + 1, TILE + cells_x)
        strip, row = (xlo, xhi)[side], pl.ds(row, 1)
        new = beside(side, ts[at], as_[at], us[at], strip_plane(strip, 3), strip_plane(strip, 4), strip_plane(strip, 5),
                     (ts[inside], as_[inside], us[inside]), [yl[0, number, row, :] for number in range(3)],
                     [yl[1, number, row, :] for number in range(3)])
        t1[0 if side == 0 else cells_x + 1] = jnp.where(flags[side] > 0, new, 0.0)

    following = 1
    for number, start in enumerate(starts):
        copies.wait(start)
        if number + 2 < len(starts):
            load(starts[number + 2])
        if start == 0:
            halo_plane(0)
        last = cells_x + 1 if start == starts[-1] else start + step - 1
        lax.fori_loop(0, (last - following) // pair, first_sweep, following)
        following = last
    halo_plane(1)

    for side, own in enumerate((own_lo, own_hi)):
        rows, up, down = pl.ds(TILE, cells_x), pl.ds(TILE - 1, 1), pl.ds(TILE + cells_x, 1)
        new = beside(side, *[yl[side, number, rows, :] for number in range(PLANES)],
                     [strip_plane(own, number) for number in range(3)],
                     [yl[side, number, up, :] for number in (0, 1, 3)],
                     [yl[side, number, down, :] for number in (0, 1, 3)])
        yt[side, rows, :] = jnp.where(flags[2 + side] > 0, new, 0.0)

    group = 4

    def second_sweep(block, carry):
        first, plane = carry
        i = first + group * block
        factors = [[cs[number, i + j - 1] for number in range(7)] + [ks[i + j - 1]] for j in range(group)]
        new = batch_apply(factors, t1, 0, i, yt.at[0], yt.at[1])
        for j in range(group):
            ts[i + j - 1] = new[j]
            shift = i + j - 1
            plane = jnp.where(lane_index((cells_y, LANES)) == shift, pltpu.roll(new[j][:, :LANES], shift, 1), plane)
        return first, plane

    plane = jnp.zeros((cells_y, LANES), jnp.float32)
    for start in starts:
        _, plane = lax.fori_loop(0, step // group, second_sweep, (start + 1, plane))
        copies.start("out", ts.at[pl.ds(start, step)], out.at[pl.ds(start, step)])
    film = jnp.zeros((cells_y, LANES), jnp.float32)
    lane = lane_index(film.shape)
    for x in range(cells_x):
        film = jnp.where(lane == x, pltpu.roll(as_[x + 2, :, pl.ds(0, LANES)], x, 1), film)
    film = jnp.where(lane * cells_y + row_index(film.shape) < rows_total, 2.0 * film, 0.0)
    rows_out(cells_x, cells_y, near_rows, route, plane, film, pair_out, to_0, to_1, to_2, to_3)
    copies.wait("out")


def fluid_call(flags, wall_t, strips, route, near_rows, temp, velo, diff):
    cells_x, cells_y, depth = temp.shape
    chunks = cells_x // TILE
    pair = jax.ShapeDtypeStruct((2, cells_x * cells_y), temp.dtype)
    band = jax.ShapeDtypeStruct((2, near_rows), temp.dtype)

    def planes(count):
        return pltpu.VMEM((count, cells_y, depth), jnp.float32)

    return pl.pallas_call(
        functools.partial(fluid_kernel, cells_x, cells_y, depth, near_rows),
        out_shape=(jax.ShapeDtypeStruct(temp.shape, temp.dtype), pair) + (band,) * 4,
        in_specs=[SMEM] + [VMEM] * 10 + [HBM] * 3,
        out_specs=(HBM,) + (VMEM,) * 5,
        scratch_shapes=[
            planes(cells_x + 4),
            planes(cells_x + 4),
            planes(cells_x + 4),
            planes(cells_x + 2),
            planes(cells_x + 2),
            planes(cells_x + 2),
            pltpu.VMEM((2, PLANES, cells_x + 2 * TILE, depth), jnp.float32),
            pltpu.VMEM((2, cells_x + 2 * TILE, depth), jnp.float32),
            pltpu.VMEM((7, cells_x, cells_y, depth), jnp.float32),
            pltpu.VMEM((cells_x, cells_y, LANES), jnp.float32),
            pltpu.SemaphoreType.DMA((6 * chunks,)),
        ],
        compiler_params=pltpu.CompilerParams(vmem_limit_bytes=VMEM_FLUID),
        cost_estimate=lasts(1),
    )(flags, wall_t, *strips, route, temp, velo, diff)


def solid_kernel(
    cells_x, cells_y, depth, pad, coefficients,
    near_rows, flags, cond, sink, heat, temp, xlo, xhi, ylo, yhi, clo, chi, film, film_lo, film_hi, landing,
    out, own_rows, to_0, to_1, to_2, to_3, ks, es, bs, us, vs, gx, gy, gz, ss, fs, sems,
):
    wide_x, wide_y = cells_x + 2 * pad, cells_y + 2 * TILE
    copies = Copies(sems)
    own_x, own_y = pl.ds(pad, cells_x), pl.ds(TILE, cells_y)

    def load(field):
        src, dst = ((cond, ks), (sink, es), (heat, bs), (temp, us))[field]
        if layers_of(field, pad) < pad:
            for x in (0, wide_x - 1):
                dst[x] = jnp.ones((wide_y, depth), jnp.float32)
        copies.start(field // 2, src, dst.at[own_x, own_y])
        for tile in range(depth // LANES):
            zs, number = pl.ds(tile * LANES, LANES), field * (depth // LANES) + tile
            key, numbers = field // 2, 4 * (depth // LANES)
            layers = layers_of(field, pad)
            x_from = pl.ds(layers_before(field, tile, depth // LANES, pad), layers)
            y_from = pl.ds(number * cells_x, cells_x)
            x_low, x_high = pl.ds(pad - layers, layers), pl.ds(pad + cells_x, layers)
            y_low, y_high = pl.ds(0, TILE), pl.ds(TILE + cells_y, TILE)
            copies.start(key, xlo.at[x_from], dst.at[x_low, own_y, zs])
            copies.start(key, xhi.at[x_from], dst.at[x_high, own_y, zs])
            copies.start(key, ylo.at[y_from], dst.at[own_x, y_low, zs])
            copies.start(key, yhi.at[y_from], dst.at[own_x, y_high, zs])
            for side, (strip, y_at) in enumerate(((clo, y_low), (chi, y_high))):
                for end in range(2):
                    for i in range(1, TILE + 1):
                        shared = min(i, TILE - i) or 1
                        tile = strip[(end * numbers + number) * (TILE // 2) + shared - 1]
                        if i > TILE // 2:
                            tile = pltpu.roll(tile, TILE - shared if side == 0 else shared, 0)
                        dst[pad - i if end == 0 else pad + cells_x + i - 1, y_at, zs] = tile
    load(0)
    load(1)
    fs[:, pl.ds(0, TILE), :] = jnp.where(flags[2] > 0, film_lo[...], 0.0)
    fs[:, own_y, :] = film[...]
    fs[:, pl.ds(TILE + cells_y, TILE), :] = jnp.where(flags[3] > 0, film_hi[...], 0.0)

    def harmonic(k, near):
        total = jnp.maximum(k + near, 1e-30)
        return (2.0 * k * near) * quick_reciprocal(total)

    def film_of(kind, x):
        return pltpu.roll(fs[kind], 2 * LANES + pad - x, 1)

    def add_first(value, extra):
        head = value[:, :LANES]
        head = head + jnp.where(lane_index(head.shape) == 0, extra, 0.0)
        return jnp.concatenate([head, value[:, LANES:]], axis=1) if depth > LANES else head

    gx[0, :, :] = jnp.zeros((wide_y, depth), jnp.float32)
    edge = row_index((wide_y, depth)) == wide_y - 1
    top = lane_index((wide_y, depth)) == depth - 1

    def conductances(x, carry):
        keep = jnp.where(x < wide_x - 1, 1.0, 0.0)
        follow = jnp.minimum(x + 1, wide_x - 1)
        k = ks[x]
        face_x = harmonic(k, ks[follow]) * keep
        face_y = jnp.where(edge, 0.0, harmonic(k, pltpu.roll(k, wide_y - 1, 0)))
        face_z = jnp.where(top, 0.0, harmonic(k, pltpu.roll(k, depth - 1, 1)))
        diag = add_first(es[x], film_of(0, x))
        diag = diag + (gx[x] + face_x) + (face_y + pltpu.roll(face_y, 1, 0))
        diag = diag + (face_z + pltpu.roll(face_z, 1, 1))
        gx[x + 1] = face_x
        gy[x] = face_y
        gz[x] = face_z
        es[x] = diag
        ss[x] = lax.rsqrt(jnp.maximum(diag, 1e-30))
        return carry

    copies.wait(0)
    load(2)
    load(3)
    for side in range(2):
        @pl.when(flags[side] == 0)
        def _():
            for j in range(pad):
                ks[side * (pad + cells_x) + j] = jnp.zeros((wide_y, depth), jnp.float32)

    lax.fori_loop(0, wide_x, conductances, 0, unroll=4)

    def scale(x, carry):
        follow = jnp.minimum(x + 1, wide_x - 1)
        s = ss[x]
        gx[x + 1] = gx[x + 1] * s * ss[follow]
        gy[x] = gy[x] * s * pltpu.roll(s, wide_y - 1, 0)
        gz[x] = gz[x] * s * pltpu.roll(s, depth - 1, 1)
        bs[x] = add_first(bs[x], film_of(1, x)) * s
        us[x] = us[x] * es[x] * s
        return carry

    copies.wait(1)
    lax.fori_loop(0, wide_x, scale, 0, unroll=4)

    total = len(coefficients)
    src, dst = us, vs
    for number, (decay, gain) in enumerate(coefficients):
        last = number == total - 1
        margin = total - 1 - number

        def some(block, surface, src=src, dst=dst, decay=decay, gain=gain, number=number, last=last, margin=margin):
            planes = [pad - margin + block * BATCH + j for j in range(BATCH)]
            here = [src[x] for x in planes]
            before = [src[planes[0] - 1]] + here[:-1]
            after = here[1:] + [src[planes[-1] + 1]]
            g_x = [gx[planes[0]]] + [gx[x + 1] for x in planes]
            results = []
            for j, x in enumerate(planes):
                g_y, g_z, value = gy[x], gz[x], here[j]
                total_in = g_x[j] * before[j] + g_x[j + 1] * after[j]
                total_in += g_y * pltpu.roll(value, wide_y - 1, 0) + pltpu.roll(g_y * value, 1, 0)
                total_in += g_z * pltpu.roll(value, depth - 1, 1) + pltpu.roll(g_z * value, 1, 1)
                fresh = value + gain * ((bs[x] - value) + total_in)
                if number > 0:
                    fresh = fresh + decay * (value - dst[x])
                results.append(fresh)
            for j, x in enumerate(planes):
                fresh = results[j]
                if last:
                    final = (fresh * ss[x])[TILE:TILE + cells_y]
                    es[x, pl.ds(0, cells_y), :] = final
                    shift = x - pad
                    lane = lane_index((cells_y, LANES))
                    surface = jnp.where(lane == shift, pltpu.roll(final[:, :LANES], shift, 1), surface)
                else:
                    dst[x] = fresh
            return surface

        if last:
            surface = jnp.zeros((cells_y, LANES), jnp.float32)
            for block in range(cells_x // BATCH):
                surface = some(block, surface)
                here = pl.ds(block * BATCH, BATCH)
                copies.start("out", es.at[pl.ds(pad + block * BATCH, BATCH), pl.ds(0, cells_y)], out.at[here])
            gather_out(cells_x, cells_y, near_rows, landing, surface, own_rows, to_0, to_1, to_2, to_3)
            copies.wait("out")
            break
        lax.fori_loop(0, -(-(cells_x + 2 * margin) // BATCH), some, 0)
        src, dst = dst, src


def solid_step(flags, cond, sink, heat, temp, halo, films, landing, row_total, near_rows, pad):
    cells_x, cells_y, depth = cond.shape
    wide_x, wide_y = cells_x + 2 * pad, cells_y + 2 * TILE
    area = pltpu.VMEM((wide_x + BATCH, wide_y, depth), jnp.float32)
    return pl.pallas_call(
        functools.partial(solid_kernel, cells_x, cells_y, depth, pad, cheby_coefficients(SWEEPS), near_rows),
        out_shape=tuple(jax.ShapeDtypeStruct(shape, cond.dtype)
                        for shape in [(cells_x, cells_y, depth), (1, row_total)] + [(1, near_rows)] * 4),
        in_specs=[SMEM] + [HBM] * 8 + [VMEM] * 6,
        out_specs=(HBM,) + (VMEM,) * 5,
        scratch_shapes=[area] * 5
        + [area] * 4
        + [pltpu.VMEM((2, wide_y, LANES), jnp.float32), pltpu.SemaphoreType.DMA((4 + 16 * (depth // LANES) + cells_x // BATCH,))],
        compiler_params=pltpu.CompilerParams(vmem_limit_bytes=VMEM_SOLID),
        cost_estimate=lasts(30),
    )(flags, cond, sink, heat, temp, *halo, *films, landing)


def ones_where(condition):
    return jnp.where(condition, 1.0, 0.0)


def pick_dot(values, picks, dims):
    parts, rest = [], values
    for _ in range(2):
        scaled = rest * 65537.0
        parts.append(scaled - (scaled - rest))
        rest = rest - parts[-1]
    parts.append(rest)
    count = values.shape[0]
    if count % TILE:
        parts = [jnp.pad(part, ((0, TILE - count), (0, 0))) for part in parts]
    total = lax.dot_general(jnp.concatenate(parts, axis=0), picks, (dims, ((), ())),
                            precision=lax.Precision.DEFAULT, preferred_element_type=jnp.float32)
    size = parts[0].shape[0]
    total = total[:size] + (total[size:2 * size] + total[2 * size:])
    return total[:count]


def route_kernel(group_total, slot_cap, owner, out):
    dirs = owner[...]
    row_total = group_total * slot_cap
    codes = row_index((TILE, group_total))
    matched = ones_where((codes >= 1) & (codes <= 4) & (dirs == codes))
    before = ones_where(row_index((group_total, group_total)) < lane_index((group_total, group_total)))
    rank = jnp.dot(matched, before, precision=HIGHEST)
    start = jnp.where(matched > 0.5, rank * slot_cap, -1.0 * row_total)
    start = jnp.where(codes == 0, ones_where(dirs == 0), start)
    spread = ones_where(row_index((group_total, row_total)) == lane_index((group_total, row_total)) // slot_cap)
    wide = jnp.dot(start, spread, precision=HIGHEST)
    within = (lane_index((TILE, row_total)) % slot_cap).astype(jnp.float32)
    out[...] = jnp.where(row_index((TILE, row_total)) == 0, wide, wide + within)


def cell_values(plane_t, cells_x, cells_y, cells):
    count = cells.shape[1]
    in_x = ones_where(row_index((cells_x, count)) == cells // cells_y)
    in_y = ones_where(row_index((cells_y, count)) == cells % cells_y)
    lines = pick_dot(plane_t[:, :cells_x], in_x, ((1,), (0,)))
    return jnp.sum(lines * in_y, axis=0, keepdims=True)


def rows_out(cells_x, cells_y, near_rows, route, gas_t, film_t, pair, *outs):
    row_total = cells_x * cells_y
    cells = lane_index((1, row_total))
    film = cell_values(film_t, cells_x, cells_y, cells)
    gas = cell_values(gas_t, cells_x, cells_y, cells)
    values = jnp.concatenate([film, gas], axis=0)
    pair[...] = values
    for d in range(4):
        slots = route[d + 1:d + 2, :].astype(jnp.int32)
        pick = ones_where(row_index((near_rows, row_total)) == slots)
        outs[d][...] = pick_dot(values, pick, ((1,), (1,)))


def film_kernel(cells_x, cells_y, pad, flags, route, landing, pair, from_0, from_1, from_2, from_3, plane, low, high):
    cells = landing[...]
    slots = cells.shape[1]
    arrived = [jnp.where(flags[d] > 0, piece[...], 0.0) for d, piece in enumerate((from_0, from_1, from_2, from_3))]
    own = pair[...]
    film = jnp.concatenate([own[:1] * route[0:1, :]] + [piece[:1] for piece in arrived], axis=1)
    gas = jnp.concatenate([own[1:]] + [piece[1:] for piece in arrived], axis=1)
    in_x = ones_where(row_index((LANES, slots)) == cells // cells_y)
    in_y = ones_where(row_index((cells_y, slots)) == cells % cells_y)
    weighted = jnp.concatenate([in_y * film, in_y * (film * gas)], axis=0)
    total = pick_dot(weighted, in_x, ((1,), (1,)))
    lane = lane_index(total.shape)
    to_high = jnp.where(lane >= LANES - pad, pltpu.roll(total, LANES - cells_x, 1), 0.0)
    to_low = jnp.where((lane >= cells_x) & (lane < cells_x + pad), pltpu.roll(total, cells_x, 1), 0.0)
    for ref, value in ((plane, total), (low, to_low), (high, to_high)):
        ref[0] = value[:cells_y]
        ref[1] = value[cells_y:]


def widen_kernel(cells_y, flags, plane, low, high, out, first, last):
    total = plane[...] + jnp.where(flags[0] > 0, low[...], 0.0) + jnp.where(flags[1] > 0, high[...], 0.0)
    out[...] = total
    first[...] = total[:, :TILE]
    last[...] = total[:, cells_y - TILE:]


def gather_out(cells_x, cells_y, near_rows, landing, surface_t, own, *outs):
    values = cell_values(surface_t, cells_x, cells_y, landing[...])
    row_total = own.shape[1]
    own[...] = values[:, :row_total]
    for d in range(4):
        outs[d][...] = values[:, row_total + d * near_rows:row_total + (d + 1) * near_rows]


def wall_kernel(near_rows, flags, route, own, from_0, from_1, from_2, from_3, out):
    row_total = own.shape[1]
    total = own[...] * route[0:1, :]
    for d, (piece, side) in enumerate(((from_0, 1), (from_1, 0), (from_2, 3), (from_3, 2))):
        slots = route[d + 1:d + 2, :].astype(jnp.int32)
        pick = ones_where(row_index((near_rows, row_total)) == slots)
        total = total + pick_dot(jnp.where(flags[side] > 0, piece[...], 0.0), pick, ((1,), (0,)))
    out[...] = jnp.where(lane_index((1, row_total)) < flags[4], total, 0.0)


def small_call(kernel, shapes, flags, *args):
    lead = [] if flags is None else [flags]
    return pl.pallas_call(
        kernel,
        out_shape=tuple(jax.ShapeDtypeStruct(shape, jnp.float32) for shape in shapes),
        in_specs=[SMEM] * len(lead) + [VMEM] * len(args),
        out_specs=tuple(VMEM for _ in shapes),
        compiler_params=pltpu.CompilerParams(vmem_limit_bytes=32 * 1024 * 1024),
        cost_estimate=lasts(1),
    )(*lead, *args)


def on_device(
    fluid_temp, velocity, eddy_diff, wall_prev, row_count, owner_table, landing_cell,
    solid_temp, conductivity, sink, heat_source,
):
    cells_x, cells_y, cells_z = fluid_temp.shape
    solid_x, solid_y, solid_z = solid_temp.shape
    row_total = cells_x * cells_y
    group_total = owner_table.shape[1]
    slot_cap = row_total // group_total
    near_rows = group_total // 8 * slot_cap
    pad = SWEEPS
    flags = jnp.concatenate([jnp.stack([*sides("blk"), *sides("sub")]).astype(jnp.int32), row_count])
    fluid = (fluid_temp, velocity, eddy_diff)
    solids = (conductivity, sink, heat_source, solid_temp)

    xlow, xhigh, ylow, yhigh, wall_t = near_step(row_count, wall_prev.reshape(row_total // LANES, LANES), *fluid)
    xlo, xhi = exchange(xlow, xhigh, "blk", ring)
    ylo, yhi = exchange(ylow, yhigh, "sub", chain)
    after_near = lax.optimization_barrier((xlow, *solids))[1:]
    strips = solid_strips(after_near[:4], pad)
    xlo, xhi, owners, *strips = lax.optimization_barrier((xlo, xhi, owner_table, *strips))
    blk_halo = exchange(*strips[:2], "blk", ring)
    (route,) = small_call(
        functools.partial(route_kernel, group_total, slot_cap), [(TILE, row_total)], None, owners
    )
    xlo, xhi, route = lax.optimization_barrier((xlo, xhi, route))
    corner = (TILE, cells_z)
    low, high = packing(functools.partial(corner_kernel, cells_y, cells_z // LANES), (corner, corner), 0, 1, xlo, xhi)
    clo, chi = exchange(low, high, "sub", ring)
    ylo, yhi, clo, chi, *sub_strips = lax.optimization_barrier((ylo, yhi, clo, chi, *strips[2:]))
    sub_halo = exchange(*sub_strips, "sub", chain)
    fluid_new, pair, *bands = fluid_call(
        flags, wall_t, (xlo, xhi, ylo, yhi, clo, chi, ylow, yhigh), route, near_rows, *fluid
    )
    moves = (("blk", 1), ("blk", -1), ("sub", 1), ("sub", -1))
    *bands, blk_low, blk_high = lax.optimization_barrier((*bands, *blk_halo))
    bands[2], bands[3], sub_low, sub_high = lax.optimization_barrier((bands[2], bands[3], *sub_halo))
    arrived = [ring(band, axis, step) for band, (axis, step) in zip(bands, moves)]
    low, high = solid_corners(blk_low, blk_high, 4 * (solid_z // LANES))
    *arrived, low, high = lax.optimization_barrier((*arrived, low, high))
    halo = (blk_low, blk_high, sub_low, sub_high, *exchange(low, high, "sub", chain))
    plane = (2, solid_y, LANES)
    film, low, high = small_call(
        functools.partial(film_kernel, solid_x, solid_y, pad), [plane] * 3, flags, route, landing_cell, pair, *arrived
    )
    film, first, last = small_call(
        functools.partial(widen_kernel, solid_y), [plane] + [(2, TILE, LANES)] * 2,
        flags, film, ring(high, "blk", 1), ring(low, "blk", -1),
    )
    films = (film, ring(last, "sub", 1), ring(first, "sub", -1))
    solid_new, own, *backs = solid_step(flags, *solids, halo, films, landing_cell, row_total, near_rows, pad)
    returned = [ring(back, axis, -step) for back, (axis, step) in zip(backs, moves)]
    (wall_new,) = small_call(
        functools.partial(wall_kernel, near_rows), [(1, row_total)], flags, route, own, *returned
    )
    return fluid_new, solid_new, wall_new.reshape(row_total)


def solution(mesh):
    return jax.shard_map(
        on_device,
        mesh=mesh,
        in_specs=(
            P("blk", "sub", None),
            P(None, "blk", "sub", None),
            P("blk", "sub", None),
            P(("blk", "sub")),
            P(("blk", "sub")),
            P(("blk", "sub"), None),
            P(("blk", "sub"), None),
            P("blk", "sub", None),
            P("blk", "sub", None),
            P("blk", "sub", None),
            P("blk", "sub", None),
        ),
        out_specs=(P("blk", "sub", None), P("blk", "sub", None), P(("blk", "sub"))),
        check_vma=False,
    )
```

```python
import functools

import jax
import jax.numpy as jnp
from jax import lax
from jax.experimental import pallas as pl
from jax.experimental.pallas import tpu as pltpu
from jax.sharding import PartitionSpec as P

FLUID_SWEEPS = 2
SWEEPS = 8
RELAX_FACTOR = 0.8
EIG_LOW = 0.02
EIG_HIGH = 2.0
TILE = 8
LANES = 128
VMEM_ALL = 60 * 1024 * 1024
VMEM_FLUID = 53 * 1024 * 1024
VMEM_SOLID = 53 * 1024 * 1024
BATCH = 8
HIGHEST = lax.Precision.HIGHEST
VMEM = pl.BlockSpec(memory_space=pltpu.VMEM)
SMEM = pl.BlockSpec(memory_space=pltpu.SMEM)
HBM = pl.BlockSpec(memory_space=pltpu.HBM)


def cheby_coefficients(count_sweeps):
    center_eig = 0.5 * (EIG_HIGH + EIG_LOW)
    half_width = 0.5 * (EIG_HIGH - EIG_LOW)
    ratio_eig = center_eig / half_width
    damping = 1.0 / ratio_eig
    coefficients = [(0.0, 1.0 / center_eig)]
    for sweep_no in range(1, count_sweeps):
        damping_new = 1.0 / (2.0 * ratio_eig - damping)
        coefficients.append((damping_new * damping, 2.0 * damping_new / half_width))
        damping = damping_new
    return coefficients


def ring(value, axis, step):
    count = lax.axis_size(axis)
    return lax.ppermute(value, axis, [(i, (i + step) % count) for i in range(count)])


def chain(value, axis, step):
    count = lax.axis_size(axis)
    pairs = [(i, i + step) for i in range(count) if 0 <= i + step < count]
    return lax.ppermute(value, axis, pairs)


def sides(axis):
    place = lax.axis_index(axis)
    return place > 0, place < lax.axis_size(axis) - 1


def lasts(micros):
    return pl.CostEstimate(flops=0, bytes_accessed=int(micros * 3.69e6), transcendentals=0)


def quick_reciprocal(value):
    guess = pl.reciprocal(value, approx=True)
    return guess * (2.0 - value * guess)


def lane_index(shape):
    return lax.broadcasted_iota(jnp.int32, shape, 1)


def row_index(shape):
    return lax.broadcasted_iota(jnp.int32, shape, 0)


def first_lane(value, at_first):
    head = value[:, :LANES]
    head = jnp.where(lane_index(head.shape) == 0, at_first, head)
    if value.shape[1] == LANES:
        return head
    return jnp.concatenate([head, value[:, LANES:]], axis=1)


def last_lane(value, at_last):
    tail = value[:, -LANES:]
    tail = jnp.where(lane_index(tail.shape) == LANES - 1, at_last, tail)
    if value.shape[1] == LANES:
        return tail
    return jnp.concatenate([value[:, :-LANES], tail], axis=1)


def from_above(value, row):
    moved = pltpu.roll(value, 1, 0)
    head = jnp.where(row_index((TILE, value.shape[1])) == 0, row, moved[:TILE])
    return jnp.concatenate([head, moved[TILE:]], axis=0)


def from_below(value, row):
    moved = pltpu.roll(value, value.shape[0] - 1, 0)
    tail = jnp.where(row_index((TILE, value.shape[1])) == TILE - 1, row, moved[-TILE:])
    return jnp.concatenate([moved[:-TILE], tail], axis=0)


class Copies:
    def __init__(self, sems):
        self.sems, self.count, self.waits = sems, 0, {}

    def start(self, key, src, dst):
        made = pltpu.make_async_copy(src, dst, self.sems.at[self.count])
        self.count += 1
        made.start()
        self.waits.setdefault(key, []).append(made)

    def wait(self, key):
        for made in self.waits.pop(key, []):
            made.wait()

    def wait_all(self):
        for key in list(self.waits):
            self.wait(key)


PLANES = 6


def strip_sums(side, t, a, un, uz, t_far, a_far, un_far, live_two, wall):
    depth = t.shape[1]
    if side == 0:
        plus, minus = face(a, a_far, un, un_far)
        total = minus * t_far - plus * t
    else:
        plus, minus = face(a_far, a, un_far, un)
        total = plus * t_far - minus * t
    p_down, q_down = face(pltpu.roll(a, 1, 1), a, pltpu.roll(uz, 1, 1), uz)
    p_up, q_up = pltpu.roll(p_down, depth - 1, 1), pltpu.roll(q_down, depth - 1, 1)
    a_first, a_last, u_last = 2.0 * a[:, :LANES], 2.0 * a[:, -LANES:], 2.0 * uz[:, -LANES:]
    plus_last = a_last + jnp.maximum(u_last, 0.0)
    weight = (plus + minus) + first_lane(p_down + q_down, 2.0 * a_first)
    weight = weight + last_lane(p_up + q_up, 2.0 * plus_last - u_last)
    gain = a_first * live_two
    p_down, q_down = first_lane(p_down, 0.0), first_lane(q_down, gain)
    p_up, q_up = last_lane(p_up, plus_last), last_lane(q_up, 0.0)
    total = total + (p_down * pltpu.roll(t, 1, 1) + q_up * pltpu.roll(t, depth - 1, 1)) - (q_down + p_up) * t
    head = total[:, :LANES] + jnp.where(lane_index(gain.shape) == 0, gain * wall, 0.0)
    return (head if depth == LANES else jnp.concatenate([head, total[:, LANES:]], axis=1)), weight


def near_kernel(cells_x, cells_y, depth, count_ref, wall, temp, velo, diff, xlow, xhigh, ylow, yhigh, wall_t,
                sx, sy, sems):
    copies = Copies(sems)
    for side in range(2):
        edge, far = (0, 1) if side == 0 else (cells_y - 1, cells_y - 2)
        sources = ((temp, edge), (diff, edge), (velo.at[1], edge), (velo.at[0], edge), (velo.at[2], edge),
                   (temp, far), (diff, far), (velo.at[1], far))
        for plane, (src, y) in enumerate(sources):
            copies.start(("y", side), src.at[:, y, :], sy.at[side, plane])
    for side in range(2):
        edge, far = (0, 1) if side == 0 else (cells_x - 1, cells_x - 2)
        sources = ((temp, edge), (diff, edge), (velo.at[0], edge), (velo.at[1], edge), (velo.at[2], edge),
                   (temp, far), (diff, far), (velo.at[0], far))
        for plane, (src, x) in enumerate(sources):
            copies.start(("x", side), src.at[x], sx.at[side, plane])
    lines = wall[...]
    group = LANES // cells_y
    shape = (cells_x, lines.shape[0])
    plain = jnp.zeros((cells_x, LANES), jnp.float32)
    for j in range(group):
        pick = ones_where(row_index(shape) == lane_index(shape) * group + j)
        spread = jnp.dot(pick, lines, precision=HIGHEST)
        plain = plain + (pltpu.roll(spread, LANES - j * cells_y, 1) if j else spread)
    plain = jnp.where(lane_index(plain.shape) < cells_y, plain, 0.0)
    same = ones_where(row_index((cells_x, LANES)) == lane_index((cells_x, LANES)))
    turned = lax.dot_general(plain, same, (((0,), (0,)), ((), ())), precision=HIGHEST)[:cells_y]
    wall_t[...] = turned
    for side in range(2):
        x, y = side * (cells_x - 1), side * (cells_y - 1)
        for key, ref, out, plane, place, at in (
            ("x", sx, (xlow, xhigh)[side], turned, x * cells_y + row_index(turned.shape), x),
            ("y", sy, (ylow, yhigh)[side], plain, row_index(plain.shape) * cells_y + y, y),
        ):
            copies.wait((key, side))
            t, a, un, ut, uz, t_far, a_far, un_far = [ref[side, number] for number in range(8)]
            live_two = jnp.where(place < count_ref[0], 2.0, 0.0)
            sums = strip_sums(side, t, a, un, uz, t_far, a_far, un_far, live_two,
                              pltpu.roll(plane, LANES - at, 1) if at else plane)
            for number, value in enumerate((t, a, un, ut) + sums):
                for tile in range(depth // LANES):
                    out[PLANES * tile + number] = value[:, tile * LANES:(tile + 1) * LANES]


def near_step(row_count, wall, temp, velo, diff):
    cells_x, cells_y, depth = temp.shape
    planes = PLANES * (depth // LANES)
    x_strip = jax.ShapeDtypeStruct((planes, cells_y, LANES), temp.dtype)
    y_strip = jax.ShapeDtypeStruct((planes, cells_x, LANES), temp.dtype)
    return pl.pallas_call(
        functools.partial(near_kernel, cells_x, cells_y, depth),
        out_shape=(x_strip, x_strip, y_strip, y_strip, jax.ShapeDtypeStruct((cells_y, LANES), temp.dtype)),
        in_specs=[SMEM, VMEM, HBM, HBM, HBM],
        out_specs=(VMEM,) * 5,
        scratch_shapes=[
            pltpu.VMEM((2, 8, cells_y, depth), jnp.float32),
            pltpu.VMEM((2, 8, cells_x, depth), jnp.float32),
            pltpu.SemaphoreType.DMA((32,)),
        ],
        compiler_params=pltpu.CompilerParams(vmem_limit_bytes=VMEM_ALL),
        cost_estimate=lasts(4),
    )(row_count, wall, temp, velo, diff)


def corner_kernel(cells_y, count, xlo, xhi, low, high):
    for out, y in ((low, 0), (high, cells_y - 1)):
        for end, strip in enumerate((xlo, xhi)):
            for j in range(4):
                for tile in range(count):
                    out[pl.ds(4 * end + j, 1), pl.ds(tile * LANES, LANES)] = strip[PLANES * tile + j, pl.ds(y, 1), :]


def layers_of(field, pad):
    return pad


def layers_before(field, tile, tiles, pad):
    return sum(tiles * layers_of(other, pad) for other in range(field)) + tile * layers_of(field, pad)


def solid_pack_kernel(cells_x, cells_y, pad, depth, *refs):
    xlow, xhigh, ylow, yhigh, sems = refs[4:]
    copies = Copies(sems)
    for field, src in enumerate(refs[:4]):
        for tile in range(depth // LANES):
            number, zs = field * (depth // LANES) + tile, pl.ds(tile * LANES, LANES)
            layers, before = layers_of(field, pad), layers_before(field, tile, depth // LANES, pad)
            for side, out in ((0, xlow), (1, xhigh)):
                here = pl.ds(side * (cells_x - layers), layers)
                copies.start(0, src.at[here, :, zs], out.at[pl.ds(before, layers)])
            for side, out in ((0, ylow), (1, yhigh)):
                here = pl.ds(side * (cells_y - TILE), TILE)
                copies.start(0, src.at[:, here, zs], out.at[pl.ds(number * cells_x, cells_x)])
    copies.wait_all()


def solid_corner_kernel(cells_y, numbers, xlo, xhi, low, high):
    for side, out in enumerate((low, high)):
        rows = pl.ds(side * (cells_y - TILE), TILE)
        for end, strip in enumerate((xlo, xhi)):
            for number in range(numbers):
                field, part = divmod(number, numbers // 4)
                layers, before = layers_of(field, TILE), layers_before(field, part, numbers // 4, TILE)
                for i in range(1, TILE // 2 + 1):
                    near, far = (layers - i, layers - TILE + i) if end == 0 else (i - 1, TILE - 1 - i)
                    tile = strip[before + near, rows, :]
                    other = strip[before + far, rows, :]
                    row = row_index(tile.shape)
                    if side == 1:
                        tile = jnp.where(row >= i, tile, pltpu.roll(other, i, 0))
                    else:
                        tile = jnp.where(row < TILE - i, tile, pltpu.roll(other, TILE - i, 0))
                    out[(end * numbers + number) * (TILE // 2) + i - 1] = tile


def packing(kernel, shapes, copies, micros, *args):
    return pl.pallas_call(
        kernel,
        out_shape=tuple(jax.ShapeDtypeStruct(shape, jnp.float32) for shape in shapes),
        in_specs=[HBM if copies else VMEM] * len(args),
        out_specs=(VMEM,) * len(shapes),
        scratch_shapes=[pltpu.SemaphoreType.DMA((copies,))] if copies else [],
        compiler_params=pltpu.CompilerParams(vmem_limit_bytes=VMEM_ALL if copies else VMEM_ALL // 2),
        cost_estimate=lasts(micros),
    )(*args)


def exchange(low, high, axis, move):
    return move(high, axis, 1), move(low, axis, -1)


def solid_strips(solids, pad):
    cells_x, cells_y, depth = solids[0].shape
    numbers = 4 * (depth // LANES)
    planes = layers_before(4, 0, depth // LANES, pad)
    x_shape, y_shape = (planes, cells_y, LANES), (numbers * cells_x, TILE, LANES)
    return packing(functools.partial(solid_pack_kernel, cells_x, cells_y, pad, depth),
                   (x_shape, x_shape, y_shape, y_shape), 4 * numbers, 3, *solids)


def solid_corners(xlo, xhi, numbers):
    shape = (numbers * TILE, TILE, LANES)
    return packing(functools.partial(solid_corner_kernel, xlo.shape[1], numbers), (shape, shape), 0, 1, xlo, xhi)


def face(a_low, a_high, u_low, u_high):
    a_two = a_low + a_high
    u_two = u_low + u_high
    plus = a_two + jnp.maximum(u_two, 0.0)
    return plus, plus - u_two


def relaxation(a, ut, uz, low, high, above, below, live_two, wall):
    depth = a.shape[1]
    p_above, q_above = face(from_above(a, above[0]), a, from_above(ut, above[1]), ut)
    p_below, q_below = face(a, from_below(a, below[0]), ut, from_below(ut, below[1]))
    p_down, q_down = face(pltpu.roll(a, 1, 1), a, pltpu.roll(uz, 1, 1), uz)
    p_up, q_up = pltpu.roll(p_down, depth - 1, 1), pltpu.roll(q_down, depth - 1, 1)
    a_first = 2.0 * a[:, :LANES]
    u_last = 2.0 * uz[:, -LANES:]
    plus_last = 2.0 * a[:, -LANES:] + jnp.maximum(u_last, 0.0)
    gain = a_first * live_two
    p_down, q_down = first_lane(p_down, 0.0), first_lane(q_down, gain)
    p_up, q_up = last_lane(p_up, plus_last), last_lane(q_up, 0.0)
    leaving = (low[1] + high[0]) + (q_above + p_below) + (q_down + p_up)
    weight = leaving + ((low[0] + high[1]) + (p_above + q_below) + (p_down + q_up))
    head = weight[:, :LANES] + jnp.where(lane_index(gain.shape) == 0, 2.0 * a_first - gain, 0.0)
    weight = head if depth == LANES else jnp.concatenate([head, weight[:, LANES:]], axis=1)
    tail = weight[:, -LANES:] + jnp.where(lane_index(gain.shape) == LANES - 1, plus_last - u_last, 0.0)
    weight = tail if depth == LANES else jnp.concatenate([weight[:, :-LANES], tail], axis=1)
    factor = (2.0 * RELAX_FACTOR) * quick_reciprocal(weight)
    ghost = jnp.where(lane_index(gain.shape) == 0, gain * wall * factor[:, :LANES], 0.0)
    return (low[0] * factor, high[1] * factor, p_above * factor, q_below * factor, p_down * factor, q_up * factor,
            1.0 - leaving * factor, ghost)


def apply(factors, t, t_low, t_high, t_above, t_below):
    depth = t.shape[1]
    new = factors[6] * t + (factors[0] * t_low + factors[1] * t_high)
    new = new + (factors[2] * from_above(t, t_above) + factors[3] * from_below(t, t_below))
    new = new + (factors[4] * pltpu.roll(t, 1, 1) + factors[5] * pltpu.roll(t, depth - 1, 1))
    head = new[:, :LANES] + factors[7]
    return head if depth == LANES else jnp.concatenate([head, new[:, LANES:]], axis=1)


def fluid_kernel(cells_x, cells_y, depth, near_rows, flags, wall_t, xlo, xhi, ylo, yhi, clo, chi, own_lo, own_hi,
                 route, temp, velo, diff, out, pair_out, to_0, to_1, to_2, to_3, ts, us, as_, vs, ws, t1, yl, yt, cs, ks, sems):
    rows_total = flags[4]
    tiles = [(tile, pl.ds(tile * LANES, LANES)) for tile in range(depth // LANES)]
    copies = Copies(sems)
    step = TILE
    starts = list(range(0, cells_x, step))

    def load(start):
        here = pl.ds(start, step)
        copies.start(start, temp.at[here], ts.at[pl.ds(start + 2, step)])
        copies.start(start, diff.at[here], as_.at[pl.ds(start + 2, step)])
        copies.start(start, velo.at[0, here], us.at[pl.ds(start + 2, step)])
        copies.start(start, velo.at[1, here], vs.at[pl.ds(start + 1, step)])
        copies.start(start, velo.at[2, here], ws.at[pl.ds(start + 1, step)])

    for start in starts[:2]:
        load(start)
    for side, halo in enumerate((xlo, xhi)):
        at = 1 if side == 0 else cells_x + 2
        for tile, zs in tiles:
            for number, ref in enumerate((ts, as_, us)):
                ref[at, :, zs] = halo[PLANES * tile + number]

        @pl.when(flags[side] == 0)
        def _():
            for ref in (ts, as_, us):
                ref[at] = jnp.zeros(ref.shape[1:], jnp.float32)

    for side, halo in enumerate((ylo, yhi)):
        for number in range(PLANES):
            for tile, zs in tiles:
                yl[side, number, pl.ds(TILE, cells_x), zs] = halo[PLANES * tile + number]
        for end, at in enumerate((TILE - 1, TILE + cells_x)):
            good = flags[end] * flags[2 + side] > 0
            for j, number in enumerate((0, 1, 3, 2)):
                yl[side, number, pl.ds(at, 1), :] = jnp.where(good, (clo, chi)[side][pl.ds(4 * end + j, 1), :], 0.0)

    def strip_plane(strip, number):
        return jnp.concatenate([strip[PLANES * tile + number] for tile, _ in tiles], axis=1)

    def beside(side, t, a, un, ut, total, weight, own, above, below):
        low, high = (t, a, un), own
        if side == 1:
            low, high = high, low
        plus, minus = face(low[1], high[1], low[2], high[2])
        total = total + (minus * own[0] - plus * t if side == 0 else plus * own[0] - minus * t)
        weight = weight + (plus + minus)
        plus, minus = face(from_above(a, above[1]), a, from_above(ut, above[2]), ut)
        total = total + (plus * from_above(t, above[0]) - minus * t)
        weight = weight + (plus + minus)
        plus, minus = face(a, from_below(a, below[1]), ut, from_below(ut, below[2]))
        total = total + (minus * from_below(t, below[0]) - plus * t)
        weight = weight + (plus + minus)
        return t + (2.0 * RELAX_FACTOR) * total * quick_reciprocal(weight)

    def batch_factors(first, count, notes):
        a = [as_[first + j] for j in range(count + 2)]
        un = [us[first + j] for j in range(count + 2)]
        faces = [face(a[j], a[j + 1], un[j], un[j + 1]) for j in range(count + 1)]
        results = []
        for j in range(count):
            row = pl.ds(TILE - 1 + first + j, 1)
            results.append(relaxation(
                a[j + 1], vs[first + j], ws[first + j], faces[j], faces[j + 1], (yl[0, 1, row, :], yl[0, 2, row, :]),
                (yl[1, 1, row, :], yl[1, 2, row, :]), *notes[j]))
        return results

    def batch_apply(factors, ref, offset, first, rows_above, rows_below):
        t = [ref[first + offset - 1 + j] for j in range(len(factors) + 2)]
        results = []
        for j, plane in enumerate(factors):
            row = pl.ds(TILE - 1 + first + j, 1)
            results.append(apply(plane, t[j + 1], t[j], t[j + 2], rows_above[row, :], rows_below[row, :]))
        return results

    def own_note(i):
        place = (i - 1) * cells_y + row_index((cells_y, LANES))
        return jnp.where(place < rows_total, 2.0, 0.0), pltpu.roll(wall_t[...], LANES + 1 - i, 1)

    pair = 2

    def first_sweep(block, first):
        i = first + pair * block
        factors = batch_factors(i, pair, [own_note(i + j) for j in range(pair)])
        new = batch_apply(factors, ts, 1, i, yl.at[0, 0], yl.at[1, 0])
        for j in range(pair):
            for number in range(7):
                cs[number, i + j - 1] = factors[j][number]
            ks[i + j - 1] = factors[j][7]
            t1[i + j] = new[j]
        return first

    def halo_plane(side):
        at, inside, row = (1, 2, TILE - 1) if side == 0 else (cells_x + 2, cells_x + 1, TILE + cells_x)
        strip, row = (xlo, xhi)[side], pl.ds(row, 1)
        new = beside(side, ts[at], as_[at], us[at], strip_plane(strip, 3), strip_plane(strip, 4), strip_plane(strip, 5),
                     (ts[inside], as_[inside], us[inside]), [yl[0, number, row, :] for number in range(3)],
                     [yl[1, number, row, :] for number in range(3)])
        t1[0 if side == 0 else cells_x + 1] = jnp.where(flags[side] > 0, new, 0.0)

    following = 1
    for number, start in enumerate(starts):
        copies.wait(start)
        if number + 2 < len(starts):
            load(starts[number + 2])
        if start == 0:
            halo_plane(0)
        last = cells_x + 1 if start == starts[-1] else start + step - 1
        lax.fori_loop(0, (last - following) // pair, first_sweep, following)
        following = last
    halo_plane(1)

    for side, own in enumerate((own_lo, own_hi)):
        rows, up, down = pl.ds(TILE, cells_x), pl.ds(TILE - 1, 1), pl.ds(TILE + cells_x, 1)
        new = beside(side, *[yl[side, number, rows, :] for number in range(PLANES)],
                     [strip_plane(own, number) for number in range(3)],
                     [yl[side, number, up, :] for number in (0, 1, 3)],
                     [yl[side, number, down, :] for number in (0, 1, 3)])
        yt[side, rows, :] = jnp.where(flags[2 + side] > 0, new, 0.0)

    group = 4

    def second_sweep(block, carry):
        first, plane = carry
        i = first + group * block
        factors = [[cs[number, i + j - 1] for number in range(7)] + [ks[i + j - 1]] for j in range(group)]
        new = batch_apply(factors, t1, 0, i, yt.at[0], yt.at[1])
        for j in range(group):
            ts[i + j - 1] = new[j]
            shift = i + j - 1
            plane = jnp.where(lane_index((cells_y, LANES)) == shift, pltpu.roll(new[j][:, :LANES], shift, 1), plane)
        return first, plane

    plane = jnp.zeros((cells_y, LANES), jnp.float32)
    for start in starts:
        _, plane = lax.fori_loop(0, step // group, second_sweep, (start + 1, plane))
        copies.start("out", ts.at[pl.ds(start, step)], out.at[pl.ds(start, step)])
    film = jnp.zeros((cells_y, LANES), jnp.float32)
    lane = lane_index(film.shape)
    for x in range(cells_x):
        film = jnp.where(lane == x, pltpu.roll(as_[x + 2, :, pl.ds(0, LANES)], x, 1), film)
    film = jnp.where(lane * cells_y + row_index(film.shape) < rows_total, 2.0 * film, 0.0)
    rows_out(cells_x, cells_y, near_rows, route, plane, film, pair_out, to_0, to_1, to_2, to_3)
    copies.wait("out")


def fluid_call(flags, wall_t, strips, route, near_rows, temp, velo, diff):
    cells_x, cells_y, depth = temp.shape
    chunks = cells_x // TILE
    pair = jax.ShapeDtypeStruct((2, cells_x * cells_y), temp.dtype)
    band = jax.ShapeDtypeStruct((2, near_rows), temp.dtype)

    def planes(count):
        return pltpu.VMEM((count, cells_y, depth), jnp.float32)

    return pl.pallas_call(
        functools.partial(fluid_kernel, cells_x, cells_y, depth, near_rows),
        out_shape=(jax.ShapeDtypeStruct(temp.shape, temp.dtype), pair) + (band,) * 4,
        in_specs=[SMEM] + [VMEM] * 10 + [HBM] * 3,
        out_specs=(HBM,) + (VMEM,) * 5,
        scratch_shapes=[
            planes(cells_x + 4),
            planes(cells_x + 4),
            planes(cells_x + 4),
            planes(cells_x + 2),
            planes(cells_x + 2),
            planes(cells_x + 2),
            pltpu.VMEM((2, PLANES, cells_x + 2 * TILE, depth), jnp.float32),
            pltpu.VMEM((2, cells_x + 2 * TILE, depth), jnp.float32),
            pltpu.VMEM((7, cells_x, cells_y, depth), jnp.float32),
            pltpu.VMEM((cells_x, cells_y, LANES), jnp.float32),
            pltpu.SemaphoreType.DMA((6 * chunks,)),
        ],
        compiler_params=pltpu.CompilerParams(vmem_limit_bytes=VMEM_FLUID),
        cost_estimate=lasts(1),
    )(flags, wall_t, *strips, route, temp, velo, diff)


def solid_kernel(
    cells_x, cells_y, depth, pad, coefficients,
    near_rows, flags, cond, sink, heat, temp, xlo, xhi, ylo, yhi, clo, chi, film, film_lo, film_hi, landing,
    out, own_rows, to_0, to_1, to_2, to_3, ks, es, bs, us, vs, gx, gy, gz, ss, fs, sems,
):
    wide_x, wide_y = cells_x + 2 * pad, cells_y + 2 * TILE
    copies = Copies(sems)
    own_x, own_y = pl.ds(pad, cells_x), pl.ds(TILE, cells_y)

    def load(field):
        src, dst = ((cond, ks), (sink, es), (heat, bs), (temp, us))[field]
        if layers_of(field, pad) < pad:
            for x in (0, wide_x - 1):
                dst[x] = jnp.ones((wide_y, depth), jnp.float32)
        copies.start(field // 2, src, dst.at[own_x, own_y])
        for tile in range(depth // LANES):
            zs, number = pl.ds(tile * LANES, LANES), field * (depth // LANES) + tile
            key, numbers = field // 2, 4 * (depth // LANES)
            layers = layers_of(field, pad)
            x_from = pl.ds(layers_before(field, tile, depth // LANES, pad), layers)
            y_from = pl.ds(number * cells_x, cells_x)
            x_low, x_high = pl.ds(pad - layers, layers), pl.ds(pad + cells_x, layers)
            y_low, y_high = pl.ds(0, TILE), pl.ds(TILE + cells_y, TILE)
            copies.start(key, xlo.at[x_from], dst.at[x_low, own_y, zs])
            copies.start(key, xhi.at[x_from], dst.at[x_high, own_y, zs])
            copies.start(key, ylo.at[y_from], dst.at[own_x, y_low, zs])
            copies.start(key, yhi.at[y_from], dst.at[own_x, y_high, zs])
            for side, (strip, y_at) in enumerate(((clo, y_low), (chi, y_high))):
                for end in range(2):
                    for i in range(1, TILE + 1):
                        shared = min(i, TILE - i) or 1
                        tile = strip[(end * numbers + number) * (TILE // 2) + shared - 1]
                        if i > TILE // 2:
                            tile = pltpu.roll(tile, TILE - shared if side == 0 else shared, 0)
                        dst[pad - i if end == 0 else pad + cells_x + i - 1, y_at, zs] = tile
    load(0)
    load(1)
    fs[:, pl.ds(0, TILE), :] = jnp.where(flags[2] > 0, film_lo[...], 0.0)
    fs[:, own_y, :] = film[...]
    fs[:, pl.ds(TILE + cells_y, TILE), :] = jnp.where(flags[3] > 0, film_hi[...], 0.0)

    def harmonic(k, near):
        total = jnp.maximum(k + near, 1e-30)
        return (2.0 * k * near) * quick_reciprocal(total)

    def film_of(kind, x):
        return pltpu.roll(fs[kind], 2 * LANES + pad - x, 1)

    def add_first(value, extra):
        head = value[:, :LANES]
        head = head + jnp.where(lane_index(head.shape) == 0, extra, 0.0)
        return jnp.concatenate([head, value[:, LANES:]], axis=1) if depth > LANES else head

    gx[0, :, :] = jnp.zeros((wide_y, depth), jnp.float32)
    edge = row_index((wide_y, depth)) == wide_y - 1
    top = lane_index((wide_y, depth)) == depth - 1

    def conductances(x, carry):
        keep = jnp.where(x < wide_x - 1, 1.0, 0.0)
        follow = jnp.minimum(x + 1, wide_x - 1)
        k = ks[x]
        face_x = harmonic(k, ks[follow]) * keep
        face_y = jnp.where(edge, 0.0, harmonic(k, pltpu.roll(k, wide_y - 1, 0)))
        face_z = jnp.where(top, 0.0, harmonic(k, pltpu.roll(k, depth - 1, 1)))
        diag = add_first(es[x], film_of(0, x))
        diag = diag + (gx[x] + face_x) + (face_y + pltpu.roll(face_y, 1, 0))
        diag = diag + (face_z + pltpu.roll(face_z, 1, 1))
        gx[x + 1] = face_x
        gy[x] = face_y
        gz[x] = face_z
        es[x] = diag
        ss[x] = lax.rsqrt(jnp.maximum(diag, 1e-30))
        return carry

    copies.wait(0)
    load(2)
    load(3)
    for side in range(2):
        @pl.when(flags[side] == 0)
        def _():
            for j in range(pad):
                ks[side * (pad + cells_x) + j] = jnp.zeros((wide_y, depth), jnp.float32)

    lax.fori_loop(0, wide_x, conductances, 0, unroll=6)

    def scale(x, carry):
        follow = jnp.minimum(x + 1, wide_x - 1)
        s = ss[x]
        gx[x + 1] = gx[x + 1] * s * ss[follow]
        gy[x] = gy[x] * s * pltpu.roll(s, wide_y - 1, 0)
        gz[x] = gz[x] * s * pltpu.roll(s, depth - 1, 1)
        bs[x] = add_first(bs[x], film_of(1, x)) * s
        us[x] = us[x] * es[x] * s
        return carry

    copies.wait(1)
    lax.fori_loop(0, wide_x, scale, 0, unroll=8)

    total = len(coefficients)
    src, dst = us, vs
    for number, (decay, gain) in enumerate(coefficients):
        last = number == total - 1
        margin = total - 1 - number

        def some(block, surface, src=src, dst=dst, decay=decay, gain=gain, number=number, last=last, margin=margin):
            planes = [pad - margin + block * BATCH + j for j in range(BATCH)]
            here = [src[x] for x in planes]
            before = [src[planes[0] - 1]] + here[:-1]
            after = here[1:] + [src[planes[-1] + 1]]
            g_x = [gx[planes[0]]] + [gx[x + 1] for x in planes]
            results = []
            for j, x in enumerate(planes):
                g_y, g_z, value = gy[x], gz[x], here[j]
                total_in = g_x[j] * before[j] + g_x[j + 1] * after[j]
                total_in += g_y * pltpu.roll(value, wide_y - 1, 0) + pltpu.roll(g_y * value, 1, 0)
                total_in += g_z * pltpu.roll(value, depth - 1, 1) + pltpu.roll(g_z * value, 1, 1)
                fresh = value + gain * ((bs[x] - value) + total_in)
                if number > 0:
                    fresh = fresh + decay * (value - dst[x])
                results.append(fresh)
            for j, x in enumerate(planes):
                fresh = results[j]
                if last:
                    final = (fresh * ss[x])[TILE:TILE + cells_y]
                    es[x, pl.ds(0, cells_y), :] = final
                    shift = x - pad
                    lane = lane_index((cells_y, LANES))
                    surface = jnp.where(lane == shift, pltpu.roll(final[:, :LANES], shift, 1), surface)
                else:
                    dst[x] = fresh
            return surface

        if last:
            surface = jnp.zeros((cells_y, LANES), jnp.float32)
            for block in range(cells_x // BATCH):
                surface = some(block, surface)
                here = pl.ds(block * BATCH, BATCH)
                copies.start("out", es.at[pl.ds(pad + block * BATCH, BATCH), pl.ds(0, cells_y)], out.at[here])
            gather_out(cells_x, cells_y, near_rows, landing, surface, own_rows, to_0, to_1, to_2, to_3)
            copies.wait("out")
            break
        lax.fori_loop(0, -(-(cells_x + 2 * margin) // BATCH), some, 0)
        src, dst = dst, src


def solid_step(flags, cond, sink, heat, temp, halo, films, landing, row_total, near_rows, pad):
    cells_x, cells_y, depth = cond.shape
    wide_x, wide_y = cells_x + 2 * pad, cells_y + 2 * TILE
    area = pltpu.VMEM((wide_x + BATCH, wide_y, depth), jnp.float32)
    return pl.pallas_call(
        functools.partial(solid_kernel, cells_x, cells_y, depth, pad, cheby_coefficients(SWEEPS), near_rows),
        out_shape=tuple(jax.ShapeDtypeStruct(shape, cond.dtype)
                        for shape in [(cells_x, cells_y, depth), (1, row_total)] + [(1, near_rows)] * 4),
        in_specs=[SMEM] + [HBM] * 8 + [VMEM] * 6,
        out_specs=(HBM,) + (VMEM,) * 5,
        scratch_shapes=[area] * 5
        + [area] * 4
        + [pltpu.VMEM((2, wide_y, LANES), jnp.float32), pltpu.SemaphoreType.DMA((4 + 16 * (depth // LANES) + cells_x // BATCH,))],
        compiler_params=pltpu.CompilerParams(vmem_limit_bytes=VMEM_SOLID),
        cost_estimate=lasts(30),
    )(flags, cond, sink, heat, temp, *halo, *films, landing)


def ones_where(condition):
    return jnp.where(condition, 1.0, 0.0)


def pick_dot(values, picks, dims):
    parts, rest = [], values
    for _ in range(2):
        scaled = rest * 65537.0
        parts.append(scaled - (scaled - rest))
        rest = rest - parts[-1]
    parts.append(rest)
    count = values.shape[0]
    if count % TILE:
        parts = [jnp.pad(part, ((0, TILE - count), (0, 0))) for part in parts]
    total = lax.dot_general(jnp.concatenate(parts, axis=0), picks, (dims, ((), ())),
                            precision=lax.Precision.DEFAULT, preferred_element_type=jnp.float32)
    size = parts[0].shape[0]
    total = total[:size] + (total[size:2 * size] + total[2 * size:])
    return total[:count]


def route_kernel(group_total, slot_cap, owner, out):
    dirs = owner[...]
    row_total = group_total * slot_cap
    codes = row_index((TILE, group_total))
    matched = ones_where((codes >= 1) & (codes <= 4) & (dirs == codes))
    before = ones_where(row_index((group_total, group_total)) < lane_index((group_total, group_total)))
    rank = jnp.dot(matched, before, precision=HIGHEST)
    start = jnp.where(matched > 0.5, rank * slot_cap, -1.0 * row_total)
    start = jnp.where(codes == 0, ones_where(dirs == 0), start)
    spread = ones_where(row_index((group_total, row_total)) == lane_index((group_total, row_total)) // slot_cap)
    wide = jnp.dot(start, spread, precision=HIGHEST)
    within = (lane_index((TILE, row_total)) % slot_cap).astype(jnp.float32)
    out[...] = jnp.where(row_index((TILE, row_total)) == 0, wide, wide + within)


def cell_values(plane_t, cells_x, cells_y, cells):
    count = cells.shape[1]
    in_x = ones_where(row_index((cells_x, count)) == cells // cells_y)
    in_y = ones_where(row_index((cells_y, count)) == cells % cells_y)
    lines = pick_dot(plane_t[:, :cells_x], in_x, ((1,), (0,)))
    return jnp.sum(lines * in_y, axis=0, keepdims=True)


def rows_out(cells_x, cells_y, near_rows, route, gas_t, film_t, pair, *outs):
    row_total = cells_x * cells_y
    cells = lane_index((1, row_total))
    film = cell_values(film_t, cells_x, cells_y, cells)
    gas = cell_values(gas_t, cells_x, cells_y, cells)
    values = jnp.concatenate([film, gas], axis=0)
    pair[...] = values
    for d in range(4):
        slots = route[d + 1:d + 2, :].astype(jnp.int32)
        pick = ones_where(row_index((near_rows, row_total)) == slots)
        outs[d][...] = pick_dot(values, pick, ((1,), (1,)))


def film_kernel(cells_x, cells_y, pad, flags, route, landing, pair, from_0, from_1, from_2, from_3, plane, low, high):
    cells = landing[...]
    slots = cells.shape[1]
    arrived = [jnp.where(flags[d] > 0, piece[...], 0.0) for d, piece in enumerate((from_0, from_1, from_2, from_3))]
    own = pair[...]
    film = jnp.concatenate([own[:1] * route[0:1, :]] + [piece[:1] for piece in arrived], axis=1)
    gas = jnp.concatenate([own[1:]] + [piece[1:] for piece in arrived], axis=1)
    in_x = ones_where(row_index((LANES, slots)) == cells // cells_y)
    in_y = ones_where(row_index((cells_y, slots)) == cells % cells_y)
    weighted = jnp.concatenate([in_y * film, in_y * (film * gas)], axis=0)
    total = pick_dot(weighted, in_x, ((1,), (1,)))
    lane = lane_index(total.shape)
    to_high = jnp.where(lane >= LANES - pad, pltpu.roll(total, LANES - cells_x, 1), 0.0)
    to_low = jnp.where((lane >= cells_x) & (lane < cells_x + pad), pltpu.roll(total, cells_x, 1), 0.0)
    for ref, value in ((plane, total), (low, to_low), (high, to_high)):
        ref[0] = value[:cells_y]
        ref[1] = value[cells_y:]


def widen_kernel(cells_y, flags, plane, low, high, out, first, last):
    total = plane[...] + jnp.where(flags[0] > 0, low[...], 0.0) + jnp.where(flags[1] > 0, high[...], 0.0)
    out[...] = total
    first[...] = total[:, :TILE]
    last[...] = total[:, cells_y - TILE:]


def gather_out(cells_x, cells_y, near_rows, landing, surface_t, own, *outs):
    values = cell_values(surface_t, cells_x, cells_y, landing[...])
    row_total = own.shape[1]
    own[...] = values[:, :row_total]
    for d in range(4):
        outs[d][...] = values[:, row_total + d * near_rows:row_total + (d + 1) * near_rows]


def wall_kernel(near_rows, flags, route, own, from_0, from_1, from_2, from_3, out):
    row_total = own.shape[1]
    total = own[...] * route[0:1, :]
    for d, (piece, side) in enumerate(((from_0, 1), (from_1, 0), (from_2, 3), (from_3, 2))):
        slots = route[d + 1:d + 2, :].astype(jnp.int32)
        pick = ones_where(row_index((near_rows, row_total)) == slots)
        total = total + pick_dot(jnp.where(flags[side] > 0, piece[...], 0.0), pick, ((1,), (0,)))
    out[...] = jnp.where(lane_index((1, row_total)) < flags[4], total, 0.0)


def small_call(kernel, shapes, flags, *args):
    lead = [] if flags is None else [flags]
    return pl.pallas_call(
        kernel,
        out_shape=tuple(jax.ShapeDtypeStruct(shape, jnp.float32) for shape in shapes),
        in_specs=[SMEM] * len(lead) + [VMEM] * len(args),
        out_specs=tuple(VMEM for _ in shapes),
        compiler_params=pltpu.CompilerParams(vmem_limit_bytes=32 * 1024 * 1024),
        cost_estimate=lasts(1),
    )(*lead, *args)


def on_device(
    fluid_temp, velocity, eddy_diff, wall_prev, row_count, owner_table, landing_cell,
    solid_temp, conductivity, sink, heat_source,
):
    cells_x, cells_y, cells_z = fluid_temp.shape
    solid_x, solid_y, solid_z = solid_temp.shape
    row_total = cells_x * cells_y
    group_total = owner_table.shape[1]
    slot_cap = row_total // group_total
    near_rows = group_total // 8 * slot_cap
    pad = SWEEPS
    flags = jnp.concatenate([jnp.stack([*sides("blk"), *sides("sub")]).astype(jnp.int32), row_count])
    fluid = (fluid_temp, velocity, eddy_diff)
    solids = (conductivity, sink, heat_source, solid_temp)

    xlow, xhigh, ylow, yhigh, wall_t = near_step(row_count, wall_prev.reshape(row_total // LANES, LANES), *fluid)
    xlo, xhi = exchange(xlow, xhigh, "blk", ring)
    ylo, yhi = exchange(ylow, yhigh, "sub", chain)
    after_near = lax.optimization_barrier((xlow, *solids))[1:]
    strips = solid_strips(after_near[:4], pad)
    xlo, xhi, owners, *strips = lax.optimization_barrier((xlo, xhi, owner_table, *strips))
    blk_halo = exchange(*strips[:2], "blk", ring)
    (route,) = small_call(
        functools.partial(route_kernel, group_total, slot_cap), [(TILE, row_total)], None, owners
    )
    xlo, xhi, route = lax.optimization_barrier((xlo, xhi, route))
    corner = (TILE, cells_z)
    low, high = packing(functools.partial(corner_kernel, cells_y, cells_z // LANES), (corner, corner), 0, 1, xlo, xhi)
    clo, chi = exchange(low, high, "sub", ring)
    ylo, yhi, clo, chi, *sub_strips = lax.optimization_barrier((ylo, yhi, clo, chi, *strips[2:]))
    sub_halo = exchange(*sub_strips, "sub", chain)
    fluid_new, pair, *bands = fluid_call(
        flags, wall_t, (xlo, xhi, ylo, yhi, clo, chi, ylow, yhigh), route, near_rows, *fluid
    )
    moves = (("blk", 1), ("blk", -1), ("sub", 1), ("sub", -1))
    *bands, blk_low, blk_high = lax.optimization_barrier((*bands, *blk_halo))
    bands[2], bands[3], sub_low, sub_high = lax.optimization_barrier((bands[2], bands[3], *sub_halo))
    arrived = [ring(band, axis, step) for band, (axis, step) in zip(bands, moves)]
    low, high = solid_corners(blk_low, blk_high, 4 * (solid_z // LANES))
    *arrived, low, high = lax.optimization_barrier((*arrived, low, high))
    halo = (blk_low, blk_high, sub_low, sub_high, *exchange(low, high, "sub", chain))
    plane = (2, solid_y, LANES)
    film, low, high = small_call(
        functools.partial(film_kernel, solid_x, solid_y, pad), [plane] * 3, flags, route, landing_cell, pair, *arrived
    )
    film, first, last = small_call(
        functools.partial(widen_kernel, solid_y), [plane] + [(2, TILE, LANES)] * 2,
        flags, film, ring(high, "blk", 1), ring(low, "blk", -1),
    )
    films = (film, ring(last, "sub", 1), ring(first, "sub", -1))
    solid_new, own, *backs = solid_step(flags, *solids, halo, films, landing_cell, row_total, near_rows, pad)
    returned = {d: ring(backs[d], moves[d][0], -moves[d][1]) for d in (2, 3, 0, 1)}
    returned = [returned[d] for d in range(4)]
    (wall_new,) = small_call(
        functools.partial(wall_kernel, near_rows), [(1, row_total)], flags, route, own, *returned
    )
    return fluid_new, solid_new, wall_new.reshape(row_total)


def solution(mesh):
    return jax.shard_map(
        on_device,
        mesh=mesh,
        in_specs=(
            P("blk", "sub", None),
            P(None, "blk", "sub", None),
            P("blk", "sub", None),
            P(("blk", "sub")),
            P(("blk", "sub")),
            P(("blk", "sub"), None),
            P(("blk", "sub"), None),
            P("blk", "sub", None),
            P("blk", "sub", None),
            P("blk", "sub", None),
            P("blk", "sub", None),
        ),
        out_specs=(P("blk", "sub", None), P("blk", "sub", None), P(("blk", "sub"))),
        check_vma=False,
    )
```

```python
import functools

import jax
import jax.numpy as jnp
from jax import lax
from jax.experimental import pallas as pl
from jax.experimental.pallas import tpu as pltpu
from jax.sharding import PartitionSpec as P

FLUID_SWEEPS = 2
SWEEPS = 8
RELAX_FACTOR = 0.8
EIG_LOW = 0.02
EIG_HIGH = 2.0
TILE = 8
LANES = 128
VMEM_ALL = 60 * 1024 * 1024
VMEM_FLUID = 52 * 1024 * 1024
VMEM_SOLID = 53 * 1024 * 1024
BATCH = 8
HIGHEST = lax.Precision.HIGHEST
VMEM = pl.BlockSpec(memory_space=pltpu.VMEM)
SMEM = pl.BlockSpec(memory_space=pltpu.SMEM)
HBM = pl.BlockSpec(memory_space=pltpu.HBM)


def cheby_coefficients(count_sweeps):
    center_eig = 0.5 * (EIG_HIGH + EIG_LOW)
    half_width = 0.5 * (EIG_HIGH - EIG_LOW)
    ratio_eig = center_eig / half_width
    damping = 1.0 / ratio_eig
    coefficients = [(0.0, 1.0 / center_eig)]
    for sweep_no in range(1, count_sweeps):
        damping_new = 1.0 / (2.0 * ratio_eig - damping)
        coefficients.append((damping_new * damping, 2.0 * damping_new / half_width))
        damping = damping_new
    return coefficients


def ring(value, axis, step):
    count = lax.axis_size(axis)
    return lax.ppermute(value, axis, [(i, (i + step) % count) for i in range(count)])


def chain(value, axis, step):
    count = lax.axis_size(axis)
    pairs = [(i, i + step) for i in range(count) if 0 <= i + step < count]
    return lax.ppermute(value, axis, pairs)


def sides(axis):
    place = lax.axis_index(axis)
    return place > 0, place < lax.axis_size(axis) - 1


def lasts(micros):
    return pl.CostEstimate(flops=0, bytes_accessed=int(micros * 3.69e6), transcendentals=0)


def quick_reciprocal(value):
    guess = pl.reciprocal(value, approx=True)
    return guess * (2.0 - value * guess)


def lane_index(shape):
    return lax.broadcasted_iota(jnp.int32, shape, 1)


def row_index(shape):
    return lax.broadcasted_iota(jnp.int32, shape, 0)


def first_lane(value, at_first):
    head = value[:, :LANES]
    head = jnp.where(lane_index(head.shape) == 0, at_first, head)
    if value.shape[1] == LANES:
        return head
    return jnp.concatenate([head, value[:, LANES:]], axis=1)


def last_lane(value, at_last):
    tail = value[:, -LANES:]
    tail = jnp.where(lane_index(tail.shape) == LANES - 1, at_last, tail)
    if value.shape[1] == LANES:
        return tail
    return jnp.concatenate([value[:, :-LANES], tail], axis=1)


def from_above(value, row):
    moved = pltpu.roll(value, 1, 0)
    head = jnp.where(row_index((TILE, value.shape[1])) == 0, row, moved[:TILE])
    return jnp.concatenate([head, moved[TILE:]], axis=0)


def from_below(value, row):
    moved = pltpu.roll(value, value.shape[0] - 1, 0)
    tail = jnp.where(row_index((TILE, value.shape[1])) == TILE - 1, row, moved[-TILE:])
    return jnp.concatenate([moved[:-TILE], tail], axis=0)


class Copies:
    def __init__(self, sems):
        self.sems, self.count, self.waits = sems, 0, {}

    def start(self, key, src, dst):
        made = pltpu.make_async_copy(src, dst, self.sems.at[self.count])
        self.count += 1
        made.start()
        self.waits.setdefault(key, []).append(made)

    def wait(self, key):
        for made in self.waits.pop(key, []):
            made.wait()

    def wait_all(self):
        for key in list(self.waits):
            self.wait(key)


PLANES = 6


def strip_sums(side, t, a, un, uz, t_far, a_far, un_far, live_two, wall):
    depth = t.shape[1]
    if side == 0:
        plus, minus = face(a, a_far, un, un_far)
        total = minus * t_far - plus * t
    else:
        plus, minus = face(a_far, a, un_far, un)
        total = plus * t_far - minus * t
    p_down, q_down = face(pltpu.roll(a, 1, 1), a, pltpu.roll(uz, 1, 1), uz)
    p_up, q_up = pltpu.roll(p_down, depth - 1, 1), pltpu.roll(q_down, depth - 1, 1)
    a_first, a_last, u_last = 2.0 * a[:, :LANES], 2.0 * a[:, -LANES:], 2.0 * uz[:, -LANES:]
    plus_last = a_last + jnp.maximum(u_last, 0.0)
    weight = (plus + minus) + first_lane(p_down + q_down, 2.0 * a_first)
    weight = weight + last_lane(p_up + q_up, 2.0 * plus_last - u_last)
    gain = a_first * live_two
    p_down, q_down = first_lane(p_down, 0.0), first_lane(q_down, gain)
    p_up, q_up = last_lane(p_up, plus_last), last_lane(q_up, 0.0)
    total = total + (p_down * pltpu.roll(t, 1, 1) + q_up * pltpu.roll(t, depth - 1, 1)) - (q_down + p_up) * t
    head = total[:, :LANES] + jnp.where(lane_index(gain.shape) == 0, gain * wall, 0.0)
    return (head if depth == LANES else jnp.concatenate([head, total[:, LANES:]], axis=1)), weight


def near_kernel(cells_x, cells_y, depth, count_ref, wall, temp, velo, diff, xlow, xhigh, ylow, yhigh, wall_t,
                sx, sy, sems):
    copies = Copies(sems)
    for side in range(2):
        edge, far = (0, 1) if side == 0 else (cells_y - 1, cells_y - 2)
        sources = ((temp, edge), (diff, edge), (velo.at[1], edge), (velo.at[0], edge), (velo.at[2], edge),
                   (temp, far), (diff, far), (velo.at[1], far))
        for plane, (src, y) in enumerate(sources):
            copies.start(("y", side), src.at[:, y, :], sy.at[side, plane])
    for side in range(2):
        edge, far = (0, 1) if side == 0 else (cells_x - 1, cells_x - 2)
        sources = ((temp, edge), (diff, edge), (velo.at[0], edge), (velo.at[1], edge), (velo.at[2], edge),
                   (temp, far), (diff, far), (velo.at[0], far))
        for plane, (src, x) in enumerate(sources):
            copies.start(("x", side), src.at[x], sx.at[side, plane])
    lines = wall[...]
    group = LANES // cells_y
    shape = (cells_x, lines.shape[0])
    plain = jnp.zeros((cells_x, LANES), jnp.float32)
    for j in range(group):
        pick = ones_where(row_index(shape) == lane_index(shape) * group + j)
        spread = jnp.dot(pick, lines, precision=HIGHEST)
        plain = plain + (pltpu.roll(spread, LANES - j * cells_y, 1) if j else spread)
    plain = jnp.where(lane_index(plain.shape) < cells_y, plain, 0.0)
    same = ones_where(row_index((cells_x, LANES)) == lane_index((cells_x, LANES)))
    turned = lax.dot_general(plain, same, (((0,), (0,)), ((), ())), precision=HIGHEST)[:cells_y]
    wall_t[...] = turned
    for side in range(2):
        x, y = side * (cells_x - 1), side * (cells_y - 1)
        for key, ref, out, plane, place, at in (
            ("x", sx, (xlow, xhigh)[side], turned, x * cells_y + row_index(turned.shape), x),
            ("y", sy, (ylow, yhigh)[side], plain, row_index(plain.shape) * cells_y + y, y),
        ):
            copies.wait((key, side))
            t, a, un, ut, uz, t_far, a_far, un_far = [ref[side, number] for number in range(8)]
            live_two = jnp.where(place < count_ref[0], 2.0, 0.0)
            sums = strip_sums(side, t, a, un, uz, t_far, a_far, un_far, live_two,
                              pltpu.roll(plane, LANES - at, 1) if at else plane)
            for number, value in enumerate((t, a, un, ut) + sums):
                for tile in range(depth // LANES):
                    out[PLANES * tile + number] = value[:, tile * LANES:(tile + 1) * LANES]


def near_step(row_count, wall, temp, velo, diff):
    cells_x, cells_y, depth = temp.shape
    planes = PLANES * (depth // LANES)
    x_strip = jax.ShapeDtypeStruct((planes, cells_y, LANES), temp.dtype)
    y_strip = jax.ShapeDtypeStruct((planes, cells_x, LANES), temp.dtype)
    return pl.pallas_call(
        functools.partial(near_kernel, cells_x, cells_y, depth),
        out_shape=(x_strip, x_strip, y_strip, y_strip, jax.ShapeDtypeStruct((cells_y, LANES), temp.dtype)),
        in_specs=[SMEM, VMEM, HBM, HBM, HBM],
        out_specs=(VMEM,) * 5,
        scratch_shapes=[
            pltpu.VMEM((2, 8, cells_y, depth), jnp.float32),
            pltpu.VMEM((2, 8, cells_x, depth), jnp.float32),
            pltpu.SemaphoreType.DMA((32,)),
        ],
        compiler_params=pltpu.CompilerParams(vmem_limit_bytes=VMEM_ALL),
        cost_estimate=lasts(4),
    )(row_count, wall, temp, velo, diff)


def corner_kernel(cells_y, count, xlo, xhi, low, high):
    for out, y in ((low, 0), (high, cells_y - 1)):
        for end, strip in enumerate((xlo, xhi)):
            for j in range(4):
                for tile in range(count):
                    out[pl.ds(4 * end + j, 1), pl.ds(tile * LANES, LANES)] = strip[PLANES * tile + j, pl.ds(y, 1), :]


def layers_of(field, pad):
    return pad


def layers_before(field, tile, tiles, pad):
    return sum(tiles * layers_of(other, pad) for other in range(field)) + tile * layers_of(field, pad)


def solid_pack_kernel(cells_x, cells_y, pad, depth, *refs):
    xlow, xhigh, ylow, yhigh, sems = refs[4:]
    copies = Copies(sems)
    for field, src in enumerate(refs[:4]):
        for tile in range(depth // LANES):
            number, zs = field * (depth // LANES) + tile, pl.ds(tile * LANES, LANES)
            layers, before = layers_of(field, pad), layers_before(field, tile, depth // LANES, pad)
            for side, out in ((0, xlow), (1, xhigh)):
                here = pl.ds(side * (cells_x - layers), layers)
                copies.start(0, src.at[here, :, zs], out.at[pl.ds(before, layers)])
            for side, out in ((0, ylow), (1, yhigh)):
                here = pl.ds(side * (cells_y - TILE), TILE)
                copies.start(0, src.at[:, here, zs], out.at[pl.ds(number * cells_x, cells_x)])
    copies.wait_all()


def solid_corner_kernel(cells_y, numbers, xlo, xhi, low, high):
    for side, out in enumerate((low, high)):
        rows = pl.ds(side * (cells_y - TILE), TILE)
        for end, strip in enumerate((xlo, xhi)):
            for number in range(numbers):
                field, part = divmod(number, numbers // 4)
                layers, before = layers_of(field, TILE), layers_before(field, part, numbers // 4, TILE)
                for i in range(1, TILE // 2 + 1):
                    near, far = (layers - i, layers - TILE + i) if end == 0 else (i - 1, TILE - 1 - i)
                    tile = strip[before + near, rows, :]
                    other = strip[before + far, rows, :]
                    row = row_index(tile.shape)
                    if side == 1:
                        tile = jnp.where(row >= i, tile, pltpu.roll(other, i, 0))
                    else:
                        tile = jnp.where(row < TILE - i, tile, pltpu.roll(other, TILE - i, 0))
                    out[(end * numbers + number) * (TILE // 2) + i - 1] = tile


def packing(kernel, shapes, copies, micros, *args):
    return pl.pallas_call(
        kernel,
        out_shape=tuple(jax.ShapeDtypeStruct(shape, jnp.float32) for shape in shapes),
        in_specs=[HBM if copies else VMEM] * len(args),
        out_specs=(VMEM,) * len(shapes),
        scratch_shapes=[pltpu.SemaphoreType.DMA((copies,))] if copies else [],
        compiler_params=pltpu.CompilerParams(vmem_limit_bytes=VMEM_ALL if copies else VMEM_ALL // 2),
        cost_estimate=lasts(micros),
    )(*args)


def exchange(low, high, axis, move):
    return move(high, axis, 1), move(low, axis, -1)


def solid_strips(solids, pad):
    cells_x, cells_y, depth = solids[0].shape
    numbers = 4 * (depth // LANES)
    planes = layers_before(4, 0, depth // LANES, pad)
    x_shape, y_shape = (planes, cells_y, LANES), (numbers * cells_x, TILE, LANES)
    return packing(functools.partial(solid_pack_kernel, cells_x, cells_y, pad, depth),
                   (x_shape, x_shape, y_shape, y_shape), 4 * numbers, 3, *solids)


def solid_corners(xlo, xhi, numbers):
    shape = (numbers * TILE, TILE, LANES)
    return packing(functools.partial(solid_corner_kernel, xlo.shape[1], numbers), (shape, shape), 0, 1, xlo, xhi)


def face(a_low, a_high, u_low, u_high):
    a_two = a_low + a_high
    u_two = u_low + u_high
    plus = a_two + jnp.maximum(u_two, 0.0)
    return plus, plus - u_two


def relaxation(a, ut, uz, low, high, above, below, live_two, wall):
    depth = a.shape[1]
    p_above, q_above = face(from_above(a, above[0]), a, from_above(ut, above[1]), ut)
    p_below, q_below = face(a, from_below(a, below[0]), ut, from_below(ut, below[1]))
    p_down, q_down = face(pltpu.roll(a, 1, 1), a, pltpu.roll(uz, 1, 1), uz)
    p_up, q_up = pltpu.roll(p_down, depth - 1, 1), pltpu.roll(q_down, depth - 1, 1)
    a_first = 2.0 * a[:, :LANES]
    u_last = 2.0 * uz[:, -LANES:]
    plus_last = 2.0 * a[:, -LANES:] + jnp.maximum(u_last, 0.0)
    gain = a_first * live_two
    p_down, q_down = first_lane(p_down, 0.0), first_lane(q_down, gain)
    p_up, q_up = last_lane(p_up, plus_last), last_lane(q_up, 0.0)
    leaving = (low[1] + high[0]) + (q_above + p_below) + (q_down + p_up)
    weight = leaving + ((low[0] + high[1]) + (p_above + q_below) + (p_down + q_up))
    head = weight[:, :LANES] + jnp.where(lane_index(gain.shape) == 0, 2.0 * a_first - gain, 0.0)
    weight = head if depth == LANES else jnp.concatenate([head, weight[:, LANES:]], axis=1)
    tail = weight[:, -LANES:] + jnp.where(lane_index(gain.shape) == LANES - 1, plus_last - u_last, 0.0)
    weight = tail if depth == LANES else jnp.concatenate([weight[:, :-LANES], tail], axis=1)
    factor = (2.0 * RELAX_FACTOR) * quick_reciprocal(weight)
    ghost = jnp.where(lane_index(gain.shape) == 0, gain * wall * factor[:, :LANES], 0.0)
    return (low[0] * factor, high[1] * factor, p_above * factor, q_below * factor, p_down * factor, q_up * factor,
            1.0 - leaving * factor, ghost)


def apply(factors, t, t_low, t_high, t_above, t_below):
    depth = t.shape[1]
    new = factors[6] * t + (factors[0] * t_low + factors[1] * t_high)
    new = new + (factors[2] * from_above(t, t_above) + factors[3] * from_below(t, t_below))
    new = new + (factors[4] * pltpu.roll(t, 1, 1) + factors[5] * pltpu.roll(t, depth - 1, 1))
    head = new[:, :LANES] + factors[7]
    return head if depth == LANES else jnp.concatenate([head, new[:, LANES:]], axis=1)


def fluid_kernel(cells_x, cells_y, depth, near_rows, flags, wall_t, xlo, xhi, ylo, yhi, clo, chi, own_lo, own_hi,
                 route, temp, velo, diff, out, pair_out, to_0, to_1, to_2, to_3, ts, us, as_, vs, ws, t1, yl, yt, cs, ks, sems):
    rows_total = flags[4]
    tiles = [(tile, pl.ds(tile * LANES, LANES)) for tile in range(depth // LANES)]
    copies = Copies(sems)
    step = TILE
    starts = list(range(0, cells_x, step))

    def load(start):
        here = pl.ds(start, step)
        copies.start(start, temp.at[here], ts.at[pl.ds(start + 2, step)])
        copies.start(start, diff.at[here], as_.at[pl.ds(start + 2, step)])
        copies.start(start, velo.at[0, here], us.at[pl.ds(start + 2, step)])
        copies.start(start, velo.at[1, here], vs.at[pl.ds(start + 1, step)])
        copies.start(start, velo.at[2, here], ws.at[pl.ds(start + 1, step)])

    for start in starts[:2]:
        load(start)
    for side, halo in enumerate((xlo, xhi)):
        at = 1 if side == 0 else cells_x + 2
        for tile, zs in tiles:
            for number, ref in enumerate((ts, as_, us)):
                ref[at, :, zs] = halo[PLANES * tile + number]

        @pl.when(flags[side] == 0)
        def _():
            for ref in (ts, as_, us):
                ref[at] = jnp.zeros(ref.shape[1:], jnp.float32)

    for side, halo in enumerate((ylo, yhi)):
        for number in range(PLANES):
            for tile, zs in tiles:
                yl[side, number, pl.ds(TILE, cells_x), zs] = halo[PLANES * tile + number]
        for end, at in enumerate((TILE - 1, TILE + cells_x)):
            good = flags[end] * flags[2 + side] > 0
            for j, number in enumerate((0, 1, 3, 2)):
                yl[side, number, pl.ds(at, 1), :] = jnp.where(good, (clo, chi)[side][pl.ds(4 * end + j, 1), :], 0.0)

    def strip_plane(strip, number):
        return jnp.concatenate([strip[PLANES * tile + number] for tile, _ in tiles], axis=1)

    def beside(side, t, a, un, ut, total, weight, own, above, below):
        low, high = (t, a, un), own
        if side == 1:
            low, high = high, low
        plus, minus = face(low[1], high[1], low[2], high[2])
        total = total + (minus * own[0] - plus * t if side == 0 else plus * own[0] - minus * t)
        weight = weight + (plus + minus)
        plus, minus = face(from_above(a, above[1]), a, from_above(ut, above[2]), ut)
        total = total + (plus * from_above(t, above[0]) - minus * t)
        weight = weight + (plus + minus)
        plus, minus = face(a, from_below(a, below[1]), ut, from_below(ut, below[2]))
        total = total + (minus * from_below(t, below[0]) - plus * t)
        weight = weight + (plus + minus)
        return t + (2.0 * RELAX_FACTOR) * total * quick_reciprocal(weight)

    def batch_factors(first, count, notes):
        a = [as_[first + j] for j in range(count + 2)]
        un = [us[first + j] for j in range(count + 2)]
        faces = [face(a[j], a[j + 1], un[j], un[j + 1]) for j in range(count + 1)]
        results = []
        for j in range(count):
            row = pl.ds(TILE - 1 + first + j, 1)
            results.append(relaxation(
                a[j + 1], vs[first + j], ws[first + j], faces[j], faces[j + 1], (yl[0, 1, row, :], yl[0, 2, row, :]),
                (yl[1, 1, row, :], yl[1, 2, row, :]), *notes[j]))
        return results

    def batch_apply(factors, ref, offset, first, rows_above, rows_below):
        t = [ref[first + offset - 1 + j] for j in range(len(factors) + 2)]
        results = []
        for j, plane in enumerate(factors):
            row = pl.ds(TILE - 1 + first + j, 1)
            results.append(apply(plane, t[j + 1], t[j], t[j + 2], rows_above[row, :], rows_below[row, :]))
        return results

    def own_note(i):
        place = (i - 1) * cells_y + row_index((cells_y, LANES))
        return jnp.where(place < rows_total, 2.0, 0.0), pltpu.roll(wall_t[...], LANES + 1 - i, 1)

    pair = 2

    def first_sweep(block, first):
        i = first + pair * block
        factors = batch_factors(i, pair, [own_note(i + j) for j in range(pair)])
        new = batch_apply(factors, ts, 1, i, yl.at[0, 0], yl.at[1, 0])
        for j in range(pair):
            for number in range(7):
                cs[number, i + j - 1] = factors[j][number]
            ks[i + j - 1] = factors[j][7]
            t1[i + j] = new[j]
        return first

    def halo_plane(side):
        at, inside, row = (1, 2, TILE - 1) if side == 0 else (cells_x + 2, cells_x + 1, TILE + cells_x)
        strip, row = (xlo, xhi)[side], pl.ds(row, 1)
        new = beside(side, ts[at], as_[at], us[at], strip_plane(strip, 3), strip_plane(strip, 4), strip_plane(strip, 5),
                     (ts[inside], as_[inside], us[inside]), [yl[0, number, row, :] for number in range(3)],
                     [yl[1, number, row, :] for number in range(3)])
        t1[0 if side == 0 else cells_x + 1] = jnp.where(flags[side] > 0, new, 0.0)

    following = 1
    for number, start in enumerate(starts):
        copies.wait(start)
        if number + 2 < len(starts):
            load(starts[number + 2])
        if start == 0:
            halo_plane(0)
        last = cells_x + 1 if start == starts[-1] else start + step - 1
        lax.fori_loop(0, (last - following) // pair, first_sweep, following)
        following = last
    halo_plane(1)

    for side, own in enumerate((own_lo, own_hi)):
        rows, up, down = pl.ds(TILE, cells_x), pl.ds(TILE - 1, 1), pl.ds(TILE + cells_x, 1)
        new = beside(side, *[yl[side, number, rows, :] for number in range(PLANES)],
                     [strip_plane(own, number) for number in range(3)],
                     [yl[side, number, up, :] for number in (0, 1, 3)],
                     [yl[side, number, down, :] for number in (0, 1, 3)])
        yt[side, rows, :] = jnp.where(flags[2 + side] > 0, new, 0.0)

    group = 4

    def second_sweep(block, carry):
        first, plane = carry
        i = first + group * block
        factors = [[cs[number, i + j - 1] for number in range(7)] + [ks[i + j - 1]] for j in range(group)]
        new = batch_apply(factors, t1, 0, i, yt.at[0], yt.at[1])
        for j in range(group):
            ts[i + j - 1] = new[j]
            shift = i + j - 1
            plane = jnp.where(lane_index((cells_y, LANES)) == shift, pltpu.roll(new[j][:, :LANES], shift, 1), plane)
        return first, plane

    plane = jnp.zeros((cells_y, LANES), jnp.float32)
    for start in starts:
        _, plane = lax.fori_loop(0, step // group, second_sweep, (start + 1, plane))
        copies.start("out", ts.at[pl.ds(start, step)], out.at[pl.ds(start, step)])
    film = jnp.zeros((cells_y, LANES), jnp.float32)
    lane = lane_index(film.shape)
    for x in range(cells_x):
        film = jnp.where(lane == x, pltpu.roll(as_[x + 2, :, pl.ds(0, LANES)], x, 1), film)
    film = jnp.where(lane * cells_y + row_index(film.shape) < rows_total, 2.0 * film, 0.0)
    rows_out(cells_x, cells_y, near_rows, route, plane, film, pair_out, to_0, to_1, to_2, to_3)
    copies.wait("out")


def fluid_call(flags, wall_t, strips, route, near_rows, temp, velo, diff):
    cells_x, cells_y, depth = temp.shape
    chunks = cells_x // TILE
    pair = jax.ShapeDtypeStruct((2, cells_x * cells_y), temp.dtype)
    band = jax.ShapeDtypeStruct((2, near_rows), temp.dtype)

    def planes(count):
        return pltpu.VMEM((count, cells_y, depth), jnp.float32)

    return pl.pallas_call(
        functools.partial(fluid_kernel, cells_x, cells_y, depth, near_rows),
        out_shape=(jax.ShapeDtypeStruct(temp.shape, temp.dtype), pair) + (band,) * 4,
        in_specs=[SMEM] + [VMEM] * 10 + [HBM] * 3,
        out_specs=(HBM,) + (VMEM,) * 5,
        scratch_shapes=[
            planes(cells_x + 4),
            planes(cells_x + 4),
            planes(cells_x + 4),
            planes(cells_x + 2),
            planes(cells_x + 2),
            planes(cells_x + 2),
            pltpu.VMEM((2, PLANES, cells_x + 2 * TILE, depth), jnp.float32),
            pltpu.VMEM((2, cells_x + 2 * TILE, depth), jnp.float32),
            pltpu.VMEM((7, cells_x, cells_y, depth), jnp.float32),
            pltpu.VMEM((cells_x, cells_y, LANES), jnp.float32),
            pltpu.SemaphoreType.DMA((6 * chunks,)),
        ],
        compiler_params=pltpu.CompilerParams(vmem_limit_bytes=VMEM_FLUID),
        cost_estimate=lasts(1),
    )(flags, wall_t, *strips, route, temp, velo, diff)


def solid_kernel(
    cells_x, cells_y, depth, pad, coefficients,
    near_rows, flags, cond, sink, heat, temp, xlo, xhi, ylo, yhi, clo, chi, film, film_lo, film_hi, landing,
    out, own_rows, to_0, to_1, to_2, to_3, ks, es, bs, us, vs, gx, gy, gz, ss, fs, sems,
):
    wide_x, wide_y = cells_x + 2 * pad, cells_y + 2 * TILE
    copies = Copies(sems)
    own_x, own_y = pl.ds(pad, cells_x), pl.ds(TILE, cells_y)

    def load(field):
        src, dst = ((cond, ks), (sink, es), (heat, bs), (temp, us))[field]
        if layers_of(field, pad) < pad:
            for x in (0, wide_x - 1):
                dst[x] = jnp.ones((wide_y, depth), jnp.float32)
        copies.start(field // 2, src, dst.at[own_x, own_y])
        for tile in range(depth // LANES):
            zs, number = pl.ds(tile * LANES, LANES), field * (depth // LANES) + tile
            key, numbers = field // 2, 4 * (depth // LANES)
            layers = layers_of(field, pad)
            x_from = pl.ds(layers_before(field, tile, depth // LANES, pad), layers)
            y_from = pl.ds(number * cells_x, cells_x)
            x_low, x_high = pl.ds(pad - layers, layers), pl.ds(pad + cells_x, layers)
            y_low, y_high = pl.ds(0, TILE), pl.ds(TILE + cells_y, TILE)
            copies.start(key, xlo.at[x_from], dst.at[x_low, own_y, zs])
            copies.start(key, xhi.at[x_from], dst.at[x_high, own_y, zs])
            copies.start(key, ylo.at[y_from], dst.at[own_x, y_low, zs])
            copies.start(key, yhi.at[y_from], dst.at[own_x, y_high, zs])
            for side, (strip, y_at) in enumerate(((clo, y_low), (chi, y_high))):
                for end in range(2):
                    for i in range(1, TILE + 1):
                        shared = min(i, TILE - i) or 1
                        tile = strip[(end * numbers + number) * (TILE // 2) + shared - 1]
                        if i > TILE // 2:
                            tile = pltpu.roll(tile, TILE - shared if side == 0 else shared, 0)
                        dst[pad - i if end == 0 else pad + cells_x + i - 1, y_at, zs] = tile
    load(0)
    load(1)
    fs[:, pl.ds(0, TILE), :] = jnp.where(flags[2] > 0, film_lo[...], 0.0)
    fs[:, own_y, :] = film[...]
    fs[:, pl.ds(TILE + cells_y, TILE), :] = jnp.where(flags[3] > 0, film_hi[...], 0.0)

    def harmonic(k, near):
        total = jnp.maximum(k + near, 1e-30)
        return (2.0 * k * near) * quick_reciprocal(total)

    def film_of(kind, x):
        return pltpu.roll(fs[kind], 2 * LANES + pad - x, 1)

    def add_first(value, extra):
        head = value[:, :LANES]
        head = head + jnp.where(lane_index(head.shape) == 0, extra, 0.0)
        return jnp.concatenate([head, value[:, LANES:]], axis=1) if depth > LANES else head

    gx[0, :, :] = jnp.zeros((wide_y, depth), jnp.float32)
    edge = row_index((wide_y, depth)) == wide_y - 1
    top = lane_index((wide_y, depth)) == depth - 1

    def conductances(x, carry):
        keep = jnp.where(x < wide_x - 1, 1.0, 0.0)
        follow = jnp.minimum(x + 1, wide_x - 1)
        k = ks[x]
        face_x = harmonic(k, ks[follow]) * keep
        face_y = jnp.where(edge, 0.0, harmonic(k, pltpu.roll(k, wide_y - 1, 0)))
        face_z = jnp.where(top, 0.0, harmonic(k, pltpu.roll(k, depth - 1, 1)))
        diag = add_first(es[x], film_of(0, x))
        diag = diag + (gx[x] + face_x) + (face_y + pltpu.roll(face_y, 1, 0))
        diag = diag + (face_z + pltpu.roll(face_z, 1, 1))
        gx[x + 1] = face_x
        gy[x] = face_y
        gz[x] = face_z
        es[x] = diag
        ss[x] = lax.rsqrt(jnp.maximum(diag, 1e-30))
        return carry

    copies.wait(0)
    load(2)
    load(3)
    for side in range(2):
        @pl.when(flags[side] == 0)
        def _():
            for j in range(pad):
                ks[side * (pad + cells_x) + j] = jnp.zeros((wide_y, depth), jnp.float32)

    lax.fori_loop(0, wide_x, conductances, 0, unroll=6)

    def scale(x, carry):
        follow = jnp.minimum(x + 1, wide_x - 1)
        s = ss[x]
        gx[x + 1] = gx[x + 1] * s * ss[follow]
        gy[x] = gy[x] * s * pltpu.roll(s, wide_y - 1, 0)
        gz[x] = gz[x] * s * pltpu.roll(s, depth - 1, 1)
        bs[x] = add_first(bs[x], film_of(1, x)) * s
        us[x] = us[x] * es[x] * s
        return carry

    copies.wait(1)
    lax.fori_loop(0, wide_x, scale, 0, unroll=8)

    total = len(coefficients)
    src, dst = us, vs
    for number, (decay, gain) in enumerate(coefficients):
        last = number == total - 1
        margin = total - 1 - number

        def some(block, surface, src=src, dst=dst, decay=decay, gain=gain, number=number, last=last, margin=margin):
            planes = [pad - margin + block * BATCH + j for j in range(BATCH)]
            here = [src[x] for x in planes]
            before = [src[planes[0] - 1]] + here[:-1]
            after = here[1:] + [src[planes[-1] + 1]]
            g_x = [gx[planes[0]]] + [gx[x + 1] for x in planes]
            results = []
            for j, x in enumerate(planes):
                g_y, g_z, value = gy[x], gz[x], here[j]
                total_in = g_x[j] * before[j] + g_x[j + 1] * after[j]
                total_in += g_y * pltpu.roll(value, wide_y - 1, 0) + pltpu.roll(g_y * value, 1, 0)
                total_in += g_z * pltpu.roll(value, depth - 1, 1) + pltpu.roll(g_z * value, 1, 1)
                fresh = value + gain * ((bs[x] - value) + total_in)
                if number > 0:
                    fresh = fresh + decay * (value - dst[x])
                results.append(fresh)
            for j, x in enumerate(planes):
                fresh = results[j]
                if last:
                    final = (fresh * ss[x])[TILE:TILE + cells_y]
                    es[x, pl.ds(0, cells_y), :] = final
                    shift = x - pad
                    lane = lane_index((cells_y, LANES))
                    surface = jnp.where(lane == shift, pltpu.roll(final[:, :LANES], shift, 1), surface)
                else:
                    dst[x] = fresh
            return surface

        if last:
            surface = jnp.zeros((cells_y, LANES), jnp.float32)
            for block in range(cells_x // BATCH):
                surface = some(block, surface)
                here = pl.ds(block * BATCH, BATCH)
                copies.start("out", es.at[pl.ds(pad + block * BATCH, BATCH), pl.ds(0, cells_y)], out.at[here])
            gather_out(cells_x, cells_y, near_rows, landing, surface, own_rows, to_0, to_1, to_2, to_3)
            copies.wait("out")
            break
        lax.fori_loop(0, -(-(cells_x + 2 * margin) // BATCH), some, 0)
        src, dst = dst, src


def solid_step(flags, cond, sink, heat, temp, halo, films, landing, row_total, near_rows, pad):
    cells_x, cells_y, depth = cond.shape
    wide_x, wide_y = cells_x + 2 * pad, cells_y + 2 * TILE
    area = pltpu.VMEM((wide_x + BATCH, wide_y, depth), jnp.float32)
    return pl.pallas_call(
        functools.partial(solid_kernel, cells_x, cells_y, depth, pad, cheby_coefficients(SWEEPS), near_rows),
        out_shape=tuple(jax.ShapeDtypeStruct(shape, cond.dtype)
                        for shape in [(cells_x, cells_y, depth), (1, row_total)] + [(1, near_rows)] * 4),
        in_specs=[SMEM] + [HBM] * 8 + [VMEM] * 6,
        out_specs=(HBM,) + (VMEM,) * 5,
        scratch_shapes=[area] * 5
        + [area] * 4
        + [pltpu.VMEM((2, wide_y, LANES), jnp.float32), pltpu.SemaphoreType.DMA((4 + 16 * (depth // LANES) + cells_x // BATCH,))],
        compiler_params=pltpu.CompilerParams(vmem_limit_bytes=VMEM_SOLID),
        cost_estimate=lasts(30),
    )(flags, cond, sink, heat, temp, *halo, *films, landing)


def ones_where(condition):
    return jnp.where(condition, 1.0, 0.0)


def pick_dot(values, picks, dims):
    parts, rest = [], values
    for _ in range(2):
        scaled = rest * 65537.0
        parts.append(scaled - (scaled - rest))
        rest = rest - parts[-1]
    parts.append(rest)
    count = values.shape[0]
    if count % TILE:
        parts = [jnp.pad(part, ((0, TILE - count), (0, 0))) for part in parts]
    total = lax.dot_general(jnp.concatenate(parts, axis=0), picks, (dims, ((), ())),
                            precision=lax.Precision.DEFAULT, preferred_element_type=jnp.float32)
    size = parts[0].shape[0]
    total = total[:size] + (total[size:2 * size] + total[2 * size:])
    return total[:count]


def route_kernel(group_total, slot_cap, owner, out):
    dirs = owner[...]
    row_total = group_total * slot_cap
    codes = row_index((TILE, group_total))
    matched = ones_where((codes >= 1) & (codes <= 4) & (dirs == codes))
    before = ones_where(row_index((group_total, group_total)) < lane_index((group_total, group_total)))
    rank = jnp.dot(matched, before, precision=HIGHEST)
    start = jnp.where(matched > 0.5, rank * slot_cap, -1.0 * row_total)
    start = jnp.where(codes == 0, ones_where(dirs == 0), start)
    spread = ones_where(row_index((group_total, row_total)) == lane_index((group_total, row_total)) // slot_cap)
    wide = jnp.dot(start, spread, precision=HIGHEST)
    within = (lane_index((TILE, row_total)) % slot_cap).astype(jnp.float32)
    out[...] = jnp.where(row_index((TILE, row_total)) == 0, wide, wide + within)


def cell_values(plane_t, cells_x, cells_y, cells):
    count = cells.shape[1]
    in_x = ones_where(row_index((cells_x, count)) == cells // cells_y)
    in_y = ones_where(row_index((cells_y, count)) == cells % cells_y)
    lines = pick_dot(plane_t[:, :cells_x], in_x, ((1,), (0,)))
    return jnp.sum(lines * in_y, axis=0, keepdims=True)


def rows_out(cells_x, cells_y, near_rows, route, gas_t, film_t, pair, *outs):
    row_total = cells_x * cells_y
    cells = lane_index((1, row_total))
    film = cell_values(film_t, cells_x, cells_y, cells)
    gas = cell_values(gas_t, cells_x, cells_y, cells)
    values = jnp.concatenate([film, gas], axis=0)
    pair[...] = values
    for d in range(4):
        slots = route[d + 1:d + 2, :].astype(jnp.int32)
        pick = ones_where(row_index((near_rows, row_total)) == slots)
        outs[d][...] = pick_dot(values, pick, ((1,), (1,)))


def film_kernel(cells_x, cells_y, pad, flags, route, landing, pair, from_0, from_1, from_2, from_3, plane, low, high):
    cells = landing[...]
    slots = cells.shape[1]
    arrived = [jnp.where(flags[d] > 0, piece[...], 0.0) for d, piece in enumerate((from_0, from_1, from_2, from_3))]
    own = pair[...]
    film = jnp.concatenate([own[:1] * route[0:1, :]] + [piece[:1] for piece in arrived], axis=1)
    gas = jnp.concatenate([own[1:]] + [piece[1:] for piece in arrived], axis=1)
    in_x = ones_where(row_index((LANES, slots)) == cells // cells_y)
    in_y = ones_where(row_index((cells_y, slots)) == cells % cells_y)
    weighted = jnp.concatenate([in_y * film, in_y * (film * gas)], axis=0)
    total = pick_dot(weighted, in_x, ((1,), (1,)))
    lane = lane_index(total.shape)
    to_high = jnp.where(lane >= LANES - pad, pltpu.roll(total, LANES - cells_x, 1), 0.0)
    to_low = jnp.where((lane >= cells_x) & (lane < cells_x + pad), pltpu.roll(total, cells_x, 1), 0.0)
    for ref, value in ((plane, total), (low, to_low), (high, to_high)):
        ref[0] = value[:cells_y]
        ref[1] = value[cells_y:]


def widen_kernel(cells_y, flags, plane, low, high, out, first, last):
    total = plane[...] + jnp.where(flags[0] > 0, low[...], 0.0) + jnp.where(flags[1] > 0, high[...], 0.0)
    out[...] = total
    first[...] = total[:, :TILE]
    last[...] = total[:, cells_y - TILE:]


def gather_out(cells_x, cells_y, near_rows, landing, surface_t, own, *outs):
    values = cell_values(surface_t, cells_x, cells_y, landing[...])
    row_total = own.shape[1]
    own[...] = values[:, :row_total]
    for d in range(4):
        outs[d][...] = values[:, row_total + d * near_rows:row_total + (d + 1) * near_rows]


def wall_kernel(near_rows, flags, route, own, from_0, from_1, from_2, from_3, out):
    row_total = own.shape[1]
    total = own[...] * route[0:1, :]
    for d, (piece, side) in enumerate(((from_0, 1), (from_1, 0), (from_2, 3), (from_3, 2))):
        slots = route[d + 1:d + 2, :].astype(jnp.int32)
        pick = ones_where(row_index((near_rows, row_total)) == slots)
        total = total + pick_dot(jnp.where(flags[side] > 0, piece[...], 0.0), pick, ((1,), (0,)))
    out[...] = jnp.where(lane_index((1, row_total)) < flags[4], total, 0.0)


def small_call(kernel, shapes, flags, *args):
    lead = [] if flags is None else [flags]
    return pl.pallas_call(
        kernel,
        out_shape=tuple(jax.ShapeDtypeStruct(shape, jnp.float32) for shape in shapes),
        in_specs=[SMEM] * len(lead) + [VMEM] * len(args),
        out_specs=tuple(VMEM for _ in shapes),
        compiler_params=pltpu.CompilerParams(vmem_limit_bytes=32 * 1024 * 1024),
        cost_estimate=lasts(1),
    )(*lead, *args)


def on_device(
    fluid_temp, velocity, eddy_diff, wall_prev, row_count, owner_table, landing_cell,
    solid_temp, conductivity, sink, heat_source,
):
    cells_x, cells_y, cells_z = fluid_temp.shape
    solid_x, solid_y, solid_z = solid_temp.shape
    row_total = cells_x * cells_y
    group_total = owner_table.shape[1]
    slot_cap = row_total // group_total
    near_rows = group_total // 8 * slot_cap
    pad = SWEEPS
    flags = jnp.concatenate([jnp.stack([*sides("blk"), *sides("sub")]).astype(jnp.int32), row_count])
    fluid = (fluid_temp, velocity, eddy_diff)
    solids = (conductivity, sink, heat_source, solid_temp)

    xlow, xhigh, ylow, yhigh, wall_t = near_step(row_count, wall_prev.reshape(row_total // LANES, LANES), *fluid)
    xlo, xhi = exchange(xlow, xhigh, "blk", ring)
    ylo, yhi = exchange(ylow, yhigh, "sub", chain)
    after_near = lax.optimization_barrier((xlow, *solids))[1:]
    strips = solid_strips(after_near[:4], pad)
    xlo, xhi, owners, *strips = lax.optimization_barrier((xlo, xhi, owner_table, *strips))
    blk_halo = exchange(*strips[:2], "blk", ring)
    (route,) = small_call(
        functools.partial(route_kernel, group_total, slot_cap), [(TILE, row_total)], None, owners
    )
    xlo, xhi, route = lax.optimization_barrier((xlo, xhi, route))
    corner = (TILE, cells_z)
    low, high = packing(functools.partial(corner_kernel, cells_y, cells_z // LANES), (corner, corner), 0, 1, xlo, xhi)
    clo, chi = exchange(low, high, "sub", ring)
    ylo, yhi, clo, chi, *sub_strips = lax.optimization_barrier((ylo, yhi, clo, chi, *strips[2:]))
    sub_halo = exchange(*sub_strips, "sub", chain)
    fluid_new, pair, *bands = fluid_call(
        flags, wall_t, (xlo, xhi, ylo, yhi, clo, chi, ylow, yhigh), route, near_rows, *fluid
    )
    moves = (("blk", 1), ("blk", -1), ("sub", 1), ("sub", -1))
    *bands, blk_low, blk_high = lax.optimization_barrier((*bands, *blk_halo))
    bands[2], bands[3], sub_low, sub_high = lax.optimization_barrier((bands[2], bands[3], *sub_halo))
    arrived = [ring(band, axis, step) for band, (axis, step) in zip(bands, moves)]
    low, high = solid_corners(blk_low, blk_high, 4 * (solid_z // LANES))
    *arrived, low, high = lax.optimization_barrier((*arrived, low, high))
    halo = (blk_low, blk_high, sub_low, sub_high, *exchange(low, high, "sub", chain))
    plane = (2, solid_y, LANES)
    film, low, high = small_call(
        functools.partial(film_kernel, solid_x, solid_y, pad), [plane] * 3, flags, route, landing_cell, pair, *arrived
    )
    film, first, last = small_call(
        functools.partial(widen_kernel, solid_y), [plane] + [(2, TILE, LANES)] * 2,
        flags, film, ring(high, "blk", 1), ring(low, "blk", -1),
    )
    films = (film, ring(last, "sub", 1), ring(first, "sub", -1))
    solid_new, own, *backs = solid_step(flags, *solids, halo, films, landing_cell, row_total, near_rows, pad)
    returned = {d: ring(backs[d], moves[d][0], -moves[d][1]) for d in (2, 3, 0, 1)}
    returned = [returned[d] for d in range(4)]
    (wall_new,) = small_call(
        functools.partial(wall_kernel, near_rows), [(1, row_total)], flags, route, own, *returned
    )
    return fluid_new, solid_new, wall_new.reshape(row_total)


def solution(mesh):
    return jax.shard_map(
        on_device,
        mesh=mesh,
        in_specs=(
            P("blk", "sub", None),
            P(None, "blk", "sub", None),
            P("blk", "sub", None),
            P(("blk", "sub")),
            P(("blk", "sub")),
            P(("blk", "sub"), None),
            P(("blk", "sub"), None),
            P("blk", "sub", None),
            P("blk", "sub", None),
            P("blk", "sub", None),
            P("blk", "sub", None),
        ),
        out_specs=(P("blk", "sub", None), P("blk", "sub", None), P(("blk", "sub"))),
        check_vma=False,
    )
```
